128 devices in a mesh: dp: 8 (over y, x_hi), head: 16 (over z, x_lo, core).
Axes of the slice: x: 4 (x_hi: 2, x_lo: 2; x = x_hi * 2 + x_lo), y: 4, z: 4, core: 2. Of those that a mesh axis runs over, the one named last changes fastest.
Arguments:
- tokens: bfloat16 [16384, 2048], P(('dp', 'head')), may hold values from -6 to 6
- cotangent: bfloat16 [16384, 2048], P(('dp', 'head')), may hold values from -6 to 6
- doc_spans: int32 [8, 3], P('dp'), may hold values from 1 to 16, 32 in all within a row
- norm1_gain: float32 [2048], replicated, may hold values from 0.5 to 1.5
- q_weight: bfloat16 [2048, 2048], P('dp', 'head'), may hold values from -0.125 to 0.125
- k_weight: bfloat16 [2048, 2048], P('dp', 'head'), may hold values from -0.125 to 0.125
- v_weight: bfloat16 [2048, 2048], P('dp', 'head'), may hold values from -0.125 to 0.125
- gate_out_weight: bfloat16 [2048, 2048], P('dp', 'head'), may hold values from -0.125 to 0.125
- decay_weight: bfloat16 [2048, 16, 2], P('dp', 'head'), may hold values from -0.125 to 0.125
- conv_weight: bfloat16 [3, 4, 2048], P(None, None, ('head', 'dp')), may hold values from -0.796875 to 0.796875
- gate_params: float32 [2, 16], P(None, 'head'), may hold values from -4 to 0
- out_gain: float32 [128], replicated, may hold values from 0.5 to 1.5
- out_weight: bfloat16 [2048, 2048], P('dp', 'head'), may hold values from -0.1875 to 0.1875
- norm2_gain: float32 [2048], replicated, may hold values from 0.5 to 1.5
- gate_weight: bfloat16 [2048, 5632], P('dp', 'head'), may hold values from -0.125 to 0.125
- up_weight: bfloat16 [2048, 5632], P('dp', 'head'), may hold values from -0.125 to 0.125
- down_weight: bfloat16 [2048, 5632], P('dp', 'head'), may hold values from -0.15625 to 0.15625
Outputs:
- block_out: bfloat16 [16384, 2048], P(('dp', 'head'))
- tokens_grad: float32 [16384, 2048], P(('dp', 'head'))
- norm1_gain_grad: float32 [2048], replicated
- q_weight_grad: float32 [2048, 2048], P('dp', 'head')
- k_weight_grad: float32 [2048, 2048], P('dp', 'head')
- v_weight_grad: float32 [2048, 2048], P('dp', 'head')
- gate_out_weight_grad: float32 [2048, 2048], P('dp', 'head')
- decay_weight_grad: float32 [2048, 16, 2], P('dp', 'head')
- conv_weight_grad: float32 [3, 4, 2048], P(None, None, ('head', 'dp'))
- gate_params_grad: float32 [2, 16], P(None, 'head')
- out_gain_grad: float32 [128], replicated
- out_weight_grad: float32 [2048, 2048], P('dp', 'head')
- norm2_gain_grad: float32 [2048], replicated
- gate_weight_grad: float32 [2048, 5632], P('dp', 'head')
- up_weight_grad: float32 [2048, 5632], P('dp', 'head')
- down_weight_grad: float32 [2048, 5632], P('dp', 'head')
The draws below stay inside these ranges and needn't reach their ends.
Inputs may be any that keep to these rules, and one draw needn't show every extreme that they name: `doc_spans`: each group's 3 lengths sum to 32, and the longest is exactly half of that.
All inputs are finite; a program needn't handle non-finite values.
Results may differ from the reference program's by a relative error of at most 0.033.
Values may be sent and summed in bfloat16 or wider, within the bound.
No kernel may reach another device: no remote copies, remote signals or barrier semaphores. Data moves between devices by JAX's collectives and lax.ppermute only.
A program may use at most 256 MiB of HBM per device.

```python
import math
from functools import partial
import jax
import jax.numpy as jnp
import numpy as np
from jax import lax

D = 2048
HEADS = 16
HEAD_DIM = 128
FF = 5632
SPAN = 64
CONV = 4
DOCS = 3
TOK_GRP = 2048
GROUPS = 8
TOKENS = 16384


def levels(rng, extent, cuts, least, top_value):
    level, own = 1.0, jax.random.fold_in(rng, 6)
    for position, parts in cuts:
        heights = jnp.exp(jax.random.uniform(jax.random.fold_in(own, position), (parts,), jnp.float32, least / len(cuts), top_value / len(cuts)))
        level = level * jnp.repeat(heights, extent[position] // parts).reshape([-1 if axis == position else 1 for axis in range(len(extent))])
    return level


def split_up(amount, total, reach, skew):
    weights = [(1 << 20) // math.isqrt(standing ** skew) + 1 for standing in range(2, amount + 1)]
    rest, counts = total - reach - (amount - 1), [1] * (amount - 1)
    while rest > 0:
        candidates = [i for i in range(amount - 1) if counts[i] < reach]
        pool, remaining = sum([weights[i] for i in candidates]), rest
        for i in candidates:
            more = min(reach - counts[i], max(1, remaining * weights[i] // pool), rest)
            counts[i] = counts[i] + more
            rest = rest - more
    return np.array([reach] + counts)


def ragged(stream_key, count, total, most, lean):
    if count == 2:
        one = jax.random.randint(stream_key, (), max(1, total - most), min(most, total - 1) + 1)
        return jnp.stack([one, total - one])
    lengths = jnp.asarray(split_up(count, total, most, lean), jnp.int32)
    couples = (count - 1) // 2
    giver, receiver = lengths[1:1 + 2 * couples:2], lengths[2:2 + 2 * couples:2]
    margin = jnp.minimum(giver - 1, most - receiver)
    moved = jax.random.randint(jax.random.fold_in(stream_key, 1), (couples,), 0, 1 << 20) % (margin + 1)
    lengths = lengths.at[1:1 + 2 * couples:2].set(giver - moved).at[2:2 + 2 * couples:2].set(receiver + moved)
    return lengths[jax.random.permutation(jax.random.fold_in(stream_key, 2), count)]


def centred(own_key, dims, deviation, most, cuts=(), held_as=jnp.bfloat16):
    values = deviation * jax.random.normal(own_key, dims, jnp.float32)
    if cuts:
        values = values * levels(own_key, dims, cuts, -0.22, 0.18)
    return jnp.clip(values, -most, most).astype(held_as)


def setup_inputs(seed: int = 0) -> dict:
    keys = jax.random.split(jax.random.key(seed), 18)
    tokens = centred(keys[0], (TOKENS, D), 1.0, 6.0, ((0, 128),))
    cotangent = centred(keys[1], (TOKENS, D), 1.0, 6.0, ((0, 128),))
    doc_spans = jax.vmap(lambda own: ragged(own, DOCS, TOK_GRP // SPAN, TOK_GRP // SPAN // 2, 2))(jax.random.split(keys[2], GROUPS)).reshape((GROUPS, DOCS)).astype(jnp.int32)
    norm1_gain = jnp.clip(1.0 + 0.1 * jax.random.normal(keys[3], (D,), jnp.float32), 0.5, 1.5)
    q_weight = centred(keys[4], (D, D), D ** -0.5, 0.125, ((0, 8), (1, 16)))
    k_weight = centred(keys[5], (D, D), D ** -0.5, 0.125, ((0, 8), (1, 16)))
    v_weight = centred(keys[6], (D, D), D ** -0.5, 0.125, ((0, 8), (1, 16)))
    gate_out_weight = centred(keys[7], (D, D), D ** -0.5, 0.125, ((0, 8), (1, 16)))
    decay_weight = centred(keys[8], (D, HEADS, 2), D ** -0.5, 0.125, ((0, 8), (1, 16)))
    conv_weight = jnp.clip(jax.random.uniform(keys[9], (3, CONV, D), jnp.float32, -0.796875, 0.796875) * levels(keys[9], (3, CONV, D), ((2, 128),), -0.4, 0.0), -0.796875, 0.796875).astype(jnp.bfloat16)
    gate_params = jnp.clip(-4.0 + 4.0 * jax.random.uniform(keys[10], (2, HEADS), jnp.float32) ** levels(keys[10], (2, HEADS), ((1, 16),), -0.2, 0.2), -4.0, 0.0)
    out_gain = jnp.clip(1.0 + 0.1 * jax.random.normal(keys[11], (HEAD_DIM,), jnp.float32), 0.5, 1.5)
    out_weight = centred(keys[12], (D, D), (D // 2) ** -0.5, 0.1875, ((0, 8), (1, 16)))
    norm2_gain = jnp.clip(1.0 + 0.1 * jax.random.normal(keys[13], (D,), jnp.float32), 0.5, 1.5)
    gate_weight = centred(keys[14], (D, FF), D ** -0.5, 0.125, ((0, 8), (1, 16)))
    up_weight = centred(keys[15], (D, FF), D ** -0.5, 0.125, ((0, 8), (1, 16)))
    down_weight = centred(keys[16], (D, FF), (FF // 4) ** -0.5, 0.15625, ((0, 8), (1, 16)))
    return {"tokens": tokens, "cotangent": cotangent, "doc_spans": doc_spans, "norm1_gain": norm1_gain, "q_weight": q_weight, "k_weight": k_weight, "v_weight": v_weight, "gate_out_weight": gate_out_weight, "decay_weight": decay_weight, "conv_weight": conv_weight, "gate_params": gate_params, "out_gain": out_gain, "out_weight": out_weight, "norm2_gain": norm2_gain, "gate_weight": gate_weight, "up_weight": up_weight, "down_weight": down_weight}


@jax.custom_vjp
def low(v):
    return lax.optimization_barrier(v.astype(jnp.bfloat16)).astype(jnp.float32)

@jax.custom_vjp
def low_back(v):
    return v

def low_keep(v):
    return (low(v), None)

def low_pass(kept, grad):
    return (grad,)

def back_keep(v):
    return (v, None)

def back_low(kept, grad):
    return (low(grad),)
low.defvjp(low_keep, low_pass)
low_back.defvjp(back_keep, back_low)

def product(form, left, right):
    return jnp.einsum(form, left, right, precision=lax.Precision.HIGHEST, preferred_element_type=jnp.float32)

def mat_product(left, right):
    return jnp.dot(left, right, precision=lax.Precision.HIGHEST, preferred_element_type=jnp.float32)

def rms_rows(values, gain):
    return values * lax.rsqrt(lax.optimization_barrier(jnp.mean(values * values, axis=-1, keepdims=True)) + 1e-05) * gain

def doc_masks(doc_lengths, seq_length, block_len, tap_count):
    doc_bounds = (jnp.cumsum(doc_lengths)[:-1] * block_len).astype(jnp.int32)
    positions = jnp.arange(seq_length, dtype=jnp.int32)
    doc_index = lax.optimization_barrier(jnp.sum((positions[:, None] >= doc_bounds[None, :]).astype(jnp.int32), axis=1))
    same_doc = []
    for offset in range(1, tap_count):
        earlier_doc = jnp.concatenate([jnp.full((offset,), -1, jnp.int32), doc_index[:seq_length - offset]])
        same_doc.append((earlier_doc == doc_index).astype(jnp.float32))
    block_starts = jnp.arange(seq_length // block_len, dtype=jnp.int32) * block_len
    doc_starts = jnp.any(block_starts[:, None] == doc_bounds[None, :], axis=1) | (block_starts == 0)
    carry_mask = 1.0 - doc_starts.astype(jnp.float32)
    return (same_doc, carry_mask)

def short_conv(raw_in, tap_weights, same_doc):
    tap_count = tap_weights.shape[0]
    seq_length = raw_in.shape[0]
    summed = raw_in * tap_weights[tap_count - 1]
    for offset in range(1, tap_count):
        shifted = jnp.concatenate([jnp.zeros((offset, raw_in.shape[1]), raw_in.dtype), raw_in[:seq_length - offset]], axis=0)
        summed = summed + shifted * same_doc[offset - 1][:, None] * tap_weights[tap_count - 1 - offset]
    return jax.nn.silu(summed)

def delta_head(queries, keys_in, values_in, beta_gate, decay_log, carry_mask, block_len):
    seq_length, head_width = queries.shape
    block_count = seq_length // block_len
    queries = queries.reshape(block_count, block_len, head_width)
    keys_in = keys_in.reshape(block_count, block_len, head_width)
    values_in = values_in.reshape(block_count, block_len, head_width)
    beta_gate = beta_gate.reshape(block_count, block_len)
    log_decay_sum = jnp.cumsum(decay_log.reshape(block_count, block_len), axis=1)
    positions = jnp.arange(block_len)
    lower_mask = positions[:, None] >= positions[None, :]
    strict_mask = positions[:, None] > positions[None, :]
    log_gap = log_decay_sum[:, :, None] - log_decay_sum[:, None, :]
    decay_mask = jnp.where(lower_mask, jnp.exp(jnp.where(lower_mask, log_gap, 0.0)), 0.0)
    keys_beta = keys_in * beta_gate[:, :, None]
    strict_part = jnp.where(strict_mask, product('cip,cjp->cij', keys_beta, keys_in) * decay_mask, 0.0)
    identity = jnp.eye(block_len, dtype=jnp.float32)
    inverse = identity - strict_part
    rounds_left = block_len.bit_length() - 2
    nil_power = product('cij,cjk->cik', strict_part, strict_part)
    for doubling in range(rounds_left):
        inverse = product('cij,cjk->cik', inverse, identity + nil_power)
        if doubling + 1 < rounds_left:
            nil_power = product('cij,cjk->cik', nil_power, nil_power)
    fresh_base = product('cij,cjp->cip', inverse, values_in * beta_gate[:, :, None])
    key_weighted = product('cij,cjp->cip', inverse, keys_beta * jnp.exp(log_decay_sum)[:, :, None])
    inner_scores = jnp.where(lower_mask, product('cip,cjp->cij', queries, keys_in) * decay_mask, 0.0)
    query_faded = queries * jnp.exp(log_decay_sum)[:, :, None]
    key_tail = jnp.exp(log_decay_sum[:, -1:] - log_decay_sum)[:, :, None] * keys_in
    span_decay = jnp.exp(log_decay_sum[:, -1])

    def span_step(state_mat, pieces):
        base_now, weighted_now, scores_now, faded_now, tail_now, decay_now, carry_now = pieces
        state_mat = state_mat * carry_now
        fresh_vals = base_now - product('ij,jk->ik', weighted_now, state_mat)
        span_out = product('ij,jk->ik', faded_now, state_mat) + product('ij,jk->ik', scores_now, fresh_vals)
        state_mat = state_mat * decay_now + product('ip,iv->pv', tail_now, fresh_vals)
        return (state_mat, span_out)
    state_start = jnp.zeros((head_width, head_width), jnp.float32)
    _, span_outs = lax.scan(jax.checkpoint(span_step), state_start, (fresh_base, key_weighted, inner_scores, query_faded, key_tail, span_decay, carry_mask))
    return span_outs.reshape(seq_length, head_width)

def token_mixer(q_raw, k_raw, v_raw, gate_raw, decay_raw, conv_taps, gate_par, out_gain, doc_lengths, block_len):
    seq_length = q_raw.shape[0]
    head_count = gate_par.shape[1]
    head_width = q_raw.shape[1] // head_count
    same_doc, carry_mask = doc_masks(doc_lengths, seq_length, block_len, conv_taps.shape[1])
    queries = short_conv(q_raw, conv_taps[0], same_doc).reshape(seq_length, head_count, head_width)
    keys_in = short_conv(k_raw, conv_taps[1], same_doc).reshape(seq_length, head_count, head_width)
    values_in = short_conv(v_raw, conv_taps[2], same_doc).reshape(seq_length, head_count, head_width)
    queries = queries * lax.rsqrt(lax.optimization_barrier(jnp.sum(queries * queries, axis=-1, keepdims=True)) + 1e-06) * head_width ** (-0.5)
    keys_in = keys_in * lax.rsqrt(lax.optimization_barrier(jnp.sum(keys_in * keys_in, axis=-1, keepdims=True)) + 1e-06)
    gate_pair = decay_raw.reshape(seq_length, head_count, 2)
    beta_gate = jax.nn.sigmoid(gate_pair[:, :, 1])
    decay_log = -jnp.exp(gate_par[0]) * jax.nn.softplus(gate_pair[:, :, 0] + gate_par[1])
    per_head = jax.vmap(partial(delta_head, carry_mask=carry_mask, block_len=block_len), in_axes=(1, 1, 1, 1, 1), out_axes=1)
    core_out = per_head(queries, keys_in, values_in, beta_gate, decay_log)
    scaled = core_out * lax.rsqrt(lax.optimization_barrier(jnp.mean(core_out * core_out, axis=-1, keepdims=True)) + 1e-05) * out_gain
    gate_heads = gate_raw.reshape(seq_length, head_count, head_width)
    return (scaled * jax.nn.silu(gate_heads)).reshape(seq_length, head_count * head_width)

def block_forward(doc_spans, inputs, gain_one, w_query, w_key, w_value, w_outgate, w_decay, w_conv, gate_par, out_gain, w_out, gain_two, w_gate, w_up, w_down):
    model_width = inputs.shape[1]
    head_count = gate_par.shape[1]
    normed1 = low(rms_rows(inputs, gain_one))
    q_raw = low_back(mat_product(normed1, w_query))
    k_raw = low_back(mat_product(normed1, w_key))
    v_raw = low_back(mat_product(normed1, w_value))
    go_raw = low_back(mat_product(normed1, w_outgate))
    decay_raw = low_back(mat_product(normed1, w_decay.reshape(model_width, 2 * head_count)))
    group_count = doc_spans.shape[0]
    group_len = inputs.shape[0] // group_count

    def split_groups(values):
        return values.reshape(group_count, group_len, values.shape[1])

    def per_group(pieces):
        return token_mixer(pieces[0], pieces[1], pieces[2], pieces[3], pieces[4], w_conv, gate_par, out_gain, pieces[5], SPAN)
    mixed = lax.map(per_group, (split_groups(q_raw), split_groups(k_raw), split_groups(v_raw), split_groups(go_raw), split_groups(decay_raw), doc_spans))
    mixed = low(mixed.reshape(inputs.shape[0], model_width))
    attn = low_back(mat_product(mixed, w_out.T))
    resid = inputs + attn
    normed2 = low(rms_rows(resid, gain_two))
    gate_pre = low_back(mat_product(normed2, w_gate))
    up_pre = low_back(mat_product(normed2, w_up))
    hidden = low(jax.nn.silu(gate_pre) * up_pre)
    return resid + mat_product(hidden, w_down.T)

def reference(tokens, cotangent, doc_spans, norm1_gain, q_weight, k_weight, v_weight, gate_out_weight, decay_weight, conv_weight, gate_params, out_gain, out_weight, norm2_gain, gate_weight, up_weight, down_weight):
    primals = tuple((a.astype(jnp.float32) for a in (tokens, norm1_gain, q_weight, k_weight, v_weight, gate_out_weight, decay_weight, conv_weight, gate_params, out_gain, out_weight, norm2_gain, gate_weight, up_weight, down_weight)))
    result, pullback = jax.vjp(partial(block_forward, doc_spans), *primals)
    grads = pullback(cotangent.astype(jnp.float32))
    return (result.astype(jnp.bfloat16), grads[0], grads[1], grads[2], grads[3], grads[4], grads[5], grads[6], grads[7], grads[8], grads[9], grads[10], grads[11], grads[12], grads[13], grads[14])
```

```python
from functools import partial

import jax
import jax.numpy as jnp
from jax import lax
from jax.experimental import pallas as pl
from jax.experimental.pallas import tpu as pltpu

CHUNK = 128
BATCH = 4
ROWS_A = 80
ROWS_B = 48
GATE_ALONE = 9
VMEM_MAX = 56 * 1024 * 1024


def split(value):
    high = value.astype(jnp.bfloat16)
    return high, (value - high.astype(jnp.float32)).astype(jnp.bfloat16)


def left_pair(value):
    return jnp.concatenate(split(value), axis=1)


def right_pair(value):
    high, low = split(value)
    wide = jnp.concatenate([high, low], axis=1)
    return jnp.concatenate([wide, wide], axis=0)


def right_pair_t(value):
    high, low = split(value)
    return jnp.concatenate(
        [jnp.concatenate([high, high], axis=1), jnp.concatenate([low, low], axis=1)], axis=0
    )


def fold(wide):
    half = wide.shape[1] // 2
    return wide[:, :half] + wide[:, half:]


def mul_pairs(left, right):
    return fold(jnp.dot(left, right, preferred_element_type=jnp.float32))


def mul(left, right):
    return mul_pairs(left_pair(left), right_pair(right))


def mul_t(left, right):
    return fold(
        lax.dot_general(
            left_pair(left),
            right_pair_t(right),
            (((1,), (1,)), ((), ())),
            preferred_element_type=jnp.float32,
        )
    )


def iotas(rows=CHUNK, cols=CHUNK):
    return (
        lax.broadcasted_iota(jnp.int32, (rows, cols), 0),
        lax.broadcasted_iota(jnp.int32, (rows, cols), 1),
    )


def silu_parts(value):
    gate = jax.nn.sigmoid(value)
    return gate, value * gate


def tap_masks(start_first, start_second, row_index):
    keeps = []
    for offset in range(1, 4):
        first = jnp.where(row_index < offset, 1.0 - start_first, 1.0)
        second = jnp.where(
            (row_index >= CHUNK // 2) & (row_index < CHUNK // 2 + offset), 1.0 - start_second, 1.0
        )
        keeps.append(first * second)
    return keeps


def shifted_rows(current, before, keeps):
    joined = jnp.concatenate([before, current], axis=0)
    return [current] + [
        pltpu.roll(joined, offset, 0)[8:] * keeps[offset - 1] for offset in range(1, 4)
    ]


def conv_rows(rows_by_offset, taps):
    total = rows_by_offset[0] * taps[3:4]
    for offset in range(1, 4):
        total = total + rows_by_offset[offset] * taps[3 - offset : 4 - offset]
    return total


def chunk_cols(rows):
    return jnp.transpose(jnp.concatenate([rows, jnp.zeros((CHUNK - 8, CHUNK), jnp.float32)], axis=0))


def decay_matrix(rows, cols, start_second):
    row_index, col_index = iotas()
    gap = cols[:, 0:1] - rows[0:1, :]
    lower = row_index >= col_index
    cross = (row_index >= CHUNK // 2) & (col_index < CHUNK // 2)
    decay = jnp.where(lower, jnp.exp(jnp.where(lower, gap, 0.0)), 0.0)
    return decay * jnp.where(cross, 1.0 - start_second, 1.0)


def head_rows(raw_refs, place_ref, chunk, part):
    def load(start, count):
        rows = pl.ds(pl.multiple_of(start, 8), count)
        return jnp.where(half == 0, raw_refs[0][rows, lanes], raw_refs[1][rows, lanes])

    lanes = slice(None) if part == GATE_ALONE else slice(part * CHUNK, (part + 1) * CHUNK)
    half = place_ref[2, chunk]
    current = jnp.concatenate(
        [load(place_ref[0, chunk], ROWS_A), load(place_ref[1, chunk], ROWS_B)], axis=0
    )
    if part > 2:
        return current
    earlier = jnp.maximum(chunk - 1, 0)
    half = place_ref[2, earlier]
    return current, load(place_ref[1, earlier] + ROWS_B - 8, 8)


def put_rows(out_ref, place_ref, chunk, lanes, value):
    half = place_ref[2, chunk]
    first = pl.ds(pl.multiple_of(place_ref[0, chunk], 16), ROWS_A)
    second = pl.ds(pl.multiple_of(place_ref[1, chunk], 16), ROWS_B)
    out_ref[half, first, lanes] = value[:ROWS_A]
    out_ref[half, second, lanes] = value[ROWS_A:]


def spread_sum(rows, matrix):
    high, rest = split(rows)
    mid = rest
    low = (rows - high.astype(jnp.float32) - mid.astype(jnp.float32)).astype(jnp.bfloat16)
    parts = jnp.concatenate([high, mid, low, jnp.zeros_like(low)], axis=0)
    wide = jnp.dot(parts, matrix.astype(jnp.bfloat16), preferred_element_type=jnp.float32)
    return wide[:8] + wide[8:16] + wide[16:24]


def gate_rows(decay_cols, starts, params_ref):
    row_index, col_index = iotas()
    pair = jnp.transpose(decay_cols)[:8]
    position = col_index[:8]
    kind = row_index[:8]
    carry, same = 1.0 - starts[0], 1.0 - starts[1]
    second = position >= CHUNK // 2
    beta = jax.nn.sigmoid(pair[1:2])
    inside = pair[0:1] + params_ref[1, 0]
    soft = jax.nn.softplus(inside)
    decay_log = -jnp.exp(params_ref[0, 0] + jnp.zeros((8, CHUNK), jnp.float32)) * soft
    total = spread_sum(decay_log, (row_index <= col_index).astype(jnp.float32))
    end = total[:, CHUNK - 1 :]
    gam = jnp.exp(total) * carry * jnp.where(second, same, 1.0)
    tail = jnp.exp(end - total) * jnp.where(second, 1.0, same)
    span = jnp.exp(end) * carry * same
    rows = jnp.where(kind == 0, total, jnp.where(kind == 1, beta, jnp.where(kind == 2, gam, tail)))
    return jnp.where(kind == 4, span, rows)


def convolved(raw_refs, place_ref, starts, taps_ref, chunk, row_index):
    keeps = tap_masks(starts[0], starts[1], row_index)
    pieces = []
    for part in range(3):
        current, before = head_rows(raw_refs, place_ref, chunk, part)
        rows_by_offset = shifted_rows(current, before, keeps)
        pieces.append((rows_by_offset, conv_rows(rows_by_offset, taps_ref[part])))
    return keeps, pieces


def start_flags(starts_ref, chunk):
    return (
        starts_ref[2 * chunk].astype(jnp.float32),
        starts_ref[2 * chunk + 1].astype(jnp.float32),
    )


def normed_qkv(pieces):
    acts = [piece[1] * jax.nn.sigmoid(piece[1]) for piece in pieces]
    q_scale = lax.rsqrt(jnp.sum(acts[0] * acts[0], axis=-1, keepdims=True) + 1e-06)
    k_scale = lax.rsqrt(jnp.sum(acts[1] * acts[1], axis=-1, keepdims=True) + 1e-06)
    return acts[0] * q_scale * CHUNK ** (-0.5), acts[1] * k_scale, acts[2], q_scale, k_scale


def inverse_lower(stricts):
    row_index, col_index = iotas()
    eye = (row_index == col_index).astype(jnp.float32)
    near = row_index // 16 == col_index // 16
    powers = [jnp.where(near, strict, 0.0) for strict in stricts]
    inverses = [eye - power for power in powers]
    powers = [mul(power, power) for power in powers]
    for step in range(3):
        rights = [right_pair(power) for power in powers]
        if step < 2:
            stacks = [
                left_pair(jnp.concatenate([inverse, power], axis=0))
                for inverse, power in zip(inverses, powers)
            ]
            both = [mul_pairs(stack, right) for stack, right in zip(stacks, rights)]
            inverses = [inverse + pair[:CHUNK] for inverse, pair in zip(inverses, both)]
            powers = [pair[CHUNK:] for pair in both]
        else:
            inverses = [
                inverse + mul_pairs(left_pair(inverse), right)
                for inverse, right in zip(inverses, rights)
            ]
    for width in (16, 32, 64):
        beside = (row_index // (2 * width) == col_index // (2 * width)) & (
            row_index // width != col_index // width
        )
        crossed = [
            mul(inverse, jnp.where(beside, strict, 0.0))
            for inverse, strict in zip(inverses, stricts)
        ]
        inverses = [inverse - mul(cross, inverse) for cross, inverse in zip(crossed, inverses)]
    return inverses


def prepare_kernel(place_ref, starts_ref, params_ref, raw0_ref, raw1_ref, taps_ref,
                   rows_out_ref, inv_ref, kkf_ref, p_ref, uw_ref, m_ref, mt_ref, b_ref, r_ref, pu_ref):
    row_index, col_index = iotas()
    diagonal = (row_index == col_index).astype(jnp.float32)
    stricts, kept = [], []
    for member in range(BATCH):
        chunk = pl.program_id(0) * BATCH + member
        starts = start_flags(starts_ref, chunk)
        raw_refs = (raw0_ref, raw1_ref)
        _, pieces = convolved(raw_refs, place_ref, starts, taps_ref, chunk, row_index)
        queries, keys_in, values_in, _, _ = normed_qkv(pieces)
        rows = gate_rows(head_rows(raw_refs, place_ref, chunk, 4), starts, params_ref)
        rows_out_ref[member] = rows
        cols = chunk_cols(rows)
        decay = decay_matrix(rows, cols, starts[1])
        beta, gam, tail = cols[:, 1:2], cols[:, 2:3], cols[:, 3:4]
        scores = mul_t(jnp.concatenate([keys_in, queries], axis=0), keys_in)
        kkf = jnp.where(row_index > col_index, scores[:CHUNK] * decay, 0.0)
        inner = scores[CHUNK:] * decay
        stricts.append(kkf * beta)
        kkf_ref[member] = kkf
        p_ref[member] = inner
        pair = jnp.concatenate([values_in * beta, keys_in * (beta * gam)], axis=1)
        stack = jnp.concatenate([jnp.transpose(keys_in * tail), inner], axis=0)
        kept.append((pair, stack, diagonal * rows[4:5], queries * gam))
    inverses = inverse_lower(stricts)
    joined = [mul(inverse, pair) for inverse, (pair, _, _, _) in zip(inverses, kept)]
    both = [mul(stack, join) for join, (_, stack, _, _) in zip(joined, kept)]
    for member in range(BATCH):
        _, _, span, faded = kept[member]
        inv_ref[member] = inverses[member]
        uw_ref[member] = joined[member]
        state_map = span - both[member][:CHUNK, CHUNK:]
        m_ref[member] = left_pair(state_map)
        mt_ref[member] = left_pair(jnp.transpose(state_map))
        b_ref[member] = both[member][:CHUNK, :CHUNK]
        r_ref[member] = faded - both[member][CHUNK:, CHUNK:]
        pu_ref[member] = both[member][CHUNK:, :CHUNK]


def whole(shape):
    return pl.BlockSpec(shape, lambda *_: (0,) * len(shape))


def per_batch(shape, turned=False, steps=4):
    def place(step, *_):
        return ((steps - 1 - step) if turned else step,) + (0,) * (len(shape) - 1)

    return pl.BlockSpec(shape, place)


def shaped(shape, dtype=jnp.float32):
    return jax.ShapeDtypeStruct(shape, dtype)


def prepare(place, starts, params, raw0, raw1, taps):
    chunks = place.shape[1]
    square = (BATCH, CHUNK, CHUNK)
    wide = (BATCH, CHUNK, 2 * CHUNK)
    kinds = [((BATCH, 8, CHUNK), jnp.float32), (square, jnp.float32), (square, jnp.float32), (square, jnp.float32),
             (wide, jnp.float32), (wide, jnp.bfloat16), (wide, jnp.bfloat16), (square, jnp.float32),
             (square, jnp.float32), (square, jnp.float32)]
    return pl.pallas_call(
        prepare_kernel,
        grid_spec=pltpu.PrefetchScalarGridSpec(
            num_scalar_prefetch=3,
            grid=(chunks // BATCH,),
            in_specs=[whole(raw0.shape), whole(raw1.shape), whole(taps.shape)],
            out_specs=[per_batch(shape) for shape, _ in kinds],
        ),
        out_shape=[shaped((chunks,) + shape[1:], dtype) for shape, dtype in kinds],
        compiler_params=pltpu.CompilerParams(vmem_limit_bytes=VMEM_MAX),
        name="prepare",
    )(place, starts, params, raw0, raw1, taps)


def gate_rows_of(gate_refs, place_ref, chunk):
    return head_rows(gate_refs, place_ref, chunk, GATE_ALONE)


def scan_kernel(place_ref, m_ref, b_ref, r_ref, pu_ref, gate0_ref, gate1_ref, gain_ref,
                state_out_ref, core_ref, mixed_ref, stored_ref, state_ref):
    @pl.when(pl.program_id(0) == 0)
    def _():
        state_ref[...] = jnp.zeros_like(state_ref)

    state = state_ref[...]
    for member in range(BATCH):
        chunk = pl.program_id(0) * BATCH + member
        state_out_ref[member] = state
        pair = right_pair(state)
        core = mul_pairs(left_pair(r_ref[member]), pair) + pu_ref[member]
        state = mul_pairs(m_ref[member], pair) + b_ref[member]
        _, gate = silu_parts(gate_rows_of((gate0_ref, gate1_ref), place_ref, chunk))
        core_ref[member] = core
        scale = lax.rsqrt(jnp.mean(core * core, axis=-1, keepdims=True) + 1e-05)
        mixed = (core * scale * gain_ref[...] * gate).astype(jnp.bfloat16)
        mixed_ref[member] = mixed
        put_rows(stored_ref, place_ref, chunk, slice(None), mixed)
    state_ref[...] = state


def gate_columns(raw):
    return pl.BlockSpec((raw.shape[0], CHUNK), lambda *_: (0, 3))


def scan_states(place, m, b, r, pu, raw0, raw1, gain):
    chunks = m.shape[0]
    square = (BATCH, CHUNK, CHUNK)
    wide = (BATCH, CHUNK, 2 * CHUNK)
    stored = (2, raw0.shape[0], CHUNK)
    return pl.pallas_call(
        scan_kernel,
        grid_spec=pltpu.PrefetchScalarGridSpec(
            num_scalar_prefetch=1,
            grid=(chunks // BATCH,),
            in_specs=[per_batch(wide), per_batch(square), per_batch(square), per_batch(square),
                      gate_columns(raw0), gate_columns(raw1), whole((1, CHUNK))],
            out_specs=[per_batch(square)] * 3 + [whole(stored)],
            scratch_shapes=[pltpu.VMEM((CHUNK, CHUNK), jnp.float32)],
        ),
        out_shape=[shaped((chunks, CHUNK, CHUNK)), shaped((chunks, CHUNK, CHUNK)),
                   shaped((chunks, CHUNK, CHUNK), jnp.bfloat16), shaped(stored, jnp.bfloat16)],
        compiler_params=pltpu.CompilerParams(vmem_limit_bytes=VMEM_MAX),
        name="scan_states",
    )(place, m, b, r, pu, raw0, raw1, gain)


def back_scan_kernel(place_ref, mt_ref, r_ref, core_ref, gate0_ref, gate1_ref, dmixed_ref, gain_ref,
                     dcore_ref, dstate_out_ref, dgate_ref, dgain_ref, dstate_ref):
    step = pl.program_id(0)

    @pl.when(step == 0)
    def _():
        dstate_ref[...] = jnp.zeros_like(dstate_ref)
        dgain_ref[...] = jnp.zeros_like(dgain_ref)

    gain = gain_ref[...]
    dgain = jnp.zeros((8, CHUNK), jnp.float32)
    terms = []
    for member in reversed(range(BATCH)):
        chunk = (pl.num_programs(0) - 1 - step) * BATCH + member
        core = core_ref[member]
        raw_gate = gate_rows_of((gate0_ref, gate1_ref), place_ref, chunk)
        dmixed = dmixed_ref[member].astype(jnp.float32)
        gate, gated = silu_parts(raw_gate)
        scale = lax.rsqrt(jnp.mean(core * core, axis=-1, keepdims=True) + 1e-05)
        unit = core * scale
        dscaled = dmixed * gated
        dgate = dmixed * unit * gain * (gate * (1.0 + raw_gate * (1.0 - gate)))
        dgate_ref[member] = dgate.astype(jnp.bfloat16)
        product = dscaled * unit
        dgain = dgain + jnp.sum(product.reshape(CHUNK // 8, 8, CHUNK), axis=0)
        dunit = dscaled * gain
        dcore = scale * (dunit - unit * jnp.mean(dunit * unit, axis=-1, keepdims=True))
        dcore_ref[member] = dcore
        terms.append((member, mul(jnp.transpose(r_ref[member]), dcore)))
    dgain_ref[...] += dgain
    dstate = dstate_ref[...]
    for member, term in terms:
        dstate_out_ref[member] = dstate
        dstate = mul_pairs(mt_ref[member], right_pair(dstate)) + term
    dstate_ref[...] = dstate


def back_scan(place, mt, r, core, raw0, raw1, dmixed, gain):
    chunks = mt.shape[0]
    square = (BATCH, CHUNK, CHUNK)
    wide = (BATCH, CHUNK, 2 * CHUNK)
    turned = partial(per_batch, turned=True, steps=chunks // BATCH)
    return pl.pallas_call(
        back_scan_kernel,
        grid_spec=pltpu.PrefetchScalarGridSpec(
            num_scalar_prefetch=1,
            grid=(chunks // BATCH,),
            in_specs=[turned(wide), turned(square), turned(square),
                      gate_columns(raw0), gate_columns(raw1), turned(square), whole((1, CHUNK))],
            out_specs=[turned(square), turned(square), turned(square), whole((8, CHUNK))],
            scratch_shapes=[pltpu.VMEM((CHUNK, CHUNK), jnp.float32)],
        ),
        out_shape=[shaped((chunks, CHUNK, CHUNK)), shaped((chunks, CHUNK, CHUNK)),
                   shaped((chunks, CHUNK, CHUNK), jnp.bfloat16), shaped((8, CHUNK))],
        compiler_params=pltpu.CompilerParams(vmem_limit_bytes=VMEM_MAX),
        name="back_scan",
    )(place, mt, r, core, raw0, raw1, dmixed, gain)


def lane_sum(value):
    return jnp.sum(value, axis=1, keepdims=True)


def back_kernel(place_ref, starts_ref, params_ref, raw0_ref, raw1_ref, rows_ref, taps_ref, inv_ref, kkf_ref,
                p_ref, uw_ref, state_ref, dstate_ref, dcore_ref, dgate_ref,
                draw_ref, dtaps_ref, dparams_ref, next_ref):
    step = pl.program_id(0)
    row_index, col_index = iotas()
    lower = row_index >= col_index
    strict = row_index > col_index

    @pl.when(step == 0)
    def _():
        next_ref[...] = jnp.zeros_like(next_ref)
        dtaps_ref[...] = jnp.zeros_like(dtaps_ref)
        dparams_ref[...] = jnp.zeros_like(dparams_ref)

    raw_refs = (raw0_ref, raw1_ref)
    members = range(BATCH)
    setups = []
    for member in members:
        chunk = (pl.num_programs(0) - 1 - step) * BATCH + member
        starts = start_flags(starts_ref, chunk)
        keeps, pieces = convolved(raw_refs, place_ref, starts, taps_ref, chunk, row_index)
        queries, keys_in, values_in, q_scale, k_scale = normed_qkv(pieces)
        rows = rows_ref[member]
        cols = chunk_cols(rows)
        decay = decay_matrix(rows, cols, starts[1])
        setups.append((starts, keeps, pieces, queries, keys_in, values_in, q_scale, k_scale, rows, cols, decay))
    fresh = [
        uw_ref[i][:, :CHUNK] - mul(uw_ref[i][:, CHUNK:], state_ref[i]) for i in members
    ]
    dfresh = [
        mul(jnp.transpose(p_ref[i]), dcore_ref[i])
        + mul(setups[i][4] * setups[i][9][:, 3:4], dstate_ref[i])
        for i in members
    ]
    through = [
        mul_t(jnp.concatenate([dcore_ref[i], dfresh[i]], axis=0), state_ref[i]) for i in members
    ]
    dinner = [jnp.where(lower, mul_t(dcore_ref[i], fresh[i]), 0.0) for i in members]
    dkeys_tail = [mul_t(fresh[i], dstate_ref[i]) for i in members]
    dboth = [
        mul(
            jnp.transpose(inv_ref[i]),
            jnp.concatenate([dfresh[i], -through[i][CHUNK:]], axis=1),
        )
        for i in members
    ]
    dstrict = [jnp.where(strict, -mul_t(dboth[i], uw_ref[i]), 0.0) for i in members]
    stacked, crossed = [], []
    for i in members:
        queries, keys_in, cols, decay = setups[i][3], setups[i][4], setups[i][9], setups[i][10]
        dscores_n = dstrict[i] * decay * cols[:, 1:2]
        dscores = dinner[i] * decay
        stacked.append(
            mul(jnp.concatenate([dscores, dscores_n + jnp.transpose(dscores_n)], axis=0), keys_in)
        )
        crossed.append(mul(jnp.transpose(dscores), queries))
    for i in reversed(members):
        starts, keeps, pieces, queries, keys_in, values_in, q_scale, k_scale, rows, cols, _ = setups[i]
        beta, gam, tail = cols[:, 1:2], cols[:, 2:3], cols[:, 3:4]
        dqueries_faded = through[i][:CHUNK]
        dvalues_beta, dkeys_beta = dboth[i][:, :CHUNK], dboth[i][:, CHUNK:]
        keys_gam = keys_in * gam
        dqueries = stacked[i][:CHUNK] + dqueries_faded * gam
        dkeys = (
            stacked[i][CHUNK:]
            + crossed[i]
            + dkeys_beta * (beta * gam)
            + dkeys_tail[i] * tail
        )
        dvalues = dvalues_beta * beta

        dkkf = dstrict[i] * kkf_ref[i]
        flow = dkkf * beta + dinner[i] * p_ref[i]
        tail_term = lane_sum(dkeys_tail[i] * keys_in * tail)
        dbeta = lane_sum(dkkf + dvalues_beta * values_in + dkeys_beta * keys_gam)
        dsum = (
            lane_sum(flow + (dqueries_faded * queries + dkeys_beta * keys_in * beta) * gam)
            - tail_term
        )
        last = jnp.sum(tail_term) + jnp.sum(state_ref[i] * dstate_ref[i] * rows[4:5, 0:1])
        last_col = jnp.where(row_index[:, :1] == CHUNK - 1, last, 0.0)
        packed = jnp.where(
            col_index == 0, dsum + last_col, jnp.where(col_index == 1, dbeta, 0.0)
        )
        turned = jnp.transpose(packed)[:8]
        flow_rows = jnp.sum(flow, axis=0, keepdims=True)
        kind = row_index[:8]
        dtotal = jnp.where(kind == 0, turned - flow_rows, 0.0)
        dlog = spread_sum(dtotal, lower.astype(jnp.float32))[0:1]
        chunk = (pl.num_programs(0) - 1 - step) * BATCH + i
        pair = jnp.transpose(head_rows(raw_refs, place_ref, chunk, 4))[:8]
        inside = pair[0:1] + params_ref[1, 0]
        rate = -jnp.exp(params_ref[0, 0] + jnp.zeros((1, CHUNK), jnp.float32))
        dinside = dlog * rate * jax.nn.sigmoid(inside)
        beta_row = rows[1:2]
        dbeta_raw = turned[1:2] * beta_row * (1.0 - beta_row)
        drate = dlog * rate * jax.nn.softplus(inside)
        dparams_ref[...] += jnp.where(kind == 0, drate, jnp.where(kind == 1, dinside, 0.0))
        ddecay = jnp.where(kind == 0, dinside, jnp.where(kind == 1, dbeta_raw, 0.0))
        put_rows(draw_ref, place_ref, chunk, slice(3 * CHUNK, 4 * CHUNK), dgate_ref[i])
        put_rows(
            draw_ref, place_ref, chunk, slice(4 * CHUNK, 5 * CHUNK), chunk_cols(ddecay).astype(jnp.bfloat16)
        )

        d_scaled_q = dqueries * CHUNK ** (-0.5)
        gates = [jax.nn.sigmoid(piece[1]) for piece in pieces]
        unit_q, unit_k = pieces[0][1] * gates[0] * q_scale, pieces[1][1] * gates[1] * k_scale
        dact = [
            q_scale * (d_scaled_q - unit_q * lane_sum(d_scaled_q * unit_q)),
            k_scale * (dkeys - unit_k * lane_sum(dkeys * unit_k)),
            dvalues,
        ]
        for part in range(3):
            rows_by_offset, conv = pieces[part]
            gate = gates[part]
            dconv = dact[part] * (gate * (1.0 + conv * (1.0 - gate)))
            taps = taps_ref[part]
            after = next_ref[part]
            draw = dconv * taps[3:4]
            for offset in range(1, 4):
                kept = jnp.concatenate([dconv * keeps[offset - 1], after], axis=0)
                draw = draw + pltpu.roll(kept, CHUNK + 8 - offset, 0)[:CHUNK] * taps[3 - offset : 4 - offset]
            lanes = slice(part * CHUNK, (part + 1) * CHUNK)
            put_rows(draw_ref, place_ref, chunk, lanes, draw.astype(jnp.bfloat16))
            for offset in range(4):
                dtaps_ref[part, 3 - offset : 4 - offset] += jnp.sum(
                    dconv * rows_by_offset[offset], axis=0, keepdims=True
                )
            next_ref[part] = dconv[:8] * (1.0 - starts[0])


def back(place, starts, params, raw0, raw1, rows, taps, inverse, kkf, inner, joined, states, dstates, dcore, dgate):
    chunks = rows.shape[0]
    square = (BATCH, CHUNK, CHUNK)
    wide = (BATCH, CHUNK, 2 * CHUNK)
    turned = partial(per_batch, turned=True, steps=chunks // BATCH)
    draw = (2,) + raw0.shape
    return pl.pallas_call(
        back_kernel,
        grid_spec=pltpu.PrefetchScalarGridSpec(
            num_scalar_prefetch=3,
            grid=(chunks // BATCH,),
            in_specs=[whole(raw0.shape), whole(raw1.shape), turned((BATCH, 8, CHUNK)), whole(taps.shape),
                      turned(square), turned(square), turned(square), turned(wide), turned(square),
                      turned(square), turned(square), turned(square)],
            out_specs=[whole(draw), whole((3, 4, CHUNK)), whole((8, CHUNK))],
            scratch_shapes=[pltpu.VMEM((3, 8, CHUNK), jnp.float32)],
        ),
        out_shape=[shaped(draw, jnp.bfloat16), shaped((3, 4, CHUNK)), shaped((8, CHUNK))],
        compiler_params=pltpu.CompilerParams(vmem_limit_bytes=VMEM_MAX),
        name="back",
    )(place, starts, params, raw0, raw1, rows, taps, inverse, kkf, inner, joined, states, dstates, dcore, dgate)


def document_starts(doc_lengths, block_count):
    bounds = jnp.cumsum(doc_lengths)[:-1]
    blocks = jnp.arange(block_count, dtype=jnp.int32)
    opens = jnp.any(blocks[:, None] == bounds[None, :], axis=1) | (blocks == 0)
    return opens.astype(jnp.int32)


def mixer_forward(place, starts, params, raw0, raw1, taps, out_gain):
    rows, inverse, kkf, inner, joined, m, mt, b, r, pu = prepare(place, starts, params, raw0, raw1, taps)
    states, core, mixed, stored = scan_states(place, m, b, r, pu, raw0, raw1, out_gain)
    return mixed, stored, (rows, inverse, kkf, inner, joined, mt, r, states, core)


def mixer_backward(place, starts, params, raw0, raw1, taps, out_gain, kept, dmixed):
    rows, inverse, kkf, inner, joined, mt, r, states, core = kept
    dcore, dstates, dgate, dgain = back_scan(place, mt, r, core, raw0, raw1, dmixed, out_gain)
    draw, dtaps, dparams = back(
        place, starts, params, raw0, raw1, rows, taps, inverse, kkf, inner, joined, states, dstates, dcore, dgate
    )
    return draw, dtaps, dparams, dgain


from jax.sharding import PartitionSpec as P

LANES = 128
HALF = 384


def exchange_perm(count, shifted, sizes):
    pairs = []
    for target in range(count):
        source, scale, rest = 0, 1, target
        for size, offset in zip(reversed(sizes), reversed(shifted)):
            source += (rest % size + offset) % size * scale
            rest //= size
            scale *= size
        pairs.append((source, target))
    return pairs


def from_head(value, dz=0, dx=0, dc=0):
    return lax.ppermute(value, "head", exchange_perm(16, (dz, dx, dc), (4, 2, 2)))


def from_dp(value, dy=0, dx=0):
    return lax.ppermute(value, "dp", exchange_perm(8, (dy, dx), (4, 2)))


def gather_parts(value, take, cut):
    first, second = value[:cut], value[cut:]
    pair = jnp.concatenate([first, take(first, 0, 1)], axis=0)
    rings = [pair] + [take(pair, k, 0) for k in (1, 2, 3)]
    column = jnp.concatenate([second] + [take(second, k, 0) for k in (1, 2, 3)], axis=0)
    return rings, [column, take(column, 0, 1)]


def take_zx(value, ring, side):
    return from_head(value, dz=ring, dx=side)


def take_yx(value, ring, side):
    return from_dp(value, dy=ring, dx=side)


def gather_zx(value):
    rings, columns = gather_parts(value, take_zx, value.shape[0] * 5 // 8)
    return jnp.concatenate(rings + columns, axis=0)


def gather_dp(value):
    rings, columns = gather_parts(value, take_yx, value.shape[0] // 2)
    return jnp.concatenate(rings + columns, axis=0)


def wide(value):
    return value.astype(jnp.float32)


def narrow(value):
    return value.astype(jnp.bfloat16)


def reduce_parts(value, take, cut):
    rows = value.shape[0] // 8
    rest = rows - cut
    blocks = [value[2 * cut * k : 2 * cut * (k + 1)] for k in range(4)]
    near, far = value[8 * cut : 8 * cut + 4 * rest], value[8 * cut + 4 * rest :]
    summed = wide(blocks[0])
    for k in (1, 2, 3):
        summed = summed + wide(take(blocks[k], -k, 0))
    column = wide(near) + wide(take(far, 0, 1))
    first = (summed[:cut], take(narrow(summed[cut:]), 0, 1))
    second = (column[:rest],) + tuple(
        take(narrow(column[rest * k : rest * (k + 1)]), -k, 0) for k in (1, 2, 3)
    )
    return first, second


def reduce_zx(value):
    first, second = reduce_parts(value, take_zx, value.shape[0] // 8 * 5 // 8)
    return first + second


def reduce_dp(value):
    first, second = reduce_parts(value, take_yx, value.shape[0] // 16)
    return jnp.concatenate(
        [first[0] + wide(first[1]), second[0] + wide(second[1]) + wide(second[2]) + wide(second[3])], axis=0
    )


def ring_sum(value, take, position):
    pieces = [value] + [take(value, k, 0) for k in (1, 2, 3)]
    stacked = jnp.stack(pieces + pieces)
    ordered = lax.dynamic_slice_in_dim(stacked, (4 - position) % 4, 4, 0)
    return (ordered[0] + ordered[1]) + (ordered[2] + ordered[3])


def whole_call(kernel, out_shape, name, scalars, *arrays, scratch=()):
    outs = out_shape if isinstance(out_shape, (list, tuple)) else [out_shape]
    return pl.pallas_call(
        kernel,
        grid_spec=pltpu.PrefetchScalarGridSpec(
            num_scalar_prefetch=len(scalars),
            grid=(1,),
            in_specs=[whole(array.shape) for array in arrays],
            out_specs=[whole(out.shape) for out in outs],
            scratch_shapes=list(scratch),
        ),
        out_shape=list(outs),
        compiler_params=pltpu.CompilerParams(vmem_limit_bytes=VMEM_MAX),
        name=name,
    )(*scalars, *arrays)


def block_lanes(position):
    return slice(position * LANES, (position + 1) * LANES)


def placed_lanes(order_ref, position):
    return pl.ds(pl.multiple_of(order_ref[position] * LANES, LANES), LANES)


def rms_parts(values):
    scale = lax.rsqrt(jnp.mean(values * values, axis=-1, keepdims=True) + 1e-05)
    return scale, values * scale


def rms_back(grad, gain, scale, unit):
    inner = grad * gain
    return scale * (inner - unit * jnp.mean(inner * unit, axis=-1, keepdims=True))


def enter_kernel(order_ref, tokens_ref, cot_ref, gains_ref, normed_ref, rows_ref, grad_ref, gains_out_ref):
    for position in range(16):
        here, there = block_lanes(position), placed_lanes(order_ref, position)
        rows_ref[:, here] = tokens_ref[:, there]
        grad_ref[:, here] = cot_ref[:, there]
        gains_out_ref[:, here] = gains_ref[:, there]
    _, unit = rms_parts(wide(rows_ref[...]))
    normed_ref[...] = narrow(unit * gains_out_ref[0:1])


def attn_kernel(heads_ref, mixed_ref, first0_ref, first1_ref, second0_ref, second1_ref, rows_ref, gains_ref,
                resid_ref, normed_ref, total_ref):
    step = pl.program_id(0)

    @pl.when(step == 0)
    def _():
        total_ref[...] = wide(rows_ref[...])

    pair = jnp.concatenate([mixed_ref[heads_ref[0, step]], mixed_ref[heads_ref[1, step]]], axis=1)
    cut = first0_ref.shape[0]
    weights = jnp.concatenate([first0_ref[...], first1_ref[...]], axis=1)
    total_ref[:, :cut] += against(pair, weights)
    weights = jnp.concatenate([second0_ref[...], second1_ref[...]], axis=1)
    total_ref[:, cut:] += against(pair, weights)

    @pl.when(step == pl.num_programs(0) - 1)
    def _():
        resid = total_ref[...]
        resid_ref[...] = resid
        _, unit = rms_parts(resid)
        normed_ref[...] = narrow(unit * gains_ref[1:2])


def out_weight_specs(cut, rest):
    first = pl.BlockSpec((cut, LANES), lambda step, *_: (step, 0))
    second = pl.BlockSpec((rest, LANES), lambda step, *_: (step % 2 * 4 + step // 2, 0))
    return [first, first, second, second]


def attend(heads, received, out_parts, rows, gains):
    cut, rest = out_parts[0].shape[0] // 8, out_parts[2].shape[0] // 8
    shape = rows.shape
    return pl.pallas_call(
        attn_kernel,
        grid_spec=pltpu.PrefetchScalarGridSpec(
            num_scalar_prefetch=1,
            grid=(8,),
            in_specs=[whole(received.shape)] + out_weight_specs(cut, rest) + [whole(shape), whole(gains.shape)],
            out_specs=[whole(shape), whole(shape)],
            scratch_shapes=[pltpu.VMEM(shape, jnp.float32)],
        ),
        out_shape=[shaped(shape), shaped(shape, jnp.bfloat16)],
        compiler_params=pltpu.CompilerParams(vmem_limit_bytes=VMEM_MAX),
        name="attend",
    )(heads, received, *out_parts, rows, gains)


def total_of(refs):
    first = refs[0][...] + wide(refs[1][...])
    second = refs[2][...] + wide(refs[3][...]) + wide(refs[4][...]) + wide(refs[5][...])
    return jnp.concatenate([first, second], axis=0)


def middle_kernel(heads_ref, *refs):
    pieces, (resid_ref, cot_ref, gains_ref, first0_ref, first1_ref, second0_ref, second1_ref) = refs[:6], refs[6:13]
    dresid_ref, dattn_ref, dgain_ref, dmixed_ref = refs[13:]
    step = pl.program_id(0)

    @pl.when(step == 0)
    def _():
        grad = total_of(pieces)
        scale, unit = rms_parts(resid_ref[...])
        dgain_ref[...] = jnp.sum(grad * unit, axis=0, keepdims=True)
        dresid = wide(cot_ref[...]) + rms_back(grad, gains_ref[1:2], scale, unit)
        dresid_ref[...] = dresid
        dattn_ref[...] = narrow(dresid)

    cut = first0_ref.shape[0]
    dattn = dattn_ref[...]
    weights = jnp.concatenate([first0_ref[...], first1_ref[...]], axis=1)
    total = plain_product(dattn[:, :cut], weights)
    weights = jnp.concatenate([second0_ref[...], second1_ref[...]], axis=1)
    total = narrow(total + plain_product(dattn[:, cut:], weights))
    dmixed_ref[heads_ref[0, step]] = total[:, :LANES]
    dmixed_ref[heads_ref[1, step]] = total[:, LANES:]


def middle(heads, pieces, resid, cot, gains, out_parts):
    cut, rest = out_parts[0].shape[0] // 8, out_parts[2].shape[0] // 8
    shape = resid.shape
    mixed_shape = (16, shape[0], LANES)
    return pl.pallas_call(
        middle_kernel,
        grid_spec=pltpu.PrefetchScalarGridSpec(
            num_scalar_prefetch=1,
            grid=(8,),
            in_specs=[whole(piece.shape) for piece in pieces]
            + [whole(shape), whole(shape), whole(gains.shape)]
            + out_weight_specs(cut, rest),
            out_specs=[whole(shape), whole(shape), whole((1, shape[1])), whole(mixed_shape)],
        ),
        out_shape=[shaped(shape), shaped(shape, jnp.bfloat16), shaped((1, shape[1])),
                   shaped(mixed_shape, jnp.bfloat16)],
        compiler_params=pltpu.CompilerParams(vmem_limit_bytes=VMEM_MAX),
        name="middle",
    )(heads, *pieces, resid, cot, gains, *out_parts)


def leave_kernel(order_ref, *refs):
    pieces, (resid_ref, out_ref) = refs[:6], refs[6:]
    total = narrow(resid_ref[...] + total_of(pieces))
    for position in range(16):
        out_ref[:, placed_lanes(order_ref, position)] = total[:, block_lanes(position)]


def finish_kernel(order_ref, *refs):
    pieces, (rows_ref, dresid_ref, gains_ref, out_ref) = refs[:6], refs[6:]
    scale, unit = rms_parts(wide(rows_ref[...]))
    total = dresid_ref[...] + rms_back(total_of(pieces), gains_ref[0:1], scale, unit)
    for position in range(16):
        out_ref[:, placed_lanes(order_ref, position)] = total[:, block_lanes(position)]


def feed_kernel(normed_ref, cot_ref, gu0_ref, down0_ref, gu1_ref, down1_ref,
                out_ref, dnormed_ref, hidden_ref, dpre_ref):
    normed, cot = normed_ref[...], cot_ref[...]
    out, dnormed = 0.0, 0.0
    for half, (gu_ref, down_ref) in enumerate(((gu0_ref, down0_ref), (gu1_ref, down1_ref))):
        pre = plain_product(normed, gu_ref[...])
        gate, up = pre[:, :HALF], pre[:, HALF:]
        dhidden = plain_product(cot, down_ref[...])
        sigmoid = jax.nn.sigmoid(gate)
        act = gate * sigmoid
        hidden = narrow(act * up)
        dgate = narrow(dhidden * up * sigmoid * (1.0 + gate * (1.0 - sigmoid)))
        dpre = jnp.concatenate([dgate, narrow(dhidden * act)], axis=1)
        hidden_ref[:, half * HALF : (half + 1) * HALF] = hidden
        dpre_ref[:, 2 * half * HALF : 2 * (half + 1) * HALF] = dpre
        out = out + against(hidden, down_ref[...])
        dnormed = dnormed + against(dpre, gu_ref[...])
    out_ref[...] = narrow(out)
    dnormed_ref[...] = narrow(dnormed)


def feed(normed, cot, own, other):
    rows, width = normed.shape
    step = 256
    row_block = pl.BlockSpec((step, width), lambda i: (i, 0))
    gate_up = pl.BlockSpec((width, 2 * HALF), lambda i: (0, 0))
    down = pl.BlockSpec((width, HALF), lambda i: (0, 2))
    return pl.pallas_call(
        feed_kernel,
        grid=(rows // step,),
        in_specs=[row_block, row_block, gate_up, down, gate_up, down],
        out_specs=[row_block, row_block, pl.BlockSpec((step, 2 * HALF), lambda i: (i, 0)),
                   pl.BlockSpec((step, 4 * HALF), lambda i: (i, 0))],
        out_shape=[shaped((rows, width), jnp.bfloat16), shaped((rows, width), jnp.bfloat16),
                   shaped((rows, 2 * HALF), jnp.bfloat16), shaped((rows, 4 * HALF), jnp.bfloat16)],
        compiler_params=pltpu.CompilerParams(vmem_limit_bytes=VMEM_MAX),
        name="feed",
    )(normed, cot, own, own, other, other)


def plain_product(left, right):
    return jnp.dot(left, right, preferred_element_type=jnp.float32)


def against(left, right):
    return lax.dot_general(left, right, (((1,), (1,)), ((), ())), preferred_element_type=jnp.float32)


def over_rows(left, right):
    return lax.dot_general(left, right, (((0,), (0,)), ((), ())), preferred_element_type=jnp.float32)


def tables():
    head, group = lax.axis_index("head"), lax.axis_index("dp")
    ring, side, core = head // 4, head // 2 % 2, head % 2
    chunk = jnp.arange(16, dtype=jnp.int32)
    dz, dx, dc = (chunk // 4 - ring) % 4, (chunk // 2 + side) % 2, (chunk + core) % 2
    place = jnp.stack([ROWS_A * (2 * dz + dx), 8 * ROWS_A + ROWS_B * (4 * dx + dz), dc]).astype(jnp.int32)
    step = jnp.arange(8, dtype=jnp.int32)
    chip = ((step // 2 + ring) % 4) * 2 + (step + side) % 2
    heads = jnp.stack([2 * chip + core, 2 * chip + 1 - core]).astype(jnp.int32)
    up, over = group // 2, group % 2
    early = ((step // 2 + up) % 4) * 2 + (step + over) % 2
    late = ((step + up) % 4) * 2 + (step // 4 + over) % 2
    order = jnp.concatenate([2 * early, 2 * late + 1]).astype(jnp.int32)
    return place, heads, order


def body(
    tokens,
    cotangent,
    doc_spans,
    norm1_gain,
    q_weight,
    k_weight,
    v_weight,
    gate_out_weight,
    decay_weight,
    conv_weight,
    gate_params,
    out_gain,
    out_weight,
    norm2_gain,
    gate_weight,
    up_weight,
    down_weight,
):
    place, heads, order = tables()
    core = lax.axis_index("head") % 2
    starts = document_starts(doc_spans[0], 32)
    out_gain_row = out_gain[None, :]
    rows_shape = tokens.shape

    pad = lambda weight, columns: jnp.pad(weight, ((0, 0), (0, columns - weight.shape[1])))
    pack_one = jnp.concatenate(
        [q_weight, k_weight, v_weight, gate_out_weight, pad(decay_weight[:, 0], LANES), out_weight], axis=1
    )
    pack_two = jnp.concatenate([pad(gate_weight, HALF), pad(up_weight, HALF), pad(down_weight, HALF)], axis=1)
    taps = wide(lax.all_gather(conv_weight, "dp", axis=2, tiled=True))

    normed1, rows, cot, gains = whole_call(
        enter_kernel,
        [shaped(rows_shape, jnp.bfloat16)] * 3 + [shaped((2, rows_shape[1]))],
        "enter",
        (order,),
        tokens,
        cotangent,
        jnp.stack([norm1_gain, norm2_gain]),
    )
    mine_one = gather_dp(pack_one)
    weights_in = mine_one[:, : 5 * LANES]
    normed1_own = gather_zx(normed1)
    normed1_other = from_head(normed1_own, dc=1)
    raw0 = plain_product(normed1_own, weights_in)
    raw1 = plain_product(normed1_other, weights_in)

    weights_other = from_head(weights_in, dc=1)
    out_rings, out_columns = gather_parts(mine_one[:, 5 * LANES :], take_zx, 1280)
    out_first, out_second = jnp.concatenate(out_rings, axis=0), jnp.concatenate(out_columns, axis=0)
    out_parts = (out_first, from_head(out_first, dc=1), out_second, from_head(out_second, dc=1))
    mine_two = gather_dp(pack_two)
    other_two = from_head(mine_two, dc=1)
    cot_own = gather_zx(cot)

    mixed, stored, kept = mixer_forward(place, starts, gate_params, raw0, raw1, taps, out_gain_row)
    received = lax.all_to_all(mixed, "head", 0, 0, tiled=False)
    resid, normed2 = attend(heads, received, out_parts, rows, gains)
    normed2_own = gather_zx(normed2)
    fed, dnormed2, hidden, dpre = feed(normed2_own, cot_own, mine_two, other_two)

    dnormed2_pieces = reduce_zx(dnormed2)
    dresid, dattn, dgain2, dmixed = middle(heads, dnormed2_pieces, resid, cot, gains, out_parts)
    dmixed_mine = lax.all_to_all(dmixed, "head", 0, 0, tiled=False)

    (block_out,) = whole_call(
        leave_kernel, shaped(rows_shape, jnp.bfloat16), "leave", (order,), *reduce_zx(fed), resid
    )
    gate_up_grad = narrow(over_rows(normed2_own, dpre))
    down_grad = narrow(over_rows(cot_own, hidden))
    feed_own = jnp.concatenate([gate_up_grad[:, : 2 * HALF], down_grad[:, :HALF]], axis=1)
    feed_other = jnp.concatenate([gate_up_grad[:, 2 * HALF :], down_grad[:, HALF:]], axis=1)
    feed_grad = narrow(wide(feed_own) + wide(from_head(feed_other, dc=1)))
    feed_total = reduce_dp(feed_grad)

    dattn_own = gather_zx(dattn)
    mixed_pair = jnp.concatenate([stored[0], from_head(stored[1], dc=1)], axis=1)
    out_both = narrow(over_rows(dattn_own, mixed_pair))
    out_grad = narrow(wide(out_both[:, :LANES]) + wide(from_head(out_both[:, LANES:], dc=1)))

    draw, dtaps, dparams, dgain_out = mixer_backward(
        place, starts, gate_params, raw0, raw1, taps, out_gain_row, kept, dmixed_mine
    )
    draw_far = from_head(draw[1], dc=1)
    dnormed1 = against(draw[0], weights_in) + against(draw_far, weights_other)
    gain1_part = jnp.sum(dnormed1 * wide(normed1_own), axis=0) / gains[0]
    dnormed1_pieces = reduce_zx(narrow(dnormed1))

    in_grad = narrow(over_rows(normed1_own, draw[0]) + over_rows(normed1_other, draw[1]))
    one_total = reduce_dp(jnp.concatenate([in_grad, out_grad], axis=1))

    place_gain = lambda value: value.reshape(16, LANES)[inverse_order(order)]
    small = jnp.concatenate(
        [
            place_gain(gain1_part),
            place_gain(dgain2[0]),
            dgain_out,
            dparams,
            dtaps.reshape(12, LANES),
            jnp.zeros((4, LANES), jnp.float32),
        ],
        axis=0,
    )
    small = ring_sum(small, take_yx, lax.axis_index("dp") // 2)
    small = small + from_dp(small, dx=1)
    shared = small[:40]
    shared = ring_sum(shared, take_zx, lax.axis_index("head") // 4)
    shared = shared + from_head(shared, dx=1)
    shared = shared + from_head(shared, dc=1)
    gain1_total = shared[:16].reshape(-1)
    gain2_total = shared[16:32].reshape(-1)
    out_gain_total = jnp.sum(shared[32:40], axis=0)
    params_total = jnp.sum(small[40:48], axis=1)[:2, None]
    taps_total = lax.dynamic_slice_in_dim(
        small[48:60].reshape(3, 4, LANES), lax.axis_index("dp") * 16, 16, 2
    )

    (tokens_grad,) = whole_call(
        finish_kernel, shaped(rows_shape), "finish", (order,), *dnormed1_pieces, rows, dresid, gains
    )
    hidden_units = gate_weight.shape[1]
    return (
        block_out,
        tokens_grad,
        gain1_total,
        one_total[:, :LANES],
        one_total[:, LANES : 2 * LANES],
        one_total[:, 2 * LANES : 3 * LANES],
        one_total[:, 3 * LANES : 4 * LANES],
        one_total[:, 4 * LANES : 4 * LANES + 2][:, None, :],
        taps_total,
        params_total,
        out_gain_total,
        one_total[:, 5 * LANES :],
        gain2_total,
        feed_total[:, :hidden_units],
        feed_total[:, HALF : HALF + hidden_units],
        feed_total[:, 2 * HALF : 2 * HALF + hidden_units],
    )


def inverse_order(order):
    return jnp.argmax(order[None, :] == jnp.arange(16, dtype=jnp.int32)[:, None], axis=1)


def solution(mesh):
    rows, weight = P(("dp", "head"), None), P("dp", "head")
    weight3, taps = P("dp", "head", None), P(None, None, ("head", "dp"))
    params = P(None, "head")
    in_specs = (
        rows, rows, P("dp", None), P(), weight, weight, weight, weight, weight3, taps, params, P(),
        weight, P(), weight, weight, weight,
    )
    out_specs = (
        rows, rows, P(), weight, weight, weight, weight, weight3, taps, params, P(),
        weight, P(), weight, weight, weight,
    )
    return jax.shard_map(body, mesh=mesh, in_specs=in_specs, out_specs=out_specs, check_vma=False)
```

```python
from functools import partial

import jax
import jax.numpy as jnp
from jax import lax
from jax.experimental import pallas as pl
from jax.experimental.pallas import tpu as pltpu

CHUNK = 128
BATCH = 4
ROWS_A = 64
ROWS_B = 64
GATE_ALONE = 9
VMEM_MAX = 56 * 1024 * 1024


def spends(microseconds):
    return pl.CostEstimate(flops=int(microseconds * 1e6), bytes_accessed=1 << 10, transcendentals=0)


def split(value):
    high = value.astype(jnp.bfloat16)
    return high, (value - high.astype(jnp.float32)).astype(jnp.bfloat16)


def left_pair(value):
    return jnp.concatenate(split(value), axis=1)


def right_pair(value):
    high, low = split(value)
    wide = jnp.concatenate([high, low], axis=1)
    return jnp.concatenate([wide, wide], axis=0)


def right_pair_t(value):
    high, low = split(value)
    return jnp.concatenate(
        [jnp.concatenate([high, high], axis=1), jnp.concatenate([low, low], axis=1)], axis=0
    )


def fold(wide):
    half = wide.shape[1] // 2
    return wide[:, :half] + wide[:, half:]


def mul_pairs(left, right):
    return fold(jnp.dot(left, right, preferred_element_type=jnp.float32))


def mul(left, right):
    return mul_pairs(left_pair(left), right_pair(right))


def mul_t(left, right):
    return fold(
        lax.dot_general(
            left_pair(left),
            right_pair_t(right),
            (((1,), (1,)), ((), ())),
            preferred_element_type=jnp.float32,
        )
    )


def iotas(rows=CHUNK, cols=CHUNK):
    return (
        lax.broadcasted_iota(jnp.int32, (rows, cols), 0),
        lax.broadcasted_iota(jnp.int32, (rows, cols), 1),
    )


def silu_parts(value):
    gate = jax.nn.sigmoid(value)
    return gate, value * gate


def tap_masks(start_first, start_second, row_index):
    keeps = []
    for offset in range(1, 4):
        first = jnp.where(row_index < offset, 1.0 - start_first, 1.0)
        second = jnp.where(
            (row_index >= CHUNK // 2) & (row_index < CHUNK // 2 + offset), 1.0 - start_second, 1.0
        )
        keeps.append(first * second)
    return keeps


def shifted_rows(current, before, keeps):
    joined = jnp.concatenate([before, current], axis=0)
    return [current] + [
        pltpu.roll(joined, offset, 0)[8:] * keeps[offset - 1] for offset in range(1, 4)
    ]


def conv_rows(rows_by_offset, taps):
    total = rows_by_offset[0] * taps[3:4]
    for offset in range(1, 4):
        total = total + rows_by_offset[offset] * taps[3 - offset : 4 - offset]
    return total


def chunk_cols(rows):
    return jnp.transpose(jnp.concatenate([rows, jnp.zeros((CHUNK - 8, CHUNK), jnp.float32)], axis=0))


def decay_matrix(rows, cols, start_second):
    row_index, col_index = iotas()
    gap = cols[:, 0:1] - rows[0:1, :]
    lower = row_index >= col_index
    cross = (row_index >= CHUNK // 2) & (col_index < CHUNK // 2)
    decay = jnp.where(lower, jnp.exp(jnp.where(lower, gap, 0.0)), 0.0)
    return decay * jnp.where(cross, 1.0 - start_second, 1.0)


def head_rows(raw_refs, place_ref, chunk, part):
    def load(start, count):
        rows = pl.ds(pl.multiple_of(start, 8), count)
        return jnp.where(half == 0, raw_refs[0][rows, lanes], raw_refs[1][rows, lanes])

    lanes = slice(None) if part == GATE_ALONE else slice(part * CHUNK, (part + 1) * CHUNK)
    half = place_ref[2, chunk]
    current = jnp.concatenate(
        [load(place_ref[0, chunk], ROWS_A), load(place_ref[1, chunk], ROWS_B)], axis=0
    )
    if part > 2:
        return current
    earlier = jnp.maximum(chunk - 1, 0)
    half = place_ref[2, earlier]
    return current, load(place_ref[1, earlier] + ROWS_B - 8, 8)


def put_rows(out_ref, place_ref, chunk, lanes, value):
    half = place_ref[2, chunk]
    first = pl.ds(pl.multiple_of(place_ref[0, chunk], 16), ROWS_A)
    second = pl.ds(pl.multiple_of(place_ref[1, chunk], 16), ROWS_B)
    out_ref[half, first, lanes] = value[:ROWS_A]
    out_ref[half, second, lanes] = value[ROWS_A:]


def spread_sum(rows, matrix):
    high, rest = split(rows)
    mid = rest
    low = (rows - high.astype(jnp.float32) - mid.astype(jnp.float32)).astype(jnp.bfloat16)
    parts = jnp.concatenate([high, mid, low, jnp.zeros_like(low)], axis=0)
    wide = jnp.dot(parts, matrix.astype(jnp.bfloat16), preferred_element_type=jnp.float32)
    return wide[:8] + wide[8:16] + wide[16:24]


def gate_rows(decay_cols, starts, params_ref):
    row_index, col_index = iotas()
    pair = jnp.transpose(decay_cols)[:8]
    position = col_index[:8]
    kind = row_index[:8]
    carry, same = 1.0 - starts[0], 1.0 - starts[1]
    second = position >= CHUNK // 2
    beta = jax.nn.sigmoid(pair[1:2])
    inside = pair[0:1] + params_ref[1, 0]
    soft = jax.nn.softplus(inside)
    decay_log = -jnp.exp(params_ref[0, 0] + jnp.zeros((8, CHUNK), jnp.float32)) * soft
    total = spread_sum(decay_log, (row_index <= col_index).astype(jnp.float32))
    end = total[:, CHUNK - 1 :]
    gam = jnp.exp(total) * carry * jnp.where(second, same, 1.0)
    tail = jnp.exp(end - total) * jnp.where(second, 1.0, same)
    span = jnp.exp(end) * carry * same
    rows = jnp.where(kind == 0, total, jnp.where(kind == 1, beta, jnp.where(kind == 2, gam, tail)))
    return jnp.where(kind == 4, span, rows)


def convolved(raw_refs, place_ref, starts, taps_ref, chunk, row_index):
    keeps = tap_masks(starts[0], starts[1], row_index)
    pieces = []
    for part in range(3):
        current, before = head_rows(raw_refs, place_ref, chunk, part)
        rows_by_offset = shifted_rows(current, before, keeps)
        pieces.append((rows_by_offset, conv_rows(rows_by_offset, taps_ref[part])))
    return keeps, pieces


def start_flags(starts_ref, chunk):
    return (
        starts_ref[2 * chunk].astype(jnp.float32),
        starts_ref[2 * chunk + 1].astype(jnp.float32),
    )


def normed_qkv(pieces):
    acts = [piece[1] * jax.nn.sigmoid(piece[1]) for piece in pieces]
    q_scale = lax.rsqrt(jnp.sum(acts[0] * acts[0], axis=-1, keepdims=True) + 1e-06)
    k_scale = lax.rsqrt(jnp.sum(acts[1] * acts[1], axis=-1, keepdims=True) + 1e-06)
    return acts[0] * q_scale * CHUNK ** (-0.5), acts[1] * k_scale, acts[2], q_scale, k_scale


def inverse_lower(stricts):
    row_index, col_index = iotas()
    eye = (row_index == col_index).astype(jnp.float32)
    near = row_index // 16 == col_index // 16
    powers = [jnp.where(near, strict, 0.0) for strict in stricts]
    inverses = [eye - power for power in powers]
    powers = [mul(power, power) for power in powers]
    for step in range(3):
        rights = [right_pair(power) for power in powers]
        if step < 2:
            stacks = [
                left_pair(jnp.concatenate([inverse, power], axis=0))
                for inverse, power in zip(inverses, powers)
            ]
            both = [mul_pairs(stack, right) for stack, right in zip(stacks, rights)]
            inverses = [inverse + pair[:CHUNK] for inverse, pair in zip(inverses, both)]
            powers = [pair[CHUNK:] for pair in both]
        else:
            inverses = [
                inverse + mul_pairs(left_pair(inverse), right)
                for inverse, right in zip(inverses, rights)
            ]
    for width in (16, 32, 64):
        beside = (row_index // (2 * width) == col_index // (2 * width)) & (
            row_index // width != col_index // width
        )
        crossed = [
            mul(inverse, jnp.where(beside, strict, 0.0))
            for inverse, strict in zip(inverses, stricts)
        ]
        inverses = [inverse - mul(cross, inverse) for cross, inverse in zip(crossed, inverses)]
    return inverses


def prepare_kernel(place_ref, starts_ref, params_ref, raw0_ref, raw1_ref, taps_ref,
                   rows_out_ref, inv_ref, kkf_ref, p_ref, uw_ref, m_ref, mt_ref, b_ref, r_ref, pu_ref):
    row_index, col_index = iotas()
    diagonal = (row_index == col_index).astype(jnp.float32)
    stricts, kept = [], []
    for member in range(BATCH):
        chunk = pl.program_id(0) * BATCH + member
        starts = start_flags(starts_ref, chunk)
        raw_refs = (raw0_ref, raw1_ref)
        _, pieces = convolved(raw_refs, place_ref, starts, taps_ref, chunk, row_index)
        queries, keys_in, values_in, _, _ = normed_qkv(pieces)
        rows = gate_rows(head_rows(raw_refs, place_ref, chunk, 4), starts, params_ref)
        rows_out_ref[member] = rows
        cols = chunk_cols(rows)
        decay = decay_matrix(rows, cols, starts[1])
        beta, gam, tail = cols[:, 1:2], cols[:, 2:3], cols[:, 3:4]
        scores = mul_t(jnp.concatenate([keys_in, queries], axis=0), keys_in)
        kkf = jnp.where(row_index > col_index, scores[:CHUNK] * decay, 0.0)
        inner = scores[CHUNK:] * decay
        stricts.append(kkf * beta)
        kkf_ref[member] = kkf
        p_ref[member] = inner
        pair = jnp.concatenate([values_in * beta, keys_in * (beta * gam)], axis=1)
        stack = jnp.concatenate([jnp.transpose(keys_in * tail), inner], axis=0)
        kept.append((pair, stack, diagonal * rows[4:5], queries * gam))
    inverses = inverse_lower(stricts)
    joined = [mul(inverse, pair) for inverse, (pair, _, _, _) in zip(inverses, kept)]
    both = [mul(stack, join) for join, (_, stack, _, _) in zip(joined, kept)]
    for member in range(BATCH):
        _, _, span, faded = kept[member]
        inv_ref[member] = inverses[member]
        uw_ref[member] = joined[member]
        state_map = span - both[member][:CHUNK, CHUNK:]
        m_ref[member] = left_pair(state_map)
        mt_ref[member] = left_pair(jnp.transpose(state_map))
        b_ref[member] = both[member][:CHUNK, :CHUNK]
        r_ref[member] = faded - both[member][CHUNK:, CHUNK:]
        pu_ref[member] = both[member][CHUNK:, :CHUNK]


def whole(shape):
    return pl.BlockSpec(shape, lambda *_: (0,) * len(shape))


def per_batch(shape, turned=False, steps=4):
    def place(step, *_):
        return ((steps - 1 - step) if turned else step,) + (0,) * (len(shape) - 1)

    return pl.BlockSpec(shape, place)


def shaped(shape, dtype=jnp.float32):
    return jax.ShapeDtypeStruct(shape, dtype)


def prepare(place, starts, params, raw0, raw1, taps):
    chunks = place.shape[1]
    square = (BATCH, CHUNK, CHUNK)
    wide = (BATCH, CHUNK, 2 * CHUNK)
    kinds = [((BATCH, 8, CHUNK), jnp.float32), (square, jnp.float32), (square, jnp.float32), (square, jnp.float32),
             (wide, jnp.float32), (wide, jnp.bfloat16), (wide, jnp.bfloat16), (square, jnp.float32),
             (square, jnp.float32), (square, jnp.float32)]
    return pl.pallas_call(
        prepare_kernel,
        grid_spec=pltpu.PrefetchScalarGridSpec(
            num_scalar_prefetch=3,
            grid=(chunks // BATCH,),
            in_specs=[whole(raw0.shape), whole(raw1.shape), whole(taps.shape)],
            out_specs=[per_batch(shape) for shape, _ in kinds],
        ),
        out_shape=[shaped((chunks,) + shape[1:], dtype) for shape, dtype in kinds],
        compiler_params=pltpu.CompilerParams(vmem_limit_bytes=VMEM_MAX),
        cost_estimate=spends(18),
        name="prepare",
    )(place, starts, params, raw0, raw1, taps)


def gate_rows_of(gate_refs, place_ref, chunk):
    return head_rows(gate_refs, place_ref, chunk, GATE_ALONE)


def scan_kernel(place_ref, m_ref, b_ref, r_ref, pu_ref, gate0_ref, gate1_ref, gain_ref,
                state_out_ref, core_ref, mixed_ref, state_ref):
    @pl.when(pl.program_id(0) == 0)
    def _():
        state_ref[...] = jnp.zeros_like(state_ref)

    state = state_ref[...]
    for member in range(BATCH):
        chunk = pl.program_id(0) * BATCH + member
        state_out_ref[member] = state
        pair = right_pair(state)
        core = mul_pairs(left_pair(r_ref[member]), pair) + pu_ref[member]
        state = mul_pairs(m_ref[member], pair) + b_ref[member]
        _, gate = silu_parts(gate_rows_of((gate0_ref, gate1_ref), place_ref, chunk))
        core_ref[member] = core
        scale = lax.rsqrt(jnp.mean(core * core, axis=-1, keepdims=True) + 1e-05)
        mixed = (core * scale * gain_ref[...] * gate).astype(jnp.bfloat16)
        mixed_ref[member] = mixed
    state_ref[...] = state


def gate_columns(raw):
    return pl.BlockSpec((raw.shape[0], CHUNK), lambda *_: (0, 3))


def scan_states(place, m, b, r, pu, raw0, raw1, gain):
    chunks = m.shape[0]
    square = (BATCH, CHUNK, CHUNK)
    wide = (BATCH, CHUNK, 2 * CHUNK)
    return pl.pallas_call(
        scan_kernel,
        grid_spec=pltpu.PrefetchScalarGridSpec(
            num_scalar_prefetch=1,
            grid=(chunks // BATCH,),
            in_specs=[per_batch(wide), per_batch(square), per_batch(square), per_batch(square),
                      gate_columns(raw0), gate_columns(raw1), whole((1, CHUNK))],
            out_specs=[per_batch(square)] * 3,
            scratch_shapes=[pltpu.VMEM((CHUNK, CHUNK), jnp.float32)],
        ),
        out_shape=[shaped((chunks, CHUNK, CHUNK)), shaped((chunks, CHUNK, CHUNK)),
                   shaped((chunks, CHUNK, CHUNK), jnp.bfloat16)],
        compiler_params=pltpu.CompilerParams(vmem_limit_bytes=VMEM_MAX),
        cost_estimate=spends(7),
        name="scan_states",
    )(place, m, b, r, pu, raw0, raw1, gain)


def back_scan_kernel(place_ref, mt_ref, r_ref, core_ref, gate0_ref, gate1_ref, dmixed_ref, gain_ref,
                     dcore_ref, dstate_out_ref, dgate_ref, dgain_ref, dstate_ref):
    step = pl.program_id(0)

    @pl.when(step == 0)
    def _():
        dstate_ref[...] = jnp.zeros_like(dstate_ref)
        dgain_ref[...] = jnp.zeros_like(dgain_ref)

    gain = gain_ref[...]
    dgain = jnp.zeros((8, CHUNK), jnp.float32)
    terms = []
    for member in reversed(range(BATCH)):
        chunk = (pl.num_programs(0) - 1 - step) * BATCH + member
        core = core_ref[member]
        raw_gate = gate_rows_of((gate0_ref, gate1_ref), place_ref, chunk)
        dmixed = dmixed_ref[member].astype(jnp.float32)
        gate, gated = silu_parts(raw_gate)
        scale = lax.rsqrt(jnp.mean(core * core, axis=-1, keepdims=True) + 1e-05)
        unit = core * scale
        dscaled = dmixed * gated
        dgate = dmixed * unit * gain * (gate * (1.0 + raw_gate * (1.0 - gate)))
        dgate_ref[member] = dgate.astype(jnp.bfloat16)
        product = dscaled * unit
        dgain = dgain + jnp.sum(product.reshape(CHUNK // 8, 8, CHUNK), axis=0)
        dunit = dscaled * gain
        dcore = scale * (dunit - unit * jnp.mean(dunit * unit, axis=-1, keepdims=True))
        dcore_ref[member] = dcore
        terms.append((member, mul(jnp.transpose(r_ref[member]), dcore)))
    dgain_ref[...] += dgain
    dstate = dstate_ref[...]
    for member, term in terms:
        dstate_out_ref[member] = dstate
        dstate = mul_pairs(mt_ref[member], right_pair(dstate)) + term
    dstate_ref[...] = dstate


def back_scan(place, mt, r, core, raw0, raw1, dmixed, gain):
    chunks = mt.shape[0]
    square = (BATCH, CHUNK, CHUNK)
    wide = (BATCH, CHUNK, 2 * CHUNK)
    turned = partial(per_batch, turned=True, steps=chunks // BATCH)
    return pl.pallas_call(
        back_scan_kernel,
        grid_spec=pltpu.PrefetchScalarGridSpec(
            num_scalar_prefetch=1,
            grid=(chunks // BATCH,),
            in_specs=[turned(wide), turned(square), turned(square),
                      gate_columns(raw0), gate_columns(raw1), turned(square), whole((1, CHUNK))],
            out_specs=[turned(square), turned(square), turned(square), whole((8, CHUNK))],
            scratch_shapes=[pltpu.VMEM((CHUNK, CHUNK), jnp.float32)],
        ),
        out_shape=[shaped((chunks, CHUNK, CHUNK)), shaped((chunks, CHUNK, CHUNK)),
                   shaped((chunks, CHUNK, CHUNK), jnp.bfloat16), shaped((8, CHUNK))],
        compiler_params=pltpu.CompilerParams(vmem_limit_bytes=VMEM_MAX),
        cost_estimate=spends(7),
        name="back_scan",
    )(place, mt, r, core, raw0, raw1, dmixed, gain)


def lane_sum(value):
    return jnp.sum(value, axis=1, keepdims=True)


def back_kernel(place_ref, starts_ref, params_ref, raw0_ref, raw1_ref, rows_ref, taps_ref, inv_ref, kkf_ref,
                p_ref, uw_ref, state_ref, dstate_ref, dcore_ref, dgate_ref,
                draw0_ref, draw1_ref, dtaps_ref, dparams_ref, next_ref, draw_ref):
    step = pl.program_id(0)
    row_index, col_index = iotas()
    lower = row_index >= col_index
    strict = row_index > col_index

    @pl.when(step == 0)
    def _():
        next_ref[...] = jnp.zeros_like(next_ref)
        dtaps_ref[...] = jnp.zeros_like(dtaps_ref)
        dparams_ref[...] = jnp.zeros_like(dparams_ref)

    raw_refs = (raw0_ref, raw1_ref)
    members = range(BATCH)
    setups = []
    for member in members:
        chunk = (pl.num_programs(0) - 1 - step) * BATCH + member
        starts = start_flags(starts_ref, chunk)
        keeps, pieces = convolved(raw_refs, place_ref, starts, taps_ref, chunk, row_index)
        queries, keys_in, values_in, q_scale, k_scale = normed_qkv(pieces)
        rows = rows_ref[member]
        cols = chunk_cols(rows)
        decay = decay_matrix(rows, cols, starts[1])
        setups.append((starts, keeps, pieces, queries, keys_in, values_in, q_scale, k_scale, rows, cols, decay))
    fresh = [
        uw_ref[i][:, :CHUNK] - mul(uw_ref[i][:, CHUNK:], state_ref[i]) for i in members
    ]
    dfresh = [
        mul(jnp.transpose(p_ref[i]), dcore_ref[i])
        + mul(setups[i][4] * setups[i][9][:, 3:4], dstate_ref[i])
        for i in members
    ]
    through = [
        mul_t(jnp.concatenate([dcore_ref[i], dfresh[i]], axis=0), state_ref[i]) for i in members
    ]
    dinner = [jnp.where(lower, mul_t(dcore_ref[i], fresh[i]), 0.0) for i in members]
    dkeys_tail = [mul_t(fresh[i], dstate_ref[i]) for i in members]
    dboth = [
        mul(
            jnp.transpose(inv_ref[i]),
            jnp.concatenate([dfresh[i], -through[i][CHUNK:]], axis=1),
        )
        for i in members
    ]
    dstrict = [jnp.where(strict, -mul_t(dboth[i], uw_ref[i]), 0.0) for i in members]
    stacked, crossed = [], []
    for i in members:
        queries, keys_in, cols, decay = setups[i][3], setups[i][4], setups[i][9], setups[i][10]
        dscores_n = dstrict[i] * decay * cols[:, 1:2]
        dscores = dinner[i] * decay
        stacked.append(
            mul(jnp.concatenate([dscores, dscores_n + jnp.transpose(dscores_n)], axis=0), keys_in)
        )
        crossed.append(mul(jnp.transpose(dscores), queries))
    for i in reversed(members):
        starts, keeps, pieces, queries, keys_in, values_in, q_scale, k_scale, rows, cols, _ = setups[i]
        beta, gam, tail = cols[:, 1:2], cols[:, 2:3], cols[:, 3:4]
        dqueries_faded = through[i][:CHUNK]
        dvalues_beta, dkeys_beta = dboth[i][:, :CHUNK], dboth[i][:, CHUNK:]
        keys_gam = keys_in * gam
        dqueries = stacked[i][:CHUNK] + dqueries_faded * gam
        dkeys = (
            stacked[i][CHUNK:]
            + crossed[i]
            + dkeys_beta * (beta * gam)
            + dkeys_tail[i] * tail
        )
        dvalues = dvalues_beta * beta

        dkkf = dstrict[i] * kkf_ref[i]
        flow = dkkf * beta + dinner[i] * p_ref[i]
        tail_term = lane_sum(dkeys_tail[i] * keys_in * tail)
        dbeta = lane_sum(dkkf + dvalues_beta * values_in + dkeys_beta * keys_gam)
        dsum = (
            lane_sum(flow + (dqueries_faded * queries + dkeys_beta * keys_in * beta) * gam)
            - tail_term
        )
        last = jnp.sum(tail_term) + jnp.sum(state_ref[i] * dstate_ref[i] * rows[4:5, 0:1])
        last_col = jnp.where(row_index[:, :1] == CHUNK - 1, last, 0.0)
        packed = jnp.where(
            col_index == 0, dsum + last_col, jnp.where(col_index == 1, dbeta, 0.0)
        )
        turned = jnp.transpose(packed)[:8]
        flow_rows = jnp.sum(flow, axis=0, keepdims=True)
        kind = row_index[:8]
        dtotal = jnp.where(kind == 0, turned - flow_rows, 0.0)
        dlog = spread_sum(dtotal, lower.astype(jnp.float32))[0:1]
        chunk = (pl.num_programs(0) - 1 - step) * BATCH + i
        pair = jnp.transpose(head_rows(raw_refs, place_ref, chunk, 4))[:8]
        inside = pair[0:1] + params_ref[1, 0]
        rate = -jnp.exp(params_ref[0, 0] + jnp.zeros((1, CHUNK), jnp.float32))
        dinside = dlog * rate * jax.nn.sigmoid(inside)
        beta_row = rows[1:2]
        dbeta_raw = turned[1:2] * beta_row * (1.0 - beta_row)
        drate = dlog * rate * jax.nn.softplus(inside)
        dparams_ref[...] += jnp.where(kind == 0, drate, jnp.where(kind == 1, dinside, 0.0))
        ddecay = jnp.where(kind == 0, dinside, jnp.where(kind == 1, dbeta_raw, 0.0))
        put_rows(draw_ref, place_ref, chunk, slice(3 * CHUNK, 4 * CHUNK), dgate_ref[i])
        put_rows(
            draw_ref, place_ref, chunk, slice(4 * CHUNK, 5 * CHUNK), chunk_cols(ddecay).astype(jnp.bfloat16)
        )

        d_scaled_q = dqueries * CHUNK ** (-0.5)
        gates = [jax.nn.sigmoid(piece[1]) for piece in pieces]
        unit_q, unit_k = pieces[0][1] * gates[0] * q_scale, pieces[1][1] * gates[1] * k_scale
        dact = [
            q_scale * (d_scaled_q - unit_q * lane_sum(d_scaled_q * unit_q)),
            k_scale * (dkeys - unit_k * lane_sum(dkeys * unit_k)),
            dvalues,
        ]
        for part in range(3):
            rows_by_offset, conv = pieces[part]
            gate = gates[part]
            dconv = dact[part] * (gate * (1.0 + conv * (1.0 - gate)))
            taps = taps_ref[part]
            after = next_ref[part]
            draw = dconv * taps[3:4]
            for offset in range(1, 4):
                kept = jnp.concatenate([dconv * keeps[offset - 1], after], axis=0)
                draw = draw + pltpu.roll(kept, CHUNK + 8 - offset, 0)[:CHUNK] * taps[3 - offset : 4 - offset]
            lanes = slice(part * CHUNK, (part + 1) * CHUNK)
            put_rows(draw_ref, place_ref, chunk, lanes, draw.astype(jnp.bfloat16))
            for offset in range(4):
                dtaps_ref[part, 3 - offset : 4 - offset] += jnp.sum(
                    dconv * rows_by_offset[offset], axis=0, keepdims=True
                )
            next_ref[part] = dconv[:8] * (1.0 - starts[0])

    @pl.when(step == pl.num_programs(0) - 1)
    def _():
        draw0_ref[...] = draw_ref[0]
        draw1_ref[...] = draw_ref[1]


def back(place, starts, params, raw0, raw1, rows, taps, inverse, kkf, inner, joined, states, dstates, dcore, dgate):
    chunks = rows.shape[0]
    square = (BATCH, CHUNK, CHUNK)
    wide = (BATCH, CHUNK, 2 * CHUNK)
    turned = partial(per_batch, turned=True, steps=chunks // BATCH)
    draw = (2,) + raw0.shape
    return pl.pallas_call(
        back_kernel,
        grid_spec=pltpu.PrefetchScalarGridSpec(
            num_scalar_prefetch=3,
            grid=(chunks // BATCH,),
            in_specs=[whole(raw0.shape), whole(raw1.shape), turned((BATCH, 8, CHUNK)), whole(taps.shape),
                      turned(square), turned(square), turned(square), turned(wide), turned(square),
                      turned(square), turned(square), turned(square)],
            out_specs=[whole(raw0.shape), whole(raw0.shape), whole((3, 4, CHUNK)), whole((8, CHUNK))],
            scratch_shapes=[pltpu.VMEM((3, 8, CHUNK), jnp.float32), pltpu.VMEM(draw, jnp.bfloat16)],
        ),
        out_shape=[shaped(raw0.shape, jnp.bfloat16)] * 2 + [shaped((3, 4, CHUNK)), shaped((8, CHUNK))],
        compiler_params=pltpu.CompilerParams(vmem_limit_bytes=VMEM_MAX),
        cost_estimate=spends(24),
        name="back",
    )(place, starts, params, raw0, raw1, rows, taps, inverse, kkf, inner, joined, states, dstates, dcore, dgate)


def document_starts(doc_lengths, block_count):
    bounds = jnp.cumsum(doc_lengths)[:-1]
    blocks = jnp.arange(block_count, dtype=jnp.int32)
    opens = jnp.any(blocks[:, None] == bounds[None, :], axis=1) | (blocks == 0)
    return opens.astype(jnp.int32)


def mixer_forward(place, prepared, raw0, raw1, out_gain):
    rows, inverse, kkf, inner, joined, m, mt, b, r, pu = prepared
    states, core, mixed = scan_states(place, m, b, r, pu, raw0, raw1, out_gain)
    return mixed, (rows, inverse, kkf, inner, joined, mt, r, states, core)


def mixer_backward_scan(place, raw0, raw1, out_gain, kept, dmixed):
    mt, r, core = kept[5], kept[6], kept[8]
    return back_scan(place, mt, r, core, raw0, raw1, dmixed, out_gain)


def mixer_backward(place, starts, params, raw0, raw1, taps, kept, dstates, dcore, dgate):
    rows, inverse, kkf, inner, joined, _, _, states, _ = kept
    return back(
        place, starts, params, raw0, raw1, rows, taps, inverse, kkf, inner, joined, states, dstates, dcore, dgate
    )


from jax.sharding import PartitionSpec as P

LANES = 128
HALF = 384
GROUP = 256


def exchange_perm(count, shifted, sizes):
    pairs = []
    for target in range(count):
        source, scale, rest = 0, 1, target
        for size, offset in zip(reversed(sizes), reversed(shifted)):
            source += (rest % size + offset) % size * scale
            rest //= size
            scale *= size
        pairs.append((source, target))
    return pairs


def from_head(value, dz=0, dx=0, dc=0):
    return lax.ppermute(value, "head", exchange_perm(16, (dz, dx, dc), (4, 2, 2)))


def from_dp(value, dy=0, dx=0):
    return lax.ppermute(value, "dp", exchange_perm(8, (dy, dx), (4, 2)))


def after(value, *earlier):
    return lax.optimization_barrier((value,) + earlier)[0]


def gather_turn(value, cut, beside=()):
    first, second = value[:cut], value[cut:]
    arrived = [take_zx(first, 0, 1)] + [take_zx(second, k, 0) for k in (1, 2, 3)]
    arrived = lax.optimization_barrier(tuple(arrived) + tuple(beside))
    pair = jnp.concatenate([first, arrived[0]], axis=0)
    column = jnp.concatenate([second, *arrived[1:4]], axis=0)
    return lax.optimization_barrier((pair, column))


def gather_end(pair, column):
    return [pair] + [take_zx(pair, k, 0) for k in (1, 2, 3)], [column, take_zx(column, 0, 1)]


def take_zx(value, ring, side):
    return from_head(value, dz=ring, dx=side)


def take_yx(value, ring, side):
    return from_dp(value, dy=ring, dx=side)


def wide(value):
    return value.astype(jnp.float32)


def narrow(value):
    return value.astype(jnp.bfloat16)


def sum_rows(pieces, rows):
    total = wide(pieces[0][rows])
    for piece in pieces[1:]:
        total = total + wide(piece[rows])
    return total


def reduce_arrivals(rounds, far, beside=()):
    arrived = [take_zx(rounds[k - 1], -k, 0) for k in (1, 2, 3)] + [take_zx(far, 0, 1)]
    return lax.optimization_barrier(tuple(arrived) + tuple(beside))[:4]


def turn_sum_kernel(*refs):
    rounds, sides, outs = refs[:4], refs[4:6], refs[6:]
    cut = rounds[0].shape[0] // 2
    early, late = slice(0, cut), slice(cut, None)
    total = wide(rounds[0][...])
    for ref in rounds[1:]:
        total = total + wide(ref[...])
    outs[0][...] = total[early]
    outs[1][...] = narrow(total[late])
    total = wide(sides[0][...]) + wide(sides[1][...])
    rest = total.shape[0] // 4
    outs[2][...] = total[:rest]
    for k in (1, 2, 3):
        outs[2 + k][...] = narrow(total[rest * k : rest * (k + 1)])


def reduce_parts(first, near, arrived):
    width = first.shape[1]
    cut, rest = (first.shape[0] // 2, width), (near.shape[0] // 4, width)
    outs = [shaped(cut), shaped(cut, jnp.bfloat16), shaped(rest)] + [shaped(rest, jnp.bfloat16)] * 3
    return whole_call(turn_sum_kernel, outs, "turn_sum", (), first, *arrived[:3], near, arrived[3])


def side_sum_kernel(near_ref, crossed_ref, *out_refs):
    for k, out_ref in enumerate(out_refs):
        for half in range(2):
            rows = slice(ROWS_A * (4 * half + k), ROWS_A * (4 * half + k + 1))
            total = wide(near_ref[rows]) + wide(crossed_ref[rows])
            out_ref[ROWS_A * half : ROWS_A * (half + 1)] = total if k == 0 else narrow(total)


def ring_sum_kernel(over_ref, *refs):
    arrived, (kept_ref, sent_ref) = refs[:4], refs[4:]
    half = kept_ref.shape[0]
    for target, side in ((kept_ref, over_ref[0]), (sent_ref, 1 - over_ref[0])):
        rows = pl.ds(pl.multiple_of(side * half, 16), half)
        total = wide(arrived[0][rows])
        for ref in arrived[1:]:
            total = total + wide(ref[rows])
        target[...] = total.astype(target.dtype)


def reduce_end(parts):
    return (parts[0], take_zx(parts[1], 0, 1), parts[2]) + tuple(
        take_zx(parts[2 + k], -k, 0) for k in (1, 2, 3)
    )


RINGS = [[0, 2, 4, 6], [1, 3, 5, 7]]


def spread_kernel(over_ref, *refs):
    over, out_ref = over_ref[0], refs[-1]
    count = (len(refs) - 1) // 2
    for place in range(count):
        lanes = slice(place * HALF, (place + 1) * HALF)
        out_ref[0, over, :, lanes] = refs[place][...]
        out_ref[0, 1 - over, :, lanes] = refs[count + place][...]


def spread_pair(value, mate):
    rows, columns = value.shape
    count = columns // HALF
    blocks = [held((rows, HALF), lambda *_, place=place: (0, place)) for place in range(count)]
    return pl.pallas_call(
        spread_kernel,
        grid_spec=pltpu.PrefetchScalarGridSpec(
            num_scalar_prefetch=1,
            grid=(4,),
            in_specs=blocks * 2,
            out_specs=pl.BlockSpec((1, 2, rows, columns), lambda turn, *_: (turn, 0, 0, 0)),
        ),
        out_shape=shaped((4, 2, rows, columns), value.dtype),
        compiler_params=pltpu.CompilerParams(vmem_limit_bytes=VMEM_MAX),
        cost_estimate=spends(3),
        name="spread_pair",
    )((lax.axis_index("dp") % 2)[None].astype(jnp.int32), *[value] * count, *[mate] * count)


def round_ring(spread):
    everything = lax.all_to_all(spread, "dp", 0, 0, tiled=False, axis_index_groups=RINGS)
    return everything.reshape(8 * spread.shape[2], spread.shape[3])


def ring_blocks(value):
    up = lax.axis_index("dp") // 2
    rows = value.shape[0] // 4
    blocks = [lax.dynamic_slice_in_dim(value, (up + k) % 4 * rows, rows, 0) for k in range(4)]
    return lax.optimization_barrier(tuple(blocks))


def ring_arrivals(blocks):
    return [blocks[0]] + [take_yx(blocks[k], -k, 0) for k in (1, 2, 3)]


def ring_parts(arrived):
    over = (lax.axis_index("dp") % 2)[None].astype(jnp.int32)
    half = (arrived[0].shape[0] // 2, arrived[0].shape[1])
    return whole_call(ring_sum_kernel, [shaped(half), shaped(half, jnp.bfloat16)], "ring_sum", (over,), *arrived)


def exchange_ring(value):
    return lax.all_to_all(value, "dp", 0, 0, tiled=False, axis_index_groups=RINGS)


def sum_all(value, axis, count):
    spread = jnp.broadcast_to(value, (count,) + value.shape)
    return jnp.sum(lax.all_to_all(spread, axis, 0, 0, tiled=False), axis=0)


def whole_call(kernel, out_shape, name, scalars, *arrays, scratch=()):
    outs = out_shape if isinstance(out_shape, (list, tuple)) else [out_shape]
    return pl.pallas_call(
        kernel,
        grid_spec=pltpu.PrefetchScalarGridSpec(
            num_scalar_prefetch=len(scalars),
            grid=(1,),
            in_specs=[whole(array.shape) for array in arrays],
            out_specs=[whole(out.shape) for out in outs],
            scratch_shapes=list(scratch),
        ),
        out_shape=list(outs),
        compiler_params=pltpu.CompilerParams(vmem_limit_bytes=VMEM_MAX),
        cost_estimate=spends(3),
        name=name,
    )(*scalars, *arrays)


def rms_parts(values):
    scale = lax.rsqrt(jnp.mean(values * values, axis=-1, keepdims=True) + 1e-05)
    return scale, values * scale


def rms_back(grad, gain, scale, unit):
    inner = grad * gain
    return scale * (inner - unit * jnp.mean(inner * unit, axis=-1, keepdims=True))


def enter_kernel(tokens_ref, gain_ref, normed_ref):
    _, unit = rms_parts(wide(tokens_ref[...]))
    normed_ref[...] = narrow(unit * gain_ref[...])


def project_kernel(own_ref, other_ref, weights_ref, own_out_ref, other_out_ref):
    step = pl.program_id(0)
    half = pl.num_programs(0) // 2

    @pl.when(step < half)
    def _():
        own_out_ref[...] = plain_product(own_ref[...], weights_ref[...])

    @pl.when(step >= half)
    def _():
        other_out_ref[...] = plain_product(other_ref[...], weights_ref[...])


def project(own, other, weights, columns):
    count, width = own.shape
    step = 512
    half = count // step

    def early(size):
        return pl.BlockSpec((step, size), lambda i: (jnp.minimum(i, half - 1), 0))

    def late(size):
        return pl.BlockSpec((step, size), lambda i: (jnp.maximum(i - half, 0), 0))

    return pl.pallas_call(
        project_kernel,
        grid=(2 * half,),
        in_specs=[early(width), late(width), held((width, columns))],
        out_specs=[early(columns), late(columns)],
        out_shape=[shaped((count, columns))] * 2,
        compiler_params=pltpu.CompilerParams(vmem_limit_bytes=VMEM_MAX),
        cost_estimate=spends(5),
        name="project",
    )(own, other, weights)


def unproject_kernel(own_ref, far_ref, weights_ref, far_weights_ref, *piece_refs):
    step = pl.program_id(0)
    total = against(own_rows(own_ref, step), weights_ref[...]) + against(
        own_rows(far_ref, step), far_weights_ref[...]
    )
    put_pieces(narrow(total), piece_refs, step)


def unproject(own, far, weights, far_weights, piece_shapes):
    used = held((weights.shape[0], own.shape[1]))
    return pl.pallas_call(
        unproject_kernel,
        grid=(4,),
        in_specs=[held(own.shape), held(far.shape), used, used],
        out_specs=[whole(shape) for shape in piece_shapes],
        out_shape=[shaped(shape, jnp.bfloat16) for shape in piece_shapes],
        compiler_params=pltpu.CompilerParams(vmem_limit_bytes=VMEM_MAX),
        cost_estimate=spends(8),
        name="unproject",
    )(own, far, weights, far_weights)


def feed_grad_kernel(*refs):
    own_ref, far_ref = refs[8:]
    gate_up, down = 0.0, 0.0
    for normed_ref, cot_ref, dpre_ref, hidden_ref in (refs[:4], refs[4:8]):
        gate_up = gate_up + over_rows(normed_ref[...], dpre_ref[...])
        down = down + over_rows(cot_ref[...], hidden_ref[...])
    gate_up, down = narrow(gate_up), narrow(down)
    own_ref[:, : 2 * HALF] = gate_up[:, : 2 * HALF]
    far_ref[:, : 2 * HALF] = gate_up[:, 2 * HALF :]
    own_ref[:, 2 * HALF :] = down[:, :HALF]
    far_ref[:, 2 * HALF :] = down[:, HALF:]


def feed_grads(*parts):
    arrays, specs = [], []
    width = parts[0][2].shape[1]
    for hidden, dpre, normed, cot in parts:
        rows = pl.BlockSpec((normed.shape[0], GROUP), lambda i: (0, i))
        arrays += [normed, cot, dpre, hidden]
        specs += [rows, rows, held(dpre.shape), held(hidden.shape)]
    out = pl.BlockSpec((GROUP, 3 * HALF), lambda i: (i, 0))
    return pl.pallas_call(
        feed_grad_kernel,
        grid=(width // GROUP,),
        in_specs=specs,
        out_specs=[out, out],
        out_shape=[shaped((width, 3 * HALF), jnp.bfloat16)] * 2,
        compiler_params=pltpu.CompilerParams(vmem_limit_bytes=VMEM_MAX),
        cost_estimate=spends(12),
        name="feed_grads",
    )(*arrays)


def in_grad_kernel(own_ref, other_ref, draw0_ref, draw1_ref, weights_ref, gain_ref, out_ref, part_ref):
    grad = narrow(over_rows(own_ref[...], draw0_ref[...]) + over_rows(other_ref[...], draw1_ref[...]))
    out_ref[0] = grad
    product = wide(grad) * wide(weights_ref[...])
    lanes = product[:, :LANES]
    for start in range(LANES, product.shape[1], LANES):
        lanes = lanes + product[:, start : start + LANES]
    part = jnp.sum(jnp.transpose(lanes), axis=0, keepdims=True) / gain_ref[...]
    part_ref[0] = jnp.broadcast_to(part, part_ref.shape[1:])


def in_grads(own, other, draw0, draw1, weights, gain):
    count, width = own.shape
    used = draw0.shape[1]
    rows = pl.BlockSpec((count, GROUP), lambda i: (0, i))
    grad, part = pl.pallas_call(
        in_grad_kernel,
        grid=(width // GROUP,),
        in_specs=[rows, rows, held(draw0.shape), held(draw1.shape),
                  pl.BlockSpec((GROUP, used), lambda i: (i, 0)), pl.BlockSpec((1, GROUP), lambda i: (0, i))],
        out_specs=[pl.BlockSpec((1, GROUP, used), lambda i: (i // 2, i % 2, 0)),
                   pl.BlockSpec((1, 8, GROUP), lambda i: (i, 0, 0))],
        out_shape=[shaped((4, 2 * GROUP, used), jnp.bfloat16), shaped((width // GROUP, 8, GROUP))],
        compiler_params=pltpu.CompilerParams(vmem_limit_bytes=VMEM_MAX),
        cost_estimate=spends(8),
        name="in_grads",
    )(own, other, draw0, draw1, weights, gain)
    return grad, part[:, 0]


def out_grad_kernel(rows_ref, mixed_ref, out_ref):
    out_ref[0] = narrow(over_rows(rows_ref[...], mixed_ref[...]))


def out_grads(rows, mixed):
    count, width = rows.shape
    return pl.pallas_call(
        out_grad_kernel,
        grid=(width // GROUP,),
        in_specs=[pl.BlockSpec((count, GROUP), lambda i: (0, i)), held(mixed.shape)],
        out_specs=pl.BlockSpec((1, GROUP, mixed.shape[1]), lambda i: (i, 0, 0)),
        out_shape=shaped((width // GROUP, GROUP, mixed.shape[1]), jnp.bfloat16),
        compiler_params=pltpu.CompilerParams(vmem_limit_bytes=VMEM_MAX),
        cost_estimate=spends(6),
        name="out_grads",
    )(rows, mixed)


def own_rows(ref, step):
    first = pl.ds(pl.multiple_of(step * 2 * ROWS_A, 16), 2 * ROWS_A)
    near = pl.ds(pl.multiple_of(8 * ROWS_A + step * ROWS_B, 16), ROWS_B)
    far = pl.ds(pl.multiple_of(8 * ROWS_A + 4 * ROWS_B + step * ROWS_B, 16), ROWS_B)
    return jnp.concatenate([ref[first], ref[near], ref[far]], axis=0)


def put_pieces(total, piece_refs, step):
    side = pl.ds(pl.multiple_of(step * ROWS_B, 16), ROWS_B)
    for k in range(4):

        @pl.when(step == k)
        def _(k=k):
            piece_refs[k][...] = total[: 2 * ROWS_A]

    piece_refs[4][side] = total[2 * ROWS_A : 2 * ROWS_A + ROWS_B]
    piece_refs[5][side] = total[2 * ROWS_A + ROWS_B :]


def attn_kernel(heads_ref, mixed_ref, *refs):
    weight_refs, (rows_ref, gain_ref, resid_ref, normed_ref, total_ref) = refs[:4], refs[4:]
    step = pl.program_id(0)

    @pl.when(step == 0)
    def _():
        total_ref[...] = wide(rows_ref[...])

    pair = jnp.concatenate([mixed_ref[heads_ref[0, step]], mixed_ref[heads_ref[1, step]]], axis=1)
    cut = weight_refs[0].shape[0]
    total_ref[:, :cut] += against(pair, jnp.concatenate([weight_refs[0][...], weight_refs[1][...]], axis=1))
    total_ref[:, cut:] += against(pair, jnp.concatenate([weight_refs[2][...], weight_refs[3][...]], axis=1))

    @pl.when(step == pl.num_programs(0) - 1)
    def _():
        resid = total_ref[...]
        resid_ref[...] = resid
        _, unit = rms_parts(resid)
        normed_ref[...] = narrow(unit * gain_ref[...])


def out_weight_specs(out_parts):
    rows = out_parts[0].shape[0] // 16
    first = pl.BlockSpec((rows, LANES), lambda step, *_: (step % 4 * 2 + step // 4, 0))
    second = pl.BlockSpec((rows, LANES), lambda step, *_: (8 + step, 0))
    return [first, first, second, second]


def attend(heads, received, out_parts, rows, gain):
    shape = rows.shape
    return pl.pallas_call(
        attn_kernel,
        grid_spec=pltpu.PrefetchScalarGridSpec(
            num_scalar_prefetch=1,
            grid=(8,),
            in_specs=[whole(received.shape)] + out_weight_specs(out_parts) + [whole(shape), whole(gain.shape)],
            out_specs=[whole(shape), whole(shape)],
            scratch_shapes=[pltpu.VMEM(shape, jnp.float32)],
        ),
        out_shape=[shaped(shape), shaped(shape, jnp.bfloat16)],
        compiler_params=pltpu.CompilerParams(vmem_limit_bytes=VMEM_MAX),
        cost_estimate=spends(10),
        name="attend",
    )(heads, received, *out_parts, *out_parts, rows, gain)


def total_of(refs):
    first = refs[0][...] + wide(refs[1][...])
    second = refs[2][...] + wide(refs[3][...]) + wide(refs[4][...]) + wide(refs[5][...])
    return jnp.concatenate([first, second], axis=0)


def middle_kernel(heads_ref, *refs):
    pieces, (resid_ref, cot_ref, gain_ref), weight_refs = refs[:6], refs[6:9], refs[9:13]
    dresid_ref, dattn_ref, dgain_ref, dmixed_ref = refs[13:]
    step = pl.program_id(0)

    @pl.when(step == 0)
    def _():
        grad = total_of(pieces)
        scale, unit = rms_parts(resid_ref[...])
        dgain_ref[...] = jnp.sum(grad * unit, axis=0, keepdims=True)
        dresid = wide(cot_ref[...]) + rms_back(grad, gain_ref[...], scale, unit)
        dresid_ref[...] = dresid
        dattn_ref[...] = narrow(dresid)

    cut = weight_refs[0].shape[0]
    dattn = dattn_ref[...]
    weights = jnp.concatenate([weight_refs[0][...], weight_refs[1][...]], axis=1)
    total = plain_product(dattn[:, :cut], weights)
    weights = jnp.concatenate([weight_refs[2][...], weight_refs[3][...]], axis=1)
    total = narrow(total + plain_product(dattn[:, cut:], weights))
    dmixed_ref[heads_ref[0, step]] = total[:, :LANES]
    dmixed_ref[heads_ref[1, step]] = total[:, LANES:]


def middle(heads, pieces, resid, cot, gain, out_parts):
    shape = resid.shape
    mixed_shape = (16, shape[0], LANES)
    return pl.pallas_call(
        middle_kernel,
        grid_spec=pltpu.PrefetchScalarGridSpec(
            num_scalar_prefetch=1,
            grid=(8,),
            in_specs=[whole(piece.shape) for piece in pieces]
            + [whole(shape), whole(shape), whole(gain.shape)]
            + out_weight_specs(out_parts),
            out_specs=[whole(shape), whole(shape), whole((1, shape[1])), whole(mixed_shape)],
        ),
        out_shape=[shaped(shape), shaped(shape, jnp.bfloat16), shaped((1, shape[1])),
                   shaped(mixed_shape, jnp.bfloat16)],
        compiler_params=pltpu.CompilerParams(vmem_limit_bytes=VMEM_MAX),
        cost_estimate=spends(10),
        name="middle",
    )(heads, *pieces, resid, cot, gain, *out_parts, *out_parts)


def leave_kernel(*refs):
    total = refs[0][...] + refs[4][...]
    for ref in refs[1:4]:
        total = total + wide(ref[...])
    refs[5][...] = narrow(total)


def finish_kernel(*refs):
    pieces, (rows_ref, dresid_ref, gain_ref, out_ref) = refs[:6], refs[6:]
    scale, unit = rms_parts(wide(rows_ref[...]))
    out_ref[...] = dresid_ref[...] + rms_back(total_of(pieces), gain_ref[...], scale, unit)


def feed_kernel(halves, count, joins, heads_ref, *refs):
    normed_refs, refs = refs[:count], refs[count:]
    cot_refs, refs = refs[: len(halves)], refs[len(halves) :]
    weight_refs, refs = refs[:4], refs[4:]
    earlier_refs, refs = refs[: 2 * joins], refs[2 * joins :]
    fed_refs, dnormed_refs, refs = refs[:2], refs[2 : 2 + count], refs[2 + count :]
    hidden_ref, dpre_ref, normed_out_ref, cot_out_ref, normed_ref, cot_ref, out_ref, grad_ref = refs
    step, last = pl.program_id(0), pl.num_programs(0) - 1
    size = hidden_ref.shape[0]

    @pl.when(step == 0)
    def _():
        start = 0
        for ref in normed_refs:
            normed_ref[start : start + ref.shape[0]] = ref[...]
            start += ref.shape[0]
        for place, ref in enumerate(cot_refs):
            cot_ref[ROWS_A * place : ROWS_A * (place + 1)] = ref[...]

    rows = pl.ds(pl.multiple_of(step * size, 16), size)
    normed, cot = normed_ref[rows], cot_ref[rows]
    normed_out_ref[...] = normed
    cot_out_ref[...] = cot
    out, dnormed = 0.0, 0.0
    for half in range(2):
        gu_ref, down_ref = weight_refs[2 * half], weight_refs[2 * half + 1]
        pre = plain_product(normed, gu_ref[...])
        gate, up = pre[:, :HALF], pre[:, HALF:]
        dhidden = plain_product(cot, down_ref[...])
        sigmoid = jax.nn.sigmoid(gate)
        act = gate * sigmoid
        hidden = narrow(act * up)
        dgate = narrow(dhidden * up * sigmoid * (1.0 + gate * (1.0 - sigmoid)))
        dpre = jnp.concatenate([dgate, narrow(dhidden * act)], axis=1)
        hidden_ref[:, half * HALF : (half + 1) * HALF] = hidden
        dpre_ref[:, 2 * half * HALF : 2 * (half + 1) * HALF] = dpre
        out = out + against(hidden, down_ref[...])
        dnormed = dnormed + against(dpre, gu_ref[...])
    out_ref[rows] = narrow(out)
    grad_ref[rows] = narrow(dnormed)

    @pl.when(step == last)
    def _():
        start = 0
        for ref in dnormed_refs:
            ref[...] = grad_ref[start : start + ref.shape[0]]
            start += ref.shape[0]
        if joins:
            near_ref, far_ref = fed_refs
            near_ref[:ROWS_A] = earlier_refs[0][:ROWS_A]
            far_ref[:ROWS_A] = earlier_refs[0][ROWS_A:]
            for k in (1, 2, 3):
                base = 2 * ROWS_A * (k - 1)
                near_ref[ROWS_A * k : ROWS_A * (k + 1)] = out_ref[base : base + ROWS_A]
                far_ref[ROWS_A * k : ROWS_A * (k + 1)] = out_ref[base + ROWS_A : base + 2 * ROWS_A]
            near_ref[4 * ROWS_A :] = earlier_refs[1][...]
            far_ref[4 * ROWS_A :] = out_ref[6 * ROWS_A :]
        else:
            fed_refs[0][...] = out_ref[: 2 * ROWS_A]
            fed_refs[1][...] = out_ref[2 * ROWS_A :]


def held(shape, place=None):
    place = place or (lambda *_: (0,) * len(shape))
    return pl.BlockSpec(shape, place, pipeline_mode=pl.Buffered(1))


def feed(heads, pieces, halves, cot, own, other, steps, earlier=()):
    width = cot.shape[1]
    shapes = [piece.shape for piece in pieces]
    count = sum(shape[0] for shape in shapes)
    size = count // steps
    gate_up = held((width, 2 * HALF))
    down = held((width, HALF), lambda *_: (0, 2))

    def half_block(slot, half):
        return held((ROWS_A, width), lambda i, heads_ref: (2 * heads_ref[0, slot] + half, 0))

    fed_shapes = [(8 * ROWS_A, width)] * 2 if earlier else shapes
    row_widths = (2 * HALF, 4 * HALF, width, width)
    outs = pl.pallas_call(
        partial(feed_kernel, tuple(halves), len(pieces), bool(earlier)),
        grid_spec=pltpu.PrefetchScalarGridSpec(
            num_scalar_prefetch=1,
            grid=(steps,),
            in_specs=[held(shape) for shape in shapes]
            + [half_block(*half) for half in halves]
            + [gate_up, down, gate_up, down]
            + [held(piece.shape) for piece in earlier],
            out_specs=[whole(shape) for shape in fed_shapes + shapes]
            + [pl.BlockSpec((size, part), lambda i, *_: (i, 0)) for part in row_widths],
            scratch_shapes=[pltpu.VMEM((count, width), jnp.bfloat16)] * 4,
        ),
        out_shape=[shaped(shape, jnp.bfloat16) for shape in fed_shapes + shapes]
        + [shaped((count, part), jnp.bfloat16) for part in row_widths],
        compiler_params=pltpu.CompilerParams(vmem_limit_bytes=VMEM_MAX),
        cost_estimate=spends(28),
        name="feed",
    )(heads, *pieces, *[cot] * len(halves), own, own, other, other, *earlier)
    return outs[:2], outs[2 : 2 + len(shapes)], outs[2 + len(shapes) :]


def join_kernel(*refs):
    sources, target, sems = refs[:-2], refs[-2], refs[-1]
    copies, start = [], 0
    for place, ref in enumerate(sources):
        copies.append(pltpu.make_async_copy(ref, target.at[pl.ds(start, ref.shape[0])], sems.at[place]))
        copies[-1].start()
        start += ref.shape[0]
    for copy in copies:
        copy.wait()


def join(pieces):
    anywhere = pl.BlockSpec(memory_space=pl.ANY)
    rows = sum(piece.shape[0] for piece in pieces)
    return pl.pallas_call(
        join_kernel,
        in_specs=[anywhere] * len(pieces),
        out_specs=pl.BlockSpec(memory_space=pltpu.VMEM),
        out_shape=shaped((rows, pieces[0].shape[1]), pieces[0].dtype),
        scratch_shapes=[pltpu.SemaphoreType.DMA((len(pieces),))],
        compiler_params=pltpu.CompilerParams(vmem_limit_bytes=VMEM_MAX),
        cost_estimate=spends(3),
        name="join",
    )(*pieces)


def plain_product(left, right):
    return jnp.dot(left, right, preferred_element_type=jnp.float32)


def against(left, right):
    return lax.dot_general(left, right, (((1,), (1,)), ((), ())), preferred_element_type=jnp.float32)


def over_rows(left, right):
    return lax.dot_general(left, right, (((0,), (0,)), ((), ())), preferred_element_type=jnp.float32)


def tables():
    head = lax.axis_index("head")
    ring, side, core = head // 4, head // 2 % 2, head % 2
    chunk = jnp.arange(16, dtype=jnp.int32)
    dz, dx, dc = (chunk // 4 - ring) % 4, (chunk // 2 + side) % 2, (chunk + core) % 2
    place = jnp.stack([ROWS_A * (2 * dz + dx), 8 * ROWS_A + ROWS_B * (4 * dx + dz), dc]).astype(jnp.int32)
    step = jnp.arange(8, dtype=jnp.int32)
    chip = ((step + ring) % 4) * 2 + (step // 4 + side) % 2
    heads = jnp.stack([2 * chip + core, 2 * chip + 1 - core]).astype(jnp.int32)
    return place, heads


def body(
    tokens,
    cotangent,
    doc_spans,
    norm1_gain,
    q_weight,
    k_weight,
    v_weight,
    gate_out_weight,
    decay_weight,
    conv_weight,
    gate_params,
    out_gain,
    out_weight,
    norm2_gain,
    gate_weight,
    up_weight,
    down_weight,
):
    place, heads = tables()
    starts = document_starts(doc_spans[0], 32)
    out_gain_row = out_gain[None, :]
    gain1_row, gain2_row = norm1_gain[None, :], norm2_gain[None, :]
    rows_shape = tokens.shape
    width = rows_shape[1]

    def pad(weight, columns):
        return jnp.pad(weight, ((0, 0), (0, columns - weight.shape[1])))

    (normed1,) = whole_call(enter_kernel, shaped(rows_shape, jnp.bfloat16), "enter", (), tokens, gain1_row)

    packed = (conv_weight, decay_weight, q_weight, k_weight, v_weight, gate_out_weight, out_weight)
    conv_now, decay_now, *square_now = lax.optimization_barrier(packed + (normed1,))[:7]
    taps_block = jnp.pad(conv_now.reshape(12, 16), ((0, GROUP - 12), (0, 0)))
    side_block = pad(jnp.concatenate([decay_now[:, 0], taps_block], axis=1), LANES)
    pack_one = jnp.concatenate(square_now[:4] + [side_block] + square_now[4:], axis=1)
    wide_now = lax.optimization_barrier((gate_weight, up_weight, down_weight, normed1))[:3]
    pack_two = jnp.concatenate([pad(weight, HALF) for weight in wide_now], axis=1)
    cut, used = pack_one.shape[1], 5 * LANES

    mate_one = take_yx(pack_one, 0, 1)
    pair, column = gather_turn(normed1, ROWS_A, beside=(mate_one,))
    pair, column, mate_one = lax.optimization_barrier((pair, column, mate_one))
    mate_two = take_yx(after(pack_two, mate_one), 0, 1)
    mine_one = round_ring(spread_pair(pack_one, mate_one))
    rings, columns = gather_end(pair, column)
    rings, columns, mine_one, mate_two = lax.optimization_barrier((rings, columns, mine_one, mate_two))
    spread_two = spread_pair(pack_two, mate_two)
    normed1_own = join(rings + columns)
    normed1_other = from_head(normed1_own, dc=1)
    raw0, raw1 = project(normed1_own, normed1_other, mine_one, used)
    taps = mine_one.reshape(8, GROUP, cut)[:, :12, 4 * LANES + 2 : 4 * LANES + 18]
    taps = wide(taps.transpose(1, 0, 2).reshape(3, 4, LANES))

    mine_two = round_ring(spread_two)

    out_turn = gather_turn(after(mine_one[:, used:], normed1_own), width // 2, beside=(raw0,))
    raw0, raw1, out_turn = lax.optimization_barrier((raw0, raw1, out_turn))
    out_rings, out_columns = gather_end(*out_turn)
    prepared = prepare(place, starts, gate_params, raw0, raw1, taps)
    mixed, kept = mixer_forward(place, prepared, raw0, raw1, out_gain_row)
    mixed, mine_two, out_rings, out_columns = lax.optimization_barrier((mixed, mine_two, out_rings, out_columns))
    cot_group = lax.all_gather(after(cotangent, mixed), "head", axis=0, tiled=True)
    received = lax.all_to_all(mixed, "head", 0, 0, tiled=False)
    out_own = join(out_rings + out_columns)
    out_parts = (out_own, from_head(out_own, dc=1))
    other_two = from_head(mine_two, dc=1)
    received, other_two = lax.optimization_barrier((received, other_two))
    resid, normed2 = attend(heads, received, out_parts, tokens, gain2_row)
    pair, column = gather_turn(normed2, ROWS_A)
    rings, columns = gather_end(pair, column)
    near_halves = [(0, 0), (4, 0)] + [(k, 1) for k in range(4)]
    far_halves = [half for k in (1, 2, 3) for half in ((k, 0), (4 + k, 0))] + [(4 + k, 1) for k in range(4)]
    fed_early, (dpair, dnear), kept_near = feed(
        heads, [pair, column], near_halves, cot_group, mine_two, other_two, 1
    )
    rings, columns, dpair = lax.optimization_barrier((rings, columns, dpair))
    (fed_near, fed_far), (*drings, dfar), kept_far = feed(
        heads, rings[1:] + columns[1:], far_halves, cot_group, mine_two, other_two, 2, fed_early
    )

    parts = reduce_parts(dpair, dnear, reduce_arrivals(drings, dfar))
    feed_own, feed_other = feed_grads(kept_near, kept_far)
    parts, feed_own, feed_other = lax.optimization_barrier((parts, feed_own, feed_other))
    feed_grad = narrow(wide(feed_own) + wide(from_head(feed_other, dc=1)))
    dnormed2_pieces = reduce_end(parts)
    feed_blocks = ring_blocks(feed_grad)
    resid_then = after(resid, feed_blocks)
    feed_blocks = lax.optimization_barrier((feed_blocks, dnormed2_pieces))[0]
    dresid, dattn, dgain2, dmixed = middle(heads, dnormed2_pieces, resid_then, cotangent, gain2_row, out_parts)
    dmixed_mine = lax.all_to_all(dmixed, "head", 0, 0, tiled=False)
    dcore, dstates, dgate, dgain_out = mixer_backward_scan(place, raw0, raw1, out_gain_row, kept, dmixed_mine)

    feed_arrived = ring_arrivals(feed_blocks)
    fed_crossed = take_zx(after(fed_far, dcore), 0, 1)
    dattn_group = lax.all_gather(dattn, "head", axis=0, tiled=True)
    weights_other = from_head(after(mine_one, dmixed), dc=1)

    draw0, draw1, dtaps, dparams = mixer_backward(
        place, starts, gate_params, raw0, raw1, taps, kept, dstates, dcore, dgate
    )
    draw0, draw1, weights_other, feed_arrived = lax.optimization_barrier((draw0, draw1, weights_other, feed_arrived))
    draw_far = from_head(draw1, dc=1)
    in_grad, gain1_part = in_grads(normed1_own, normed1_other, draw0, draw1, mine_one, gain1_row)
    in_arrived = exchange_ring(in_grad)
    draw_far = after(draw_far, in_grad)
    dnormed1 = unproject(draw0, draw_far, mine_one, weights_other, [dpair.shape] * 4 + [dnear.shape] * 2)
    dnormed1, feed_arrived, dattn_then = lax.optimization_barrier((dnormed1, feed_arrived, dattn_group))
    feed_kept, feed_sent = ring_parts(feed_arrived)
    out_grad = out_grads(dattn_then, mixed.reshape(dattn_group.shape[0], LANES))
    arrived = reduce_arrivals(
        dnormed1[1:4], dnormed1[5], beside=(feed_kept, feed_sent, out_grad, fed_crossed)
    )
    dnormed1_pieces = reduce_end(reduce_parts(dnormed1[0], dnormed1[4], arrived))
    fed_crossed, feed_sent = lax.optimization_barrier((fed_crossed, feed_sent, arrived))[:2]
    half_rows = (ROWS_A + ROWS_B, width)
    fed_sums = whole_call(
        side_sum_kernel, [shaped(half_rows)] + [shaped(half_rows, jnp.bfloat16)] * 3, "side_sum", (), fed_near, fed_crossed
    )
    fed_pieces = [fed_sums[0]] + [take_zx(fed_sums[k], -k, 0) for k in (1, 2, 3)]
    in_kept, in_sent = ring_parts(list(after(in_arrived, *arrived)))
    one_total = in_kept + wide(take_yx(in_sent, 0, 1))
    small = jnp.concatenate(
        [
            gain1_part.reshape(16, LANES),
            dgain2.reshape(16, LANES),
            dgain_out,
            dparams,
            dtaps.reshape(12, LANES),
            jnp.zeros((4, LANES), jnp.float32),
        ],
        axis=0,
    )
    high, rest = split(small)
    small_rows = jnp.concatenate([high, rest, narrow(small - wide(high) - wide(rest))], axis=0)
    sent = jnp.concatenate(
        [out_grad, jnp.broadcast_to(small_rows, (8,) + small_rows.shape)], axis=1
    )
    got = lax.all_to_all(after(sent, in_arrived, *arrived), "dp", 0, 0, tiled=False)
    out_total = jnp.sum(wide(got[:, :GROUP]), axis=0)
    pieces = wide(got[:, GROUP:]).reshape(8, 3, small.shape[0], LANES)
    small = jnp.sum(pieces[:, 0] + pieces[:, 1] + pieces[:, 2], axis=0)
    shared = sum_all(small[:40], "head", 16)
    fed_pieces, shared = lax.optimization_barrier((fed_pieces, shared))
    (block_out,) = whole_call(leave_kernel, shaped(rows_shape, jnp.bfloat16), "leave", (), *fed_pieces, resid)
    feed_total = feed_kept + wide(take_yx(feed_sent, 0, 1))

    gain1_total = shared[:16].reshape(-1)
    gain2_total = shared[16:32].reshape(-1)
    out_gain_total = jnp.sum(shared[32:40], axis=0)
    params_total = jnp.sum(small[40:48], axis=1)[:2, None]
    taps_total = lax.dynamic_slice_in_dim(
        small[48:60].reshape(3, 4, LANES), lax.axis_index("dp") * 16, 16, 2
    )
    (tokens_grad,) = whole_call(
        finish_kernel, shaped(rows_shape), "finish", (), *dnormed1_pieces, tokens, dresid, gain1_row
    )
    hidden_units = gate_weight.shape[1]
    return (
        block_out,
        tokens_grad,
        gain1_total,
        one_total[:, :LANES],
        one_total[:, LANES : 2 * LANES],
        one_total[:, 2 * LANES : 3 * LANES],
        one_total[:, 3 * LANES : 4 * LANES],
        one_total[:, 4 * LANES : 4 * LANES + 2][:, None, :],
        taps_total,
        params_total,
        out_gain_total,
        out_total,
        gain2_total,
        feed_total[:, :hidden_units],
        feed_total[:, HALF : HALF + hidden_units],
        feed_total[:, 2 * HALF : 2 * HALF + hidden_units],
    )


def solution(mesh):
    rows, weight = P(("dp", "head"), None), P("dp", "head")
    weight3, taps = P("dp", "head", None), P(None, None, ("head", "dp"))
    params = P(None, "head")
    in_specs = (
        rows, rows, P("dp", None), P(), weight, weight, weight, weight, weight3, taps, params, P(),
        weight, P(), weight, weight, weight,
    )
    out_specs = (
        rows, rows, P(), weight, weight, weight, weight, weight3, taps, params, P(),
        weight, P(), weight, weight, weight,
    )
    return jax.shard_map(body, mesh=mesh, in_specs=in_specs, out_specs=out_specs, check_vma=False)
```

```python
from functools import partial

import jax
import jax.numpy as jnp
from jax import lax
from jax.experimental import pallas as pl
from jax.experimental.pallas import tpu as pltpu

CHUNK = 128
BATCH = 4
ROWS_A = 80
ROWS_B = 48
GATE_ALONE = 9
VMEM_MAX = 56 * 1024 * 1024


def spends(microseconds):
    return pl.CostEstimate(flops=int(microseconds * 1e6), bytes_accessed=1 << 10, transcendentals=0)


def split(value):
    high = value.astype(jnp.bfloat16)
    return high, (value - high.astype(jnp.float32)).astype(jnp.bfloat16)


def left_pair(value):
    return jnp.concatenate(split(value), axis=1)


def right_pair(value):
    high, low = split(value)
    wide = jnp.concatenate([high, low], axis=1)
    return jnp.concatenate([wide, wide], axis=0)


def right_pair_t(value):
    high, low = split(value)
    return jnp.concatenate(
        [jnp.concatenate([high, high], axis=1), jnp.concatenate([low, low], axis=1)], axis=0
    )


def fold(wide):
    half = wide.shape[1] // 2
    return wide[:, :half] + wide[:, half:]


def mul_pairs(left, right):
    return fold(jnp.dot(left, right, preferred_element_type=jnp.float32))


def mul(left, right):
    return mul_pairs(left_pair(left), right_pair(right))


def mul_t(left, right):
    return fold(
        lax.dot_general(
            left_pair(left),
            right_pair_t(right),
            (((1,), (1,)), ((), ())),
            preferred_element_type=jnp.float32,
        )
    )


def iotas(rows=CHUNK, cols=CHUNK):
    return (
        lax.broadcasted_iota(jnp.int32, (rows, cols), 0),
        lax.broadcasted_iota(jnp.int32, (rows, cols), 1),
    )


def silu_parts(value):
    gate = jax.nn.sigmoid(value)
    return gate, value * gate


def tap_masks(start_first, start_second, row_index):
    keeps = []
    for offset in range(1, 4):
        first = jnp.where(row_index < offset, 1.0 - start_first, 1.0)
        second = jnp.where(
            (row_index >= CHUNK // 2) & (row_index < CHUNK // 2 + offset), 1.0 - start_second, 1.0
        )
        keeps.append(first * second)
    return keeps


def shifted_rows(current, before, keeps):
    joined = jnp.concatenate([before, current], axis=0)
    return [current] + [
        pltpu.roll(joined, offset, 0)[8:] * keeps[offset - 1] for offset in range(1, 4)
    ]


def conv_rows(rows_by_offset, taps):
    total = rows_by_offset[0] * taps[3:4]
    for offset in range(1, 4):
        total = total + rows_by_offset[offset] * taps[3 - offset : 4 - offset]
    return total


def chunk_cols(rows):
    return jnp.transpose(jnp.concatenate([rows, jnp.zeros((CHUNK - 8, CHUNK), jnp.float32)], axis=0))


def decay_matrix(rows, cols, start_second):
    row_index, col_index = iotas()
    gap = cols[:, 0:1] - rows[0:1, :]
    lower = row_index >= col_index
    cross = (row_index >= CHUNK // 2) & (col_index < CHUNK // 2)
    decay = jnp.where(lower, jnp.exp(jnp.where(lower, gap, 0.0)), 0.0)
    return decay * jnp.where(cross, 1.0 - start_second, 1.0)


def head_rows(raw_refs, place_ref, chunk, part):
    def load(start, count):
        rows = pl.ds(pl.multiple_of(start, 8), count)
        return jnp.where(half == 0, raw_refs[0][rows, lanes], raw_refs[1][rows, lanes])

    lanes = slice(None) if part == GATE_ALONE else slice(part * CHUNK, (part + 1) * CHUNK)
    half = place_ref[2, chunk]
    current = jnp.concatenate(
        [load(place_ref[0, chunk], ROWS_A), load(place_ref[1, chunk], ROWS_B)], axis=0
    )
    if part > 2:
        return current
    earlier = jnp.maximum(chunk - 1, 0)
    half = place_ref[2, earlier]
    return current, load(place_ref[1, earlier] + ROWS_B - 8, 8)


def put_rows(out_ref, place_ref, chunk, lanes, value):
    half = place_ref[2, chunk]
    first = pl.ds(pl.multiple_of(place_ref[0, chunk], 16), ROWS_A)
    second = pl.ds(pl.multiple_of(place_ref[1, chunk], 16), ROWS_B)
    out_ref[half, first, lanes] = value[:ROWS_A]
    out_ref[half, second, lanes] = value[ROWS_A:]


def spread_sum(rows, matrix):
    high, rest = split(rows)
    mid = rest
    low = (rows - high.astype(jnp.float32) - mid.astype(jnp.float32)).astype(jnp.bfloat16)
    parts = jnp.concatenate([high, mid, low, jnp.zeros_like(low)], axis=0)
    wide = jnp.dot(parts, matrix.astype(jnp.bfloat16), preferred_element_type=jnp.float32)
    return wide[:8] + wide[8:16] + wide[16:24]


def gate_rows(decay_cols, starts, params_ref):
    row_index, col_index = iotas()
    pair = jnp.transpose(decay_cols)[:8]
    position = col_index[:8]
    kind = row_index[:8]
    carry, same = 1.0 - starts[0], 1.0 - starts[1]
    second = position >= CHUNK // 2
    beta = jax.nn.sigmoid(pair[1:2])
    inside = pair[0:1] + params_ref[1, 0]
    soft = jax.nn.softplus(inside)
    decay_log = -jnp.exp(params_ref[0, 0] + jnp.zeros((8, CHUNK), jnp.float32)) * soft
    total = spread_sum(decay_log, (row_index <= col_index).astype(jnp.float32))
    end = total[:, CHUNK - 1 :]
    gam = jnp.exp(total) * carry * jnp.where(second, same, 1.0)
    tail = jnp.exp(end - total) * jnp.where(second, 1.0, same)
    span = jnp.exp(end) * carry * same
    rows = jnp.where(kind == 0, total, jnp.where(kind == 1, beta, jnp.where(kind == 2, gam, tail)))
    return jnp.where(kind == 4, span, rows)


def convolved(raw_refs, place_ref, starts, taps_ref, chunk, row_index):
    keeps = tap_masks(starts[0], starts[1], row_index)
    pieces = []
    for part in range(3):
        current, before = head_rows(raw_refs, place_ref, chunk, part)
        rows_by_offset = shifted_rows(current, before, keeps)
        pieces.append((rows_by_offset, conv_rows(rows_by_offset, taps_ref[part])))
    return keeps, pieces


def start_flags(starts_ref, chunk):
    return (
        starts_ref[2 * chunk].astype(jnp.float32),
        starts_ref[2 * chunk + 1].astype(jnp.float32),
    )


def normed_qkv(pieces):
    acts = [piece[1] * jax.nn.sigmoid(piece[1]) for piece in pieces]
    q_scale = lax.rsqrt(jnp.sum(acts[0] * acts[0], axis=-1, keepdims=True) + 1e-06)
    k_scale = lax.rsqrt(jnp.sum(acts[1] * acts[1], axis=-1, keepdims=True) + 1e-06)
    return acts[0] * q_scale * CHUNK ** (-0.5), acts[1] * k_scale, acts[2], q_scale, k_scale


def inverse_lower(stricts):
    row_index, col_index = iotas()
    eye = (row_index == col_index).astype(jnp.float32)
    near = row_index // 16 == col_index // 16
    powers = [jnp.where(near, strict, 0.0) for strict in stricts]
    inverses = [eye - power for power in powers]
    powers = [mul(power, power) for power in powers]
    for step in range(3):
        rights = [right_pair(power) for power in powers]
        if step < 2:
            stacks = [
                left_pair(jnp.concatenate([inverse, power], axis=0))
                for inverse, power in zip(inverses, powers)
            ]
            both = [mul_pairs(stack, right) for stack, right in zip(stacks, rights)]
            inverses = [inverse + pair[:CHUNK] for inverse, pair in zip(inverses, both)]
            powers = [pair[CHUNK:] for pair in both]
        else:
            inverses = [
                inverse + mul_pairs(left_pair(inverse), right)
                for inverse, right in zip(inverses, rights)
            ]
    for width in (16, 32, 64):
        beside = (row_index // (2 * width) == col_index // (2 * width)) & (
            row_index // width != col_index // width
        )
        crossed = [
            mul(inverse, jnp.where(beside, strict, 0.0))
            for inverse, strict in zip(inverses, stricts)
        ]
        inverses = [inverse - mul(cross, inverse) for cross, inverse in zip(crossed, inverses)]
    return inverses


def prepare_kernel(place_ref, starts_ref, params_ref, raw0_ref, raw1_ref, taps_ref,
                   rows_out_ref, inv_ref, kkf_ref, p_ref, uw_ref, m_ref, mt_ref, b_ref, r_ref, pu_ref):
    row_index, col_index = iotas()
    diagonal = (row_index == col_index).astype(jnp.float32)
    stricts, kept = [], []
    for member in range(BATCH):
        chunk = pl.program_id(0) * BATCH + member
        starts = start_flags(starts_ref, chunk)
        raw_refs = (raw0_ref, raw1_ref)
        _, pieces = convolved(raw_refs, place_ref, starts, taps_ref, chunk, row_index)
        queries, keys_in, values_in, _, _ = normed_qkv(pieces)
        rows = gate_rows(head_rows(raw_refs, place_ref, chunk, 4), starts, params_ref)
        rows_out_ref[member] = rows
        cols = chunk_cols(rows)
        decay = decay_matrix(rows, cols, starts[1])
        beta, gam, tail = cols[:, 1:2], cols[:, 2:3], cols[:, 3:4]
        scores = mul_t(jnp.concatenate([keys_in, queries], axis=0), keys_in)
        kkf = jnp.where(row_index > col_index, scores[:CHUNK] * decay, 0.0)
        inner = scores[CHUNK:] * decay
        stricts.append(kkf * beta)
        kkf_ref[member] = kkf
        p_ref[member] = inner
        pair = jnp.concatenate([values_in * beta, keys_in * (beta * gam)], axis=1)
        stack = jnp.concatenate([jnp.transpose(keys_in * tail), inner], axis=0)
        kept.append((pair, stack, diagonal * rows[4:5], queries * gam))
    inverses = inverse_lower(stricts)
    joined = [mul(inverse, pair) for inverse, (pair, _, _, _) in zip(inverses, kept)]
    both = [mul(stack, join) for join, (_, stack, _, _) in zip(joined, kept)]
    for member in range(BATCH):
        _, _, span, faded = kept[member]
        inv_ref[member] = inverses[member]
        uw_ref[member] = joined[member]
        state_map = span - both[member][:CHUNK, CHUNK:]
        m_ref[member] = left_pair(state_map)
        mt_ref[member] = left_pair(jnp.transpose(state_map))
        b_ref[member] = both[member][:CHUNK, :CHUNK]
        r_ref[member] = faded - both[member][CHUNK:, CHUNK:]
        pu_ref[member] = both[member][CHUNK:, :CHUNK]


def whole(shape):
    return pl.BlockSpec(shape, lambda *_: (0,) * len(shape))


def per_batch(shape, turned=False, steps=4):
    def place(step, *_):
        return ((steps - 1 - step) if turned else step,) + (0,) * (len(shape) - 1)

    return pl.BlockSpec(shape, place)


def shaped(shape, dtype=jnp.float32):
    return jax.ShapeDtypeStruct(shape, dtype)


def prepare(place, starts, params, raw0, raw1, taps):
    chunks = place.shape[1]
    square = (BATCH, CHUNK, CHUNK)
    wide = (BATCH, CHUNK, 2 * CHUNK)
    kinds = [((BATCH, 8, CHUNK), jnp.float32), (square, jnp.float32), (square, jnp.float32), (square, jnp.float32),
             (wide, jnp.float32), (wide, jnp.bfloat16), (wide, jnp.bfloat16), (square, jnp.float32),
             (square, jnp.float32), (square, jnp.float32)]
    return pl.pallas_call(
        prepare_kernel,
        grid_spec=pltpu.PrefetchScalarGridSpec(
            num_scalar_prefetch=3,
            grid=(chunks // BATCH,),
            in_specs=[whole(raw0.shape), whole(raw1.shape), whole(taps.shape)],
            out_specs=[per_batch(shape) for shape, _ in kinds],
        ),
        out_shape=[shaped((chunks,) + shape[1:], dtype) for shape, dtype in kinds],
        compiler_params=pltpu.CompilerParams(vmem_limit_bytes=VMEM_MAX),
        cost_estimate=spends(18),
        name="prepare",
    )(place, starts, params, raw0, raw1, taps)


def gate_rows_of(gate_refs, place_ref, chunk):
    return head_rows(gate_refs, place_ref, chunk, GATE_ALONE)


def scan_kernel(place_ref, m_ref, b_ref, r_ref, pu_ref, gate0_ref, gate1_ref, gain_ref,
                state_out_ref, core_ref, mixed_ref, state_ref):
    @pl.when(pl.program_id(0) == 0)
    def _():
        state_ref[...] = jnp.zeros_like(state_ref)

    state = state_ref[...]
    for member in range(BATCH):
        chunk = pl.program_id(0) * BATCH + member
        state_out_ref[member] = state
        pair = right_pair(state)
        core = mul_pairs(left_pair(r_ref[member]), pair) + pu_ref[member]
        state = mul_pairs(m_ref[member], pair) + b_ref[member]
        _, gate = silu_parts(gate_rows_of((gate0_ref, gate1_ref), place_ref, chunk))
        core_ref[member] = core
        scale = lax.rsqrt(jnp.mean(core * core, axis=-1, keepdims=True) + 1e-05)
        mixed = (core * scale * gain_ref[...] * gate).astype(jnp.bfloat16)
        mixed_ref[member] = mixed
    state_ref[...] = state


def gate_columns(raw):
    return pl.BlockSpec((raw.shape[0], CHUNK), lambda *_: (0, 3))


def scan_states(place, m, b, r, pu, raw0, raw1, gain):
    chunks = m.shape[0]
    square = (BATCH, CHUNK, CHUNK)
    wide = (BATCH, CHUNK, 2 * CHUNK)
    return pl.pallas_call(
        scan_kernel,
        grid_spec=pltpu.PrefetchScalarGridSpec(
            num_scalar_prefetch=1,
            grid=(chunks // BATCH,),
            in_specs=[per_batch(wide), per_batch(square), per_batch(square), per_batch(square),
                      gate_columns(raw0), gate_columns(raw1), whole((1, CHUNK))],
            out_specs=[per_batch(square)] * 3,
            scratch_shapes=[pltpu.VMEM((CHUNK, CHUNK), jnp.float32)],
        ),
        out_shape=[shaped((chunks, CHUNK, CHUNK)), shaped((chunks, CHUNK, CHUNK)),
                   shaped((chunks, CHUNK, CHUNK), jnp.bfloat16)],
        compiler_params=pltpu.CompilerParams(vmem_limit_bytes=VMEM_MAX),
        cost_estimate=spends(7),
        name="scan_states",
    )(place, m, b, r, pu, raw0, raw1, gain)


def back_scan_kernel(place_ref, mt_ref, r_ref, core_ref, gate0_ref, gate1_ref, dmixed_ref, gain_ref,
                     dcore_ref, dstate_out_ref, dgate_ref, dgain_ref, dstate_ref):
    step = pl.program_id(0)

    @pl.when(step == 0)
    def _():
        dstate_ref[...] = jnp.zeros_like(dstate_ref)
        dgain_ref[...] = jnp.zeros_like(dgain_ref)

    gain = gain_ref[...]
    dgain = jnp.zeros((8, CHUNK), jnp.float32)
    terms = []
    for member in reversed(range(BATCH)):
        chunk = (pl.num_programs(0) - 1 - step) * BATCH + member
        core = core_ref[member]
        raw_gate = gate_rows_of((gate0_ref, gate1_ref), place_ref, chunk)
        dmixed = dmixed_ref[member].astype(jnp.float32)
        gate, gated = silu_parts(raw_gate)
        scale = lax.rsqrt(jnp.mean(core * core, axis=-1, keepdims=True) + 1e-05)
        unit = core * scale
        dscaled = dmixed * gated
        dgate = dmixed * unit * gain * (gate * (1.0 + raw_gate * (1.0 - gate)))
        dgate_ref[member] = dgate.astype(jnp.bfloat16)
        product = dscaled * unit
        dgain = dgain + jnp.sum(product.reshape(CHUNK // 8, 8, CHUNK), axis=0)
        dunit = dscaled * gain
        dcore = scale * (dunit - unit * jnp.mean(dunit * unit, axis=-1, keepdims=True))
        dcore_ref[member] = dcore
        terms.append((member, mul(jnp.transpose(r_ref[member]), dcore)))
    dgain_ref[...] += dgain
    dstate = dstate_ref[...]
    for member, term in terms:
        dstate_out_ref[member] = dstate
        dstate = mul_pairs(mt_ref[member], right_pair(dstate)) + term
    dstate_ref[...] = dstate


def back_scan(place, mt, r, core, raw0, raw1, dmixed, gain):
    chunks = mt.shape[0]
    square = (BATCH, CHUNK, CHUNK)
    wide = (BATCH, CHUNK, 2 * CHUNK)
    turned = partial(per_batch, turned=True, steps=chunks // BATCH)
    return pl.pallas_call(
        back_scan_kernel,
        grid_spec=pltpu.PrefetchScalarGridSpec(
            num_scalar_prefetch=1,
            grid=(chunks // BATCH,),
            in_specs=[turned(wide), turned(square), turned(square),
                      gate_columns(raw0), gate_columns(raw1), turned(square), whole((1, CHUNK))],
            out_specs=[turned(square), turned(square), turned(square), whole((8, CHUNK))],
            scratch_shapes=[pltpu.VMEM((CHUNK, CHUNK), jnp.float32)],
        ),
        out_shape=[shaped((chunks, CHUNK, CHUNK)), shaped((chunks, CHUNK, CHUNK)),
                   shaped((chunks, CHUNK, CHUNK), jnp.bfloat16), shaped((8, CHUNK))],
        compiler_params=pltpu.CompilerParams(vmem_limit_bytes=VMEM_MAX),
        cost_estimate=spends(7),
        name="back_scan",
    )(place, mt, r, core, raw0, raw1, dmixed, gain)


def lane_sum(value):
    return jnp.sum(value, axis=1, keepdims=True)


def back_kernel(place_ref, starts_ref, params_ref, raw0_ref, raw1_ref, rows_ref, taps_ref, inv_ref, kkf_ref,
                p_ref, uw_ref, state_ref, dstate_ref, dcore_ref, dgate_ref,
                draw0_ref, draw1_ref, dtaps_ref, dparams_ref, next_ref, draw_ref):
    step = pl.program_id(0)
    row_index, col_index = iotas()
    lower = row_index >= col_index
    strict = row_index > col_index

    @pl.when(step == 0)
    def _():
        next_ref[...] = jnp.zeros_like(next_ref)
        dtaps_ref[...] = jnp.zeros_like(dtaps_ref)
        dparams_ref[...] = jnp.zeros_like(dparams_ref)

    raw_refs = (raw0_ref, raw1_ref)
    members = range(BATCH)
    setups = []
    for member in members:
        chunk = (pl.num_programs(0) - 1 - step) * BATCH + member
        starts = start_flags(starts_ref, chunk)
        keeps, pieces = convolved(raw_refs, place_ref, starts, taps_ref, chunk, row_index)
        queries, keys_in, values_in, q_scale, k_scale = normed_qkv(pieces)
        rows = rows_ref[member]
        cols = chunk_cols(rows)
        decay = decay_matrix(rows, cols, starts[1])
        setups.append((starts, keeps, pieces, queries, keys_in, values_in, q_scale, k_scale, rows, cols, decay))
    fresh = [
        uw_ref[i][:, :CHUNK] - mul(uw_ref[i][:, CHUNK:], state_ref[i]) for i in members
    ]
    dfresh = [
        mul(jnp.transpose(p_ref[i]), dcore_ref[i])
        + mul(setups[i][4] * setups[i][9][:, 3:4], dstate_ref[i])
        for i in members
    ]
    through = [
        mul_t(jnp.concatenate([dcore_ref[i], dfresh[i]], axis=0), state_ref[i]) for i in members
    ]
    dinner = [jnp.where(lower, mul_t(dcore_ref[i], fresh[i]), 0.0) for i in members]
    dkeys_tail = [mul_t(fresh[i], dstate_ref[i]) for i in members]
    dboth = [
        mul(
            jnp.transpose(inv_ref[i]),
            jnp.concatenate([dfresh[i], -through[i][CHUNK:]], axis=1),
        )
        for i in members
    ]
    dstrict = [jnp.where(strict, -mul_t(dboth[i], uw_ref[i]), 0.0) for i in members]
    stacked, crossed = [], []
    for i in members:
        queries, keys_in, cols, decay = setups[i][3], setups[i][4], setups[i][9], setups[i][10]
        dscores_n = dstrict[i] * decay * cols[:, 1:2]
        dscores = dinner[i] * decay
        stacked.append(
            mul(jnp.concatenate([dscores, dscores_n + jnp.transpose(dscores_n)], axis=0), keys_in)
        )
        crossed.append(mul(jnp.transpose(dscores), queries))
    for i in reversed(members):
        starts, keeps, pieces, queries, keys_in, values_in, q_scale, k_scale, rows, cols, _ = setups[i]
        beta, gam, tail = cols[:, 1:2], cols[:, 2:3], cols[:, 3:4]
        dqueries_faded = through[i][:CHUNK]
        dvalues_beta, dkeys_beta = dboth[i][:, :CHUNK], dboth[i][:, CHUNK:]
        keys_gam = keys_in * gam
        dqueries = stacked[i][:CHUNK] + dqueries_faded * gam
        dkeys = (
            stacked[i][CHUNK:]
            + crossed[i]
            + dkeys_beta * (beta * gam)
            + dkeys_tail[i] * tail
        )
        dvalues = dvalues_beta * beta

        dkkf = dstrict[i] * kkf_ref[i]
        flow = dkkf * beta + dinner[i] * p_ref[i]
        tail_term = lane_sum(dkeys_tail[i] * keys_in * tail)
        dbeta = lane_sum(dkkf + dvalues_beta * values_in + dkeys_beta * keys_gam)
        dsum = (
            lane_sum(flow + (dqueries_faded * queries + dkeys_beta * keys_in * beta) * gam)
            - tail_term
        )
        last = jnp.sum(tail_term) + jnp.sum(state_ref[i] * dstate_ref[i] * rows[4:5, 0:1])
        last_col = jnp.where(row_index[:, :1] == CHUNK - 1, last, 0.0)
        packed = jnp.where(
            col_index == 0, dsum + last_col, jnp.where(col_index == 1, dbeta, 0.0)
        )
        turned = jnp.transpose(packed)[:8]
        flow_rows = jnp.sum(flow, axis=0, keepdims=True)
        kind = row_index[:8]
        dtotal = jnp.where(kind == 0, turned - flow_rows, 0.0)
        dlog = spread_sum(dtotal, lower.astype(jnp.float32))[0:1]
        chunk = (pl.num_programs(0) - 1 - step) * BATCH + i
        pair = jnp.transpose(head_rows(raw_refs, place_ref, chunk, 4))[:8]
        inside = pair[0:1] + params_ref[1, 0]
        rate = -jnp.exp(params_ref[0, 0] + jnp.zeros((1, CHUNK), jnp.float32))
        dinside = dlog * rate * jax.nn.sigmoid(inside)
        beta_row = rows[1:2]
        dbeta_raw = turned[1:2] * beta_row * (1.0 - beta_row)
        drate = dlog * rate * jax.nn.softplus(inside)
        dparams_ref[...] += jnp.where(kind == 0, drate, jnp.where(kind == 1, dinside, 0.0))
        ddecay = jnp.where(kind == 0, dinside, jnp.where(kind == 1, dbeta_raw, 0.0))
        put_rows(draw_ref, place_ref, chunk, slice(3 * CHUNK, 4 * CHUNK), dgate_ref[i])
        put_rows(
            draw_ref, place_ref, chunk, slice(4 * CHUNK, 5 * CHUNK), chunk_cols(ddecay).astype(jnp.bfloat16)
        )

        d_scaled_q = dqueries * CHUNK ** (-0.5)
        gates = [jax.nn.sigmoid(piece[1]) for piece in pieces]
        unit_q, unit_k = pieces[0][1] * gates[0] * q_scale, pieces[1][1] * gates[1] * k_scale
        dact = [
            q_scale * (d_scaled_q - unit_q * lane_sum(d_scaled_q * unit_q)),
            k_scale * (dkeys - unit_k * lane_sum(dkeys * unit_k)),
            dvalues,
        ]
        for part in range(3):
            rows_by_offset, conv = pieces[part]
            gate = gates[part]
            dconv = dact[part] * (gate * (1.0 + conv * (1.0 - gate)))
            taps = taps_ref[part]
            after = next_ref[part]
            draw = dconv * taps[3:4]
            for offset in range(1, 4):
                kept = jnp.concatenate([dconv * keeps[offset - 1], after], axis=0)
                draw = draw + pltpu.roll(kept, CHUNK + 8 - offset, 0)[:CHUNK] * taps[3 - offset : 4 - offset]
            lanes = slice(part * CHUNK, (part + 1) * CHUNK)
            put_rows(draw_ref, place_ref, chunk, lanes, draw.astype(jnp.bfloat16))
            for offset in range(4):
                dtaps_ref[part, 3 - offset : 4 - offset] += jnp.sum(
                    dconv * rows_by_offset[offset], axis=0, keepdims=True
                )
            next_ref[part] = dconv[:8] * (1.0 - starts[0])

    @pl.when(step == pl.num_programs(0) - 1)
    def _():
        draw0_ref[...] = draw_ref[0]
        draw1_ref[...] = draw_ref[1]


def back(place, starts, params, raw0, raw1, rows, taps, inverse, kkf, inner, joined, states, dstates, dcore, dgate):
    chunks = rows.shape[0]
    square = (BATCH, CHUNK, CHUNK)
    wide = (BATCH, CHUNK, 2 * CHUNK)
    turned = partial(per_batch, turned=True, steps=chunks // BATCH)
    draw = (2,) + raw0.shape
    return pl.pallas_call(
        back_kernel,
        grid_spec=pltpu.PrefetchScalarGridSpec(
            num_scalar_prefetch=3,
            grid=(chunks // BATCH,),
            in_specs=[whole(raw0.shape), whole(raw1.shape), turned((BATCH, 8, CHUNK)), whole(taps.shape),
                      turned(square), turned(square), turned(square), turned(wide), turned(square),
                      turned(square), turned(square), turned(square)],
            out_specs=[whole(raw0.shape), whole(raw0.shape), whole((3, 4, CHUNK)), whole((8, CHUNK))],
            scratch_shapes=[pltpu.VMEM((3, 8, CHUNK), jnp.float32), pltpu.VMEM(draw, jnp.bfloat16)],
        ),
        out_shape=[shaped(raw0.shape, jnp.bfloat16)] * 2 + [shaped((3, 4, CHUNK)), shaped((8, CHUNK))],
        compiler_params=pltpu.CompilerParams(vmem_limit_bytes=VMEM_MAX),
        cost_estimate=spends(24),
        name="back",
    )(place, starts, params, raw0, raw1, rows, taps, inverse, kkf, inner, joined, states, dstates, dcore, dgate)


def document_starts(doc_lengths, block_count):
    bounds = jnp.cumsum(doc_lengths)[:-1]
    blocks = jnp.arange(block_count, dtype=jnp.int32)
    opens = jnp.any(blocks[:, None] == bounds[None, :], axis=1) | (blocks == 0)
    return opens.astype(jnp.int32)


def mixer_forward(place, prepared, raw0, raw1, out_gain):
    rows, inverse, kkf, inner, joined, m, mt, b, r, pu = prepared
    states, core, mixed = scan_states(place, m, b, r, pu, raw0, raw1, out_gain)
    return mixed, (rows, inverse, kkf, inner, joined, mt, r, states, core)


def mixer_backward_scan(place, raw0, raw1, out_gain, kept, dmixed):
    mt, r, core = kept[5], kept[6], kept[8]
    return back_scan(place, mt, r, core, raw0, raw1, dmixed, out_gain)


def mixer_backward(place, starts, params, raw0, raw1, taps, kept, dstates, dcore, dgate):
    rows, inverse, kkf, inner, joined, _, _, states, _ = kept
    return back(
        place, starts, params, raw0, raw1, rows, taps, inverse, kkf, inner, joined, states, dstates, dcore, dgate
    )


from jax.sharding import PartitionSpec as P

LANES = 128
HALF = 384
GROUP = 256
SIDE = 64


def exchange_perm(count, shifted, sizes):
    pairs = []
    for target in range(count):
        source, scale, rest = 0, 1, target
        for size, offset in zip(reversed(sizes), reversed(shifted)):
            source += (rest % size + offset) % size * scale
            rest //= size
            scale *= size
        pairs.append((source, target))
    return pairs


def from_head(value, dz=0, dx=0, dc=0):
    return lax.ppermute(value, "head", exchange_perm(16, (dz, dx, dc), (4, 2, 2)))


def from_dp(value, dy=0, dx=0):
    return lax.ppermute(value, "dp", exchange_perm(8, (dy, dx), (4, 2)))


def after(value, *earlier):
    return lax.optimization_barrier((value,) + earlier)[0]


def gather_turn(value, cut, beside=()):
    first, second = value[:cut], value[cut:]
    arrived = [take_zx(first, 0, 1)] + [take_zx(second, k, 0) for k in (1, 2, 3)]
    arrived = lax.optimization_barrier(tuple(arrived) + tuple(beside))
    pair = jnp.concatenate([first, arrived[0]], axis=0)
    column = jnp.concatenate([second, *arrived[1:4]], axis=0)
    return lax.optimization_barrier((pair, column))


def gather_end(pair, column):
    return [pair] + [take_zx(pair, k, 0) for k in (1, 2, 3)], [column, take_zx(column, 0, 1)]


def take_zx(value, ring, side):
    return from_head(value, dz=ring, dx=side)


def take_yx(value, ring, side):
    return from_dp(value, dy=ring, dx=side)


def wide(value):
    return value.astype(jnp.float32)


def narrow(value):
    return value.astype(jnp.bfloat16)


def sum_rows(pieces, rows):
    total = wide(pieces[0][rows])
    for piece in pieces[1:]:
        total = total + wide(piece[rows])
    return total


def reduce_arrivals(rounds, far, beside=()):
    arrived = [take_zx(rounds[k - 1], -k, 0) for k in (1, 2, 3)] + [take_zx(far, 0, 1)]
    return lax.optimization_barrier(tuple(arrived) + tuple(beside))[:4], arrived[0]


def turn_sum_kernel(*refs):
    rounds, sides, outs = refs[:4], refs[4:6], refs[6:]
    cut = rounds[0].shape[0] // 2
    early, late = slice(0, cut), slice(cut, None)
    total = wide(rounds[0][...])
    for ref in rounds[1:]:
        total = total + wide(ref[...])
    outs[0][...] = total[early]
    outs[1][...] = narrow(total[late])
    total = wide(sides[0][...]) + wide(sides[1][...])
    rest = total.shape[0] // 4
    outs[2][...] = total[:rest]
    for k in (1, 2, 3):
        outs[2 + k][...] = narrow(total[rest * k : rest * (k + 1)])


def reduce_parts(first, near, arrived):
    width = first.shape[1]
    cut, rest = (first.shape[0] // 2, width), (near.shape[0] // 4, width)
    outs = [shaped(cut), shaped(cut, jnp.bfloat16), shaped(rest)] + [shaped(rest, jnp.bfloat16)] * 3
    return whole_call(turn_sum_kernel, outs, "turn_sum", (), first, *arrived[:3], near, arrived[3])


def small_kernel(gain1_ref, gain2_ref, out_gain_ref, params_ref, taps_ref, out_grad_ref, sent_ref, rows_ref):
    for row in range(8):
        for half in range(2):
            lanes = slice(half * LANES, (half + 1) * LANES)
            place = 2 * row + half
            rows_ref[place : place + 1] = gain1_ref[row, 0:1, lanes]
            rows_ref[16 + place : 17 + place] = gain2_ref[:, place * LANES : (place + 1) * LANES]
    rows_ref[32:40] = out_gain_ref[...]
    rows_ref[40:48] = params_ref[...]
    for part in range(3):
        rows_ref[48 + 4 * part : 52 + 4 * part] = taps_ref[part]
    rows_ref[60:] = jnp.zeros_like(rows_ref[60:])
    small = rows_ref[...]
    high, rest = split(small)
    low = narrow(small - wide(high) - wide(rest))
    pieces = jnp.concatenate([high, rest, low], axis=0)
    for target in range(8):
        sent_ref[target, :GROUP] = out_grad_ref[target]
        sent_ref[target, GROUP:] = pieces


def side_sum_kernel(near_ref, crossed_ref, *out_refs):
    for k, out_ref in enumerate(out_refs):
        for half in range(2):
            rows = slice(SIDE * (4 * half + k), SIDE * (4 * half + k + 1))
            total = wide(near_ref[rows]) + wide(crossed_ref[rows])
            out_ref[SIDE * half : SIDE * (half + 1)] = total if k == 0 else narrow(total)


def ring_sum_kernel(over_ref, arrived_ref, kept_ref, sent_ref):
    half = kept_ref.shape[0]
    for target, side in ((kept_ref, over_ref[0]), (sent_ref, 1 - over_ref[0])):
        rows = pl.ds(pl.multiple_of(side * half, 16), half)
        total = wide(arrived_ref[0, rows])
        for source in (1, 2, 3):
            total = total + wide(arrived_ref[source, rows])
        target[...] = total.astype(target.dtype)


def reduce_end(parts):
    return (parts[0], take_zx(parts[1], 0, 1), parts[2]) + tuple(
        take_zx(parts[2 + k], -k, 0) for k in (1, 2, 3)
    )


RINGS = [[0, 2, 4, 6], [1, 3, 5, 7]]


def pair_kernel(over_ref, value_ref, mate_ref, *out_refs):
    rows, start = value_ref.shape[0], 0
    for out_ref in out_refs:
        lanes = slice(start, start + out_ref.shape[1])
        start = lanes.stop
        for source, place in ((value_ref, over_ref[0]), (mate_ref, 1 - over_ref[0])):
            out_ref[pl.ds(pl.multiple_of(place * rows, 16), rows)] = source[:, lanes]


def ordered_pair(value, mate):
    over = (lax.axis_index("dp") % 2)[None].astype(jnp.int32)
    outs = [shaped((2 * value.shape[0], columns), value.dtype) for columns in (2 * HALF, HALF)]
    return whole_call(pair_kernel, outs, "ordered_pair", (over,), value, mate)


def ordered_join_kernel(up_ref, *refs):
    sources, target, sems = refs[:4], refs[4], refs[5]
    rows = sources[0].shape[0]
    copies = []
    for k, ref in enumerate(sources):
        place = lax.rem(up_ref[0] + k, 4)
        copies.append(
            pltpu.make_async_copy(ref, target.at[pl.ds(pl.multiple_of(place * rows, 16), rows)], sems.at[k])
        )
        copies[-1].start()
    for copy in copies:
        copy.wait()


def ordered_join(pieces):
    anywhere = pl.BlockSpec(memory_space=pl.ANY)
    rows, columns = pieces[0].shape
    return pl.pallas_call(
        ordered_join_kernel,
        grid_spec=pltpu.PrefetchScalarGridSpec(
            num_scalar_prefetch=1,
            grid=(1,),
            in_specs=[anywhere] * 4,
            out_specs=whole((4 * rows, columns)),
            scratch_shapes=[pltpu.SemaphoreType.DMA((4,))],
        ),
        out_shape=shaped((4 * rows, columns), pieces[0].dtype),
        compiler_params=pltpu.CompilerParams(vmem_limit_bytes=VMEM_MAX),
        cost_estimate=spends(4),
        name="ordered_join",
    )((lax.axis_index("dp") // 2)[None].astype(jnp.int32), *pieces)


def spread_kernel(over_ref, *refs):
    over, out_ref = over_ref[0], refs[-1]
    count = (len(refs) - 1) // 2
    for place in range(count):
        lanes = slice(place * HALF, (place + 1) * HALF)
        out_ref[0, over, :, lanes] = refs[place][...]
        out_ref[0, 1 - over, :, lanes] = refs[count + place][...]


def spread_pair(value, mate):
    rows, columns = value.shape
    count = columns // HALF
    blocks = [held((rows, HALF), lambda *_, place=place: (0, place)) for place in range(count)]
    return pl.pallas_call(
        spread_kernel,
        grid_spec=pltpu.PrefetchScalarGridSpec(
            num_scalar_prefetch=1,
            grid=(4,),
            in_specs=blocks * 2,
            out_specs=pl.BlockSpec((1, 2, rows, columns), lambda turn, *_: (turn, 0, 0, 0)),
        ),
        out_shape=shaped((4, 2, rows, columns), value.dtype),
        compiler_params=pltpu.CompilerParams(vmem_limit_bytes=VMEM_MAX),
        cost_estimate=spends(3),
        name="spread_pair",
    )((lax.axis_index("dp") % 2)[None].astype(jnp.int32), *[value] * count, *[mate] * count)


def round_ring(spread):
    everything = lax.all_to_all(spread, "dp", 0, 0, tiled=False, axis_index_groups=RINGS)
    return everything.reshape(8 * spread.shape[2], spread.shape[3])


def ring_parts(arrived):
    over = (lax.axis_index("dp") % 2)[None].astype(jnp.int32)
    half = (arrived.shape[1] // 2, arrived.shape[2])
    return whole_call(ring_sum_kernel, [shaped(half), shaped(half, jnp.bfloat16)], "ring_sum", (over,), arrived)


def exchange_ring(value):
    return lax.all_to_all(value, "dp", 0, 0, tiled=False, axis_index_groups=RINGS)


def sum_all(value, axis, count):
    spread = jnp.broadcast_to(value, (count,) + value.shape)
    return jnp.sum(lax.all_to_all(spread, axis, 0, 0, tiled=False), axis=0)


def whole_call(kernel, out_shape, name, scalars, *arrays, scratch=()):
    outs = out_shape if isinstance(out_shape, (list, tuple)) else [out_shape]
    return pl.pallas_call(
        kernel,
        grid_spec=pltpu.PrefetchScalarGridSpec(
            num_scalar_prefetch=len(scalars),
            grid=(1,),
            in_specs=[whole(array.shape) for array in arrays],
            out_specs=[whole(out.shape) for out in outs],
            scratch_shapes=list(scratch),
        ),
        out_shape=list(outs),
        compiler_params=pltpu.CompilerParams(vmem_limit_bytes=VMEM_MAX),
        cost_estimate=spends(3),
        name=name,
    )(*scalars, *arrays)


def rms_parts(values):
    scale = lax.rsqrt(jnp.mean(values * values, axis=-1, keepdims=True) + 1e-05)
    return scale, values * scale


def rms_back(grad, gain, scale, unit):
    inner = grad * gain
    return scale * (inner - unit * jnp.mean(inner * unit, axis=-1, keepdims=True))


def enter_kernel(tokens_ref, gain_ref, normed_ref):
    _, unit = rms_parts(wide(tokens_ref[...]))
    normed_ref[...] = narrow(unit * gain_ref[...])


def project_kernel(own_ref, other_ref, weights_ref, own_out_ref, other_out_ref):
    step = pl.program_id(0)
    half = pl.num_programs(0) // 2

    @pl.when(step < half)
    def _():
        own_out_ref[...] = plain_product(own_ref[...], weights_ref[...])

    @pl.when(step >= half)
    def _():
        other_out_ref[...] = plain_product(other_ref[...], weights_ref[...])


def project(own, other, weights, columns):
    count, width = own.shape
    step = 512
    half = count // step

    def early(size):
        return pl.BlockSpec((step, size), lambda i: (jnp.minimum(i, half - 1), 0))

    def late(size):
        return pl.BlockSpec((step, size), lambda i: (jnp.maximum(i - half, 0), 0))

    return pl.pallas_call(
        project_kernel,
        grid=(2 * half,),
        in_specs=[early(width), late(width), held((width, columns))],
        out_specs=[early(columns), late(columns)],
        out_shape=[shaped((count, columns))] * 2,
        compiler_params=pltpu.CompilerParams(vmem_limit_bytes=VMEM_MAX),
        cost_estimate=spends(5),
        name="project",
    )(own, other, weights)


def unproject_kernel(own_ref, far_ref, weights_ref, far_weights_ref, *piece_refs):
    step = pl.program_id(0)
    total = against(own_rows(own_ref, step), weights_ref[...]) + against(
        own_rows(far_ref, step), far_weights_ref[...]
    )
    put_pieces(narrow(total), piece_refs, step)


def unproject(own, far, weights, far_weights, piece_shapes):
    used = held((weights.shape[0], own.shape[1]))
    return pl.pallas_call(
        unproject_kernel,
        grid=(4,),
        in_specs=[held(own.shape), held(far.shape), used, used],
        out_specs=[whole(shape) for shape in piece_shapes],
        out_shape=[shaped(shape, jnp.bfloat16) for shape in piece_shapes],
        compiler_params=pltpu.CompilerParams(vmem_limit_bytes=VMEM_MAX),
        cost_estimate=spends(8),
        name="unproject",
    )(own, far, weights, far_weights)


def feed_grad_kernel(*refs):
    own_ref, far_ref = refs[8:]
    gate_up, down = 0.0, 0.0
    for normed_ref, cot_ref, dpre_ref, hidden_ref in (refs[:4], refs[4:8]):
        gate_up = gate_up + over_rows(normed_ref[...], dpre_ref[...])
        down = down + over_rows(cot_ref[...], hidden_ref[...])
    gate_up, down = narrow(gate_up), narrow(down)
    own_ref[:, : 2 * HALF] = gate_up[:, : 2 * HALF]
    far_ref[:, : 2 * HALF] = gate_up[:, 2 * HALF :]
    own_ref[:, 2 * HALF :] = down[:, :HALF]
    far_ref[:, 2 * HALF :] = down[:, HALF:]


def feed_grads(*parts):
    arrays, specs = [], []
    width = parts[0][2].shape[1]
    for hidden, dpre, normed, cot in parts:
        rows = pl.BlockSpec((normed.shape[0], GROUP), lambda i: (0, i))
        arrays += [normed, cot, dpre, hidden]
        specs += [rows, rows, held(dpre.shape), held(hidden.shape)]
    out = pl.BlockSpec((GROUP, 3 * HALF), lambda i: (i, 0))
    return pl.pallas_call(
        feed_grad_kernel,
        grid=(width // GROUP,),
        in_specs=specs,
        out_specs=[out, out],
        out_shape=[shaped((width, 3 * HALF), jnp.bfloat16)] * 2,
        compiler_params=pltpu.CompilerParams(vmem_limit_bytes=VMEM_MAX),
        cost_estimate=spends(12),
        name="feed_grads",
    )(*arrays)


def in_grad_kernel(own_ref, other_ref, draw0_ref, draw1_ref, weights_ref, gain_ref, out_ref, part_ref):
    grad = narrow(over_rows(own_ref[...], draw0_ref[...]) + over_rows(other_ref[...], draw1_ref[...]))
    out_ref[0] = grad
    product = wide(grad) * wide(weights_ref[...])
    lanes = product[:, :LANES]
    for start in range(LANES, product.shape[1], LANES):
        lanes = lanes + product[:, start : start + LANES]
    part = jnp.sum(jnp.transpose(lanes), axis=0, keepdims=True) / gain_ref[...]
    part_ref[0] = jnp.broadcast_to(part, part_ref.shape[1:])


def in_grads(own, other, draw0, draw1, weights, gain):
    count, width = own.shape
    used = draw0.shape[1]
    rows = pl.BlockSpec((count, GROUP), lambda i: (0, i))
    grad, part = pl.pallas_call(
        in_grad_kernel,
        grid=(width // GROUP,),
        in_specs=[rows, rows, held(draw0.shape), held(draw1.shape),
                  pl.BlockSpec((GROUP, used), lambda i: (i, 0)), pl.BlockSpec((1, GROUP), lambda i: (0, i))],
        out_specs=[pl.BlockSpec((1, GROUP, used), lambda i: (i // 2, i % 2, 0)),
                   pl.BlockSpec((1, 8, GROUP), lambda i: (i, 0, 0))],
        out_shape=[shaped((4, 2 * GROUP, used), jnp.bfloat16), shaped((width // GROUP, 8, GROUP))],
        compiler_params=pltpu.CompilerParams(vmem_limit_bytes=VMEM_MAX),
        cost_estimate=spends(8),
        name="in_grads",
    )(own, other, draw0, draw1, weights, gain)
    return grad, part


def out_grad_kernel(rows_ref, mixed_ref, out_ref):
    out_ref[0] = narrow(over_rows(rows_ref[...], mixed_ref[...]))


def out_grads(rows, mixed):
    count, width = rows.shape
    return pl.pallas_call(
        out_grad_kernel,
        grid=(width // GROUP,),
        in_specs=[pl.BlockSpec((count, GROUP), lambda i: (0, i)), held(mixed.shape)],
        out_specs=pl.BlockSpec((1, GROUP, mixed.shape[1]), lambda i: (i, 0, 0)),
        out_shape=shaped((width // GROUP, GROUP, mixed.shape[1]), jnp.bfloat16),
        compiler_params=pltpu.CompilerParams(vmem_limit_bytes=VMEM_MAX),
        cost_estimate=spends(6),
        name="out_grads",
    )(rows, mixed)


def own_rows(ref, step):
    first = pl.ds(pl.multiple_of(step * 2 * ROWS_A, 16), 2 * ROWS_A)
    near = pl.ds(pl.multiple_of(8 * ROWS_A + step * ROWS_B, 16), ROWS_B)
    far = pl.ds(pl.multiple_of(8 * ROWS_A + 4 * ROWS_B + step * ROWS_B, 16), ROWS_B)
    return jnp.concatenate([ref[first], ref[near], ref[far]], axis=0)


def put_pieces(total, piece_refs, step):
    side = pl.ds(pl.multiple_of(step * ROWS_B, 16), ROWS_B)
    for k in range(4):

        @pl.when(step == k)
        def _(k=k):
            piece_refs[k][...] = total[: 2 * ROWS_A]

    piece_refs[4][side] = total[2 * ROWS_A : 2 * ROWS_A + ROWS_B]
    piece_refs[5][side] = total[2 * ROWS_A + ROWS_B :]


def attn_kernel(heads_ref, mixed_ref, *refs):
    weight_refs, (rows_ref, gain_ref, resid_ref, normed_ref, total_ref) = refs[:4], refs[4:]
    step = pl.program_id(0)

    @pl.when(step == 0)
    def _():
        total_ref[...] = wide(rows_ref[...])

    mixed = jnp.concatenate([mixed_ref[heads_ref[i % 2, 2 * step + i // 2]] for i in range(4)], axis=1)
    total_ref[...] += against(mixed, jnp.concatenate([ref[0] for ref in weight_refs], axis=1))

    @pl.when(step == pl.num_programs(0) - 1)
    def _():
        resid = total_ref[...]
        resid_ref[...] = resid
        _, unit = rms_parts(resid)
        normed_ref[...] = narrow(unit * gain_ref[...])


def out_weight_specs(out_heads):
    shape = (1,) + out_heads.shape[1:]
    return [
        pl.BlockSpec(shape, lambda step, heads_ref, i=i: (heads_ref[i % 2, 2 * step + i // 2], 0, 0))
        for i in range(4)
    ]


def attend(heads, received, out_heads, rows, gain):
    shape = rows.shape
    return pl.pallas_call(
        attn_kernel,
        grid_spec=pltpu.PrefetchScalarGridSpec(
            num_scalar_prefetch=1,
            grid=(4,),
            in_specs=[whole(received.shape)] + out_weight_specs(out_heads) + [whole(shape), whole(gain.shape)],
            out_specs=[whole(shape), whole(shape)],
            scratch_shapes=[pltpu.VMEM(shape, jnp.float32)],
        ),
        out_shape=[shaped(shape), shaped(shape, jnp.bfloat16)],
        compiler_params=pltpu.CompilerParams(vmem_limit_bytes=VMEM_MAX),
        cost_estimate=spends(10),
        name="attend",
    )(heads, received, *[out_heads] * 4, rows, gain)


def total_of(refs):
    first = refs[0][...] + wide(refs[1][...])
    second = refs[2][...] + wide(refs[3][...]) + wide(refs[4][...]) + wide(refs[5][...])
    return jnp.concatenate([first, second], axis=0)


def middle_kernel(heads_ref, *refs):
    pieces, (resid_ref, cot_ref, gain_ref), weight_refs = refs[:6], refs[6:9], refs[9:13]
    dresid_ref, dattn_ref, dgain_ref, dmixed_ref = refs[13:]
    step = pl.program_id(0)

    @pl.when(step == 0)
    def _():
        grad = total_of(pieces)
        scale, unit = rms_parts(resid_ref[...])
        dgain_ref[...] = jnp.sum(grad * unit, axis=0, keepdims=True)
        dresid = wide(cot_ref[...]) + rms_back(grad, gain_ref[...], scale, unit)
        dresid_ref[...] = dresid
        dattn_ref[...] = narrow(dresid)

    weights = jnp.concatenate([ref[0] for ref in weight_refs], axis=1)
    total = narrow(plain_product(dattn_ref[...], weights))
    for i in range(4):
        dmixed_ref[heads_ref[i % 2, 2 * step + i // 2]] = total[:, i * LANES : (i + 1) * LANES]


def middle(heads, pieces, resid, cot, gain, out_heads):
    shape = resid.shape
    mixed_shape = (16, shape[0], LANES)
    return pl.pallas_call(
        middle_kernel,
        grid_spec=pltpu.PrefetchScalarGridSpec(
            num_scalar_prefetch=1,
            grid=(4,),
            in_specs=[whole(piece.shape) for piece in pieces]
            + [whole(shape), whole(shape), whole(gain.shape)]
            + out_weight_specs(out_heads),
            out_specs=[whole(shape), whole(shape), whole((1, shape[1])), whole(mixed_shape)],
        ),
        out_shape=[shaped(shape), shaped(shape, jnp.bfloat16), shaped((1, shape[1])),
                   shaped(mixed_shape, jnp.bfloat16)],
        compiler_params=pltpu.CompilerParams(vmem_limit_bytes=VMEM_MAX),
        cost_estimate=spends(10),
        name="middle",
    )(heads, *pieces, resid, cot, gain, *[out_heads] * 4)


def leave_kernel(*refs):
    total = refs[0][...] + refs[4][...]
    for ref in refs[1:4]:
        total = total + wide(ref[...])
    refs[5][...] = narrow(total)


def finish_kernel(*refs):
    pieces, (rows_ref, dresid_ref, gain_ref, out_ref) = refs[:6], refs[6:]
    scale, unit = rms_parts(wide(rows_ref[...]))
    out_ref[...] = dresid_ref[...] + rms_back(total_of(pieces), gain_ref[...], scale, unit)


def feed_kernel(halves, count, joins, heads_ref, *refs):
    normed_refs, refs = refs[:count], refs[count:]
    cot_refs, refs = refs[: len(halves)], refs[len(halves) :]
    weight_refs, refs = refs[:4], refs[4:]
    earlier_refs, refs = refs[: 2 * joins], refs[2 * joins :]
    fed_refs, dnormed_refs, refs = refs[:2], refs[2 : 2 + count], refs[2 + count :]
    hidden_ref, dpre_ref, normed_out_ref, cot_out_ref, normed_ref, cot_ref, out_ref, grad_ref = refs
    step, last = pl.program_id(0), pl.num_programs(0) - 1
    size = hidden_ref.shape[0]

    @pl.when(step == 0)
    def _():
        start = 0
        for ref in normed_refs:
            normed_ref[start : start + ref.shape[0]] = ref[...]
            start += ref.shape[0]
        for place, ref in enumerate(cot_refs):
            cot_ref[SIDE * place : SIDE * (place + 1)] = ref[...]

    rows = pl.ds(pl.multiple_of(step * size, 16), size)
    normed, cot = normed_ref[rows], cot_ref[rows]
    normed_out_ref[...] = normed
    cot_out_ref[...] = cot
    out, dnormed = 0.0, 0.0
    for half in range(2):
        gu_ref, down_ref = weight_refs[2 * half], weight_refs[2 * half + 1]
        pre = plain_product(normed, gu_ref[...])
        gate, up = pre[:, :HALF], pre[:, HALF:]
        dhidden = plain_product(cot, down_ref[...])
        sigmoid = jax.nn.sigmoid(gate)
        act = gate * sigmoid
        hidden = narrow(act * up)
        dgate = narrow(dhidden * up * sigmoid * (1.0 + gate * (1.0 - sigmoid)))
        dpre = jnp.concatenate([dgate, narrow(dhidden * act)], axis=1)
        hidden_ref[:, half * HALF : (half + 1) * HALF] = hidden
        dpre_ref[:, 2 * half * HALF : 2 * (half + 1) * HALF] = dpre
        out = out + against(hidden, down_ref[...])
        dnormed = dnormed + against(dpre, gu_ref[...])
    out_ref[rows] = narrow(out)
    grad_ref[rows] = narrow(dnormed)

    @pl.when(step == last)
    def _():
        start = 0
        for ref in dnormed_refs:
            ref[...] = grad_ref[start : start + ref.shape[0]]
            start += ref.shape[0]
        if joins:
            near_ref, far_ref = fed_refs
            for k in range(4):
                first = earlier_refs[0] if k == 0 else out_ref.at[2 * SIDE * (k - 1) : 2 * SIDE * k]
                near_ref[SIDE * k : SIDE * (k + 1)] = first[:SIDE]
                far_ref[SIDE * k : SIDE * (k + 1)] = first[SIDE:]
            near_ref[4 * SIDE :] = earlier_refs[1][...]
            far_ref[4 * SIDE :] = out_ref[6 * SIDE :]
        else:
            fed_refs[0][...] = out_ref[: 2 * SIDE]
            fed_refs[1][...] = out_ref[2 * SIDE :]


def held(shape, place=None):
    place = place or (lambda *_: (0,) * len(shape))
    return pl.BlockSpec(shape, place, pipeline_mode=pl.Buffered(1))


def feed(heads, pieces, halves, cot, own, other, steps, earlier=()):
    width = cot.shape[1]
    shapes = [piece.shape for piece in pieces]
    count = sum(shape[0] for shape in shapes)
    size = count // steps
    gate_up, down = held((width, 2 * HALF)), held((width, HALF))

    def half_block(slot, half):
        return held((SIDE, width), lambda i, heads_ref: (2 * heads_ref[0, slot] + half, 0))

    fed_shapes = [(8 * SIDE, width)] * 2 if earlier else shapes
    row_widths = (2 * HALF, 4 * HALF, width, width)
    outs = pl.pallas_call(
        partial(feed_kernel, tuple(halves), len(pieces), bool(earlier)),
        grid_spec=pltpu.PrefetchScalarGridSpec(
            num_scalar_prefetch=1,
            grid=(steps,),
            in_specs=[held(shape) for shape in shapes]
            + [half_block(*half) for half in halves]
            + [gate_up, down, gate_up, down]
            + [held(piece.shape) for piece in earlier],
            out_specs=[whole(shape) for shape in fed_shapes + shapes]
            + [pl.BlockSpec((size, part), lambda i, *_: (i, 0)) for part in row_widths],
            scratch_shapes=[pltpu.VMEM((count, width), jnp.bfloat16)] * 4,
        ),
        out_shape=[shaped(shape, jnp.bfloat16) for shape in fed_shapes + shapes]
        + [shaped((count, part), jnp.bfloat16) for part in row_widths],
        compiler_params=pltpu.CompilerParams(vmem_limit_bytes=VMEM_MAX),
        cost_estimate=spends(28),
        name="feed",
    )(heads, *pieces, *[cot] * len(halves), *own, *other, *earlier)
    feds = len(fed_shapes)
    return outs[:feds], outs[feds : feds + len(shapes)], outs[feds + len(shapes) :]


def join_kernel(*refs):
    sources, target, sems = refs[:-2], refs[-2], refs[-1]
    copies, start = [], 0
    for place, ref in enumerate(sources):
        copies.append(pltpu.make_async_copy(ref, target.at[pl.ds(start, ref.shape[0])], sems.at[place]))
        copies[-1].start()
        start += ref.shape[0]
    for copy in copies:
        copy.wait()


def join(pieces):
    anywhere = pl.BlockSpec(memory_space=pl.ANY)
    rows = sum(piece.shape[0] for piece in pieces)
    return pl.pallas_call(
        join_kernel,
        in_specs=[anywhere] * len(pieces),
        out_specs=pl.BlockSpec(memory_space=pltpu.VMEM),
        out_shape=shaped((rows, pieces[0].shape[1]), pieces[0].dtype),
        scratch_shapes=[pltpu.SemaphoreType.DMA((len(pieces),))],
        compiler_params=pltpu.CompilerParams(vmem_limit_bytes=VMEM_MAX),
        cost_estimate=spends(3),
        name="join",
    )(*pieces)


def plain_product(left, right):
    return jnp.dot(left, right, preferred_element_type=jnp.float32)


def against(left, right):
    return lax.dot_general(left, right, (((1,), (1,)), ((), ())), preferred_element_type=jnp.float32)


def over_rows(left, right):
    return lax.dot_general(left, right, (((0,), (0,)), ((), ())), preferred_element_type=jnp.float32)


def tables():
    head = lax.axis_index("head")
    ring, side, core = head // 4, head // 2 % 2, head % 2
    chunk = jnp.arange(16, dtype=jnp.int32)
    dz, dx, dc = (chunk // 4 - ring) % 4, (chunk // 2 + side) % 2, (chunk + core) % 2
    place = jnp.stack([ROWS_A * (2 * dz + dx), 8 * ROWS_A + ROWS_B * (4 * dx + dz), dc]).astype(jnp.int32)
    step = jnp.arange(8, dtype=jnp.int32)
    chip = ((step + ring) % 4) * 2 + (step // 4 + side) % 2
    heads = jnp.stack([2 * chip + core, 2 * chip + 1 - core]).astype(jnp.int32)
    return place, heads


def body(
    tokens,
    cotangent,
    doc_spans,
    norm1_gain,
    q_weight,
    k_weight,
    v_weight,
    gate_out_weight,
    decay_weight,
    conv_weight,
    gate_params,
    out_gain,
    out_weight,
    norm2_gain,
    gate_weight,
    up_weight,
    down_weight,
):
    place, heads = tables()
    starts = document_starts(doc_spans[0], 32)
    out_gain_row = out_gain[None, :]
    gain1_row, gain2_row = norm1_gain[None, :], norm2_gain[None, :]
    rows_shape = tokens.shape
    width = rows_shape[1]

    def pad(weight, columns):
        return jnp.pad(weight, ((0, 0), (0, columns - weight.shape[1])))

    (normed1,) = whole_call(enter_kernel, shaped(rows_shape, jnp.bfloat16), "enter", (), tokens, gain1_row)

    packed = (conv_weight, decay_weight, q_weight, k_weight, v_weight, gate_out_weight, out_weight)
    conv_now, decay_now, *square_now = lax.optimization_barrier(packed + (normed1,))[:7]
    taps_block = jnp.pad(conv_now.reshape(12, 16), ((0, GROUP - 12), (0, 0)))
    side_block = pad(jnp.concatenate([decay_now[:, 0], taps_block], axis=1), LANES)
    pack_one = jnp.concatenate(square_now[:4] + [side_block] + square_now[4:], axis=1)
    wide_now = lax.optimization_barrier((gate_weight, up_weight, down_weight, normed1))[:3]
    pack_two = jnp.concatenate([pad(weight, HALF) for weight in wide_now], axis=1)
    cut, used = pack_one.shape[1], 5 * LANES

    mate_one = take_yx(pack_one, 0, 1)
    pair, column = gather_turn(normed1, ROWS_A, beside=(mate_one, pack_two))
    pair, column, mate_one = lax.optimization_barrier((pair, column, mate_one))
    mate_two = take_yx(after(pack_two, mate_one), 0, 1)
    mine_one = round_ring(spread_pair(pack_one, mate_one))
    rings, columns = gather_end(pair, column)
    rings, columns, mine_one, mate_two = lax.optimization_barrier((rings, columns, mine_one, mate_two))
    pair_gu, pair_down = ordered_pair(pack_two, mate_two)
    normed1_own = join(rings + columns)
    normed1_other = from_head(normed1_own, dc=1)
    raw0, raw1 = project(normed1_own, normed1_other, mine_one, used)
    taps = mine_one.reshape(8, GROUP, cut)[:, :12, 4 * LANES + 2 : 4 * LANES + 18]
    taps = wide(taps.transpose(1, 0, 2).reshape(3, 4, LANES))

    gu_arrived = [take_yx(pair_gu, k, 0) for k in (1, 2, 3)]

    out_heads = lax.all_gather(after(mine_one[:, used:], normed1_own), "head")
    prepared = prepare(place, starts, gate_params, raw0, raw1, taps)
    mixed, kept = mixer_forward(place, prepared, raw0, raw1, out_gain_row)
    mixed, gu_arrived, out_heads, pair_down = lax.optimization_barrier((mixed, gu_arrived, out_heads, pair_down))
    down_arrived = [take_yx(pair_down, k, 0) for k in (1, 2, 3)]
    cot_group = lax.all_gather(after(cotangent, out_heads), "head", axis=0, tiled=True)
    received = lax.all_to_all(mixed, "head", 0, 0, tiled=False)
    resid, normed2 = attend(heads, received, out_heads, tokens, gain2_row)
    gu_arrived, down_arrived = lax.optimization_barrier((gu_arrived, down_arrived, normed2))[:2]
    own_two = (ordered_join([pair_gu, *gu_arrived]), ordered_join([pair_down, *down_arrived]))
    pair, column = gather_turn(normed2, SIDE, beside=own_two)
    other_two = tuple(from_head(after(weights, pair), dc=1) for weights in own_two)
    rings, columns = gather_end(pair, column)
    near_halves = [(0, 0), (4, 0)] + [(k, 1) for k in range(4)]
    far_halves = [half for k in (1, 2, 3) for half in ((k, 0), (4 + k, 0))] + [(4 + k, 1) for k in range(4)]
    fed_early, (dpair, dnear), kept_near = feed(
        heads, [pair, column], near_halves, cot_group, own_two, other_two, 1
    )
    rings, columns, dpair = lax.optimization_barrier((rings, columns, dpair))
    (fed_near, fed_far), (*drings, dfar), kept_far = feed(
        heads, rings[1:] + columns[1:], far_halves, cot_group, own_two, other_two, 2, fed_early
    )

    parts = reduce_parts(dpair, dnear, reduce_arrivals(drings, dfar)[0])
    feed_own, feed_other = feed_grads(kept_near, kept_far)
    parts, feed_own, feed_other = lax.optimization_barrier((parts, feed_own, feed_other))
    feed_grad = narrow(wide(feed_own) + wide(from_head(feed_other, dc=1)))
    dnormed2_pieces = reduce_end(parts)
    resid_then = after(resid, feed_grad)
    dresid, dattn, dgain2, dmixed = middle(heads, dnormed2_pieces, resid_then, cotangent, gain2_row, out_heads)
    dmixed_mine = lax.all_to_all(dmixed, "head", 0, 0, tiled=False)
    dcore, dstates, dgate, dgain_out = mixer_backward_scan(place, raw0, raw1, out_gain_row, kept, dmixed_mine)

    feed_arrived = exchange_ring(after(feed_grad, dmixed_mine).reshape(4, 2 * GROUP, 3 * HALF))
    fed_crossed = take_zx(after(fed_far, dcore), 0, 1)
    dattn_group = lax.all_gather(dattn, "head", axis=0, tiled=True)
    weights_other = from_head(after(mine_one, dmixed), dc=1)

    draw0, draw1, dtaps, dparams = mixer_backward(
        place, starts, gate_params, raw0, raw1, taps, kept, dstates, dcore, dgate
    )
    draw0, draw1, weights_other = lax.optimization_barrier((draw0, draw1, weights_other))
    draw_far = from_head(draw1, dc=1)
    in_grad, gain1_part = in_grads(normed1_own, normed1_other, draw0, draw1, mine_one, gain1_row)
    draw_far = after(draw_far, in_grad)
    dnormed1 = unproject(draw0, draw_far, mine_one, weights_other, [(2 * ROWS_A, width)] * 4 + [(4 * ROWS_B, width)] * 2)
    dnormed1, feed_arrived, dattn_then, in_grad = lax.optimization_barrier(
        (dnormed1, feed_arrived, dattn_group, in_grad)
    )
    in_arrived = exchange_ring(in_grad)
    feed_kept, feed_sent = ring_parts(feed_arrived)
    out_grad = out_grads(dattn_then, mixed.reshape(dattn_group.shape[0], LANES))
    (sent,) = whole_call(
        small_kernel,
        shaped((8, GROUP + 192, LANES), jnp.bfloat16),
        "small",
        (),
        gain1_part,
        dgain2,
        dgain_out,
        dparams,
        dtaps,
        out_grad,
        scratch=[pltpu.VMEM((64, LANES), jnp.float32)],
    )
    half_rows = (2 * SIDE, width)
    in_kept, in_sent = ring_parts(in_arrived)
    arrived, first_arrived = reduce_arrivals(
        dnormed1[1:4], dnormed1[5], beside=(feed_kept, feed_sent, in_kept, in_sent, sent, fed_crossed)
    )
    parts = reduce_parts(dnormed1[0], dnormed1[4], arrived)
    dnormed1_pieces = reduce_end(parts)
    fed_crossed, feed_sent, in_sent = lax.optimization_barrier((fed_crossed, feed_sent, in_sent, parts))[:3]
    fed_sums = whole_call(
        side_sum_kernel, [shaped(half_rows)] + [shaped(half_rows, jnp.bfloat16)] * 3, "side_sum", (), fed_near, fed_crossed
    )
    fed_pieces = [fed_sums[0]] + [take_zx(fed_sums[k], -k, 0) for k in (1, 2, 3)]
    one_total = in_kept + wide(take_yx(in_sent, 0, 1))
    got = lax.all_to_all(after(sent, in_arrived, first_arrived), "dp", 0, 0, tiled=False)
    dnormed1_pieces, got = lax.optimization_barrier((dnormed1_pieces, got))
    out_total = jnp.sum(wide(got[:, :GROUP]), axis=0)
    pieces = wide(got[:, GROUP:]).reshape(8, 3, 64, LANES)
    small = jnp.sum(pieces[:, 0] + pieces[:, 1] + pieces[:, 2], axis=0)
    shared = sum_all(small[:40], "head", 16)
    fed_pieces, shared = lax.optimization_barrier((fed_pieces, shared))
    (block_out,) = whole_call(leave_kernel, shaped(rows_shape, jnp.bfloat16), "leave", (), *fed_pieces, resid)
    feed_got, shared = lax.optimization_barrier((take_yx(feed_sent, 0, 1), shared))
    feed_total = feed_kept + wide(feed_got)

    gain1_total = shared[:16].reshape(-1)
    gain2_total = shared[16:32].reshape(-1)
    out_gain_total = jnp.sum(shared[32:40], axis=0)
    params_total = jnp.sum(small[40:48], axis=1)[:2, None]
    taps_total = lax.dynamic_slice_in_dim(
        small[48:60].reshape(3, 4, LANES), lax.axis_index("dp") * 16, 16, 2
    )
    (tokens_grad,) = whole_call(
        finish_kernel, shaped(rows_shape), "finish", (), *dnormed1_pieces, tokens, dresid, gain1_row
    )
    hidden_units = gate_weight.shape[1]
    return (
        block_out,
        tokens_grad,
        gain1_total,
        one_total[:, :LANES],
        one_total[:, LANES : 2 * LANES],
        one_total[:, 2 * LANES : 3 * LANES],
        one_total[:, 3 * LANES : 4 * LANES],
        one_total[:, 4 * LANES : 4 * LANES + 2][:, None, :],
        taps_total,
        params_total,
        out_gain_total,
        out_total,
        gain2_total,
        feed_total[:, :hidden_units],
        feed_total[:, HALF : HALF + hidden_units],
        feed_total[:, 2 * HALF : 2 * HALF + hidden_units],
    )


def solution(mesh):
    rows, weight = P(("dp", "head"), None), P("dp", "head")
    weight3, taps = P("dp", "head", None), P(None, None, ("head", "dp"))
    params = P(None, "head")
    in_specs = (
        rows, rows, P("dp", None), P(), weight, weight, weight, weight, weight3, taps, params, P(),
        weight, P(), weight, weight, weight,
    )
    out_specs = (
        rows, rows, P(), weight, weight, weight, weight, weight3, taps, params, P(),
        weight, P(), weight, weight, weight,
    )
    return jax.shard_map(body, mesh=mesh, in_specs=in_specs, out_specs=out_specs, check_vma=False)
```

```python
from functools import partial

import jax
import jax.numpy as jnp
from jax import lax
from jax.experimental import pallas as pl
from jax.experimental.pallas import tpu as pltpu

CHUNK = 128
PREPARE_BATCH = 8
SCAN_BATCH = 4
BACK_BATCH = 2
ROWS_A = 80
ROWS_B = 48
GATE_ALONE = 9
VMEM_MAX = 56 * 1024 * 1024


def spends(microseconds):
    return pl.CostEstimate(flops=int(microseconds * 1e6), bytes_accessed=1 << 10, transcendentals=0)


def split(value):
    high = value.astype(jnp.bfloat16)
    return high, (value - high.astype(jnp.float32)).astype(jnp.bfloat16)


def left_pair(value):
    return jnp.concatenate(split(value), axis=1)


def right_pair(value):
    high, low = split(value)
    wide = jnp.concatenate([high, low], axis=1)
    return jnp.concatenate([wide, wide], axis=0)


def right_pair_t(value):
    high, low = split(value)
    return jnp.concatenate(
        [jnp.concatenate([high, high], axis=1), jnp.concatenate([low, low], axis=1)], axis=0
    )


def fold(wide):
    half = wide.shape[1] // 2
    return wide[:, :half] + wide[:, half:]


def mul_pairs(left, right):
    return fold(jnp.dot(left, right, preferred_element_type=jnp.float32))


def mul(left, right):
    return mul_pairs(left_pair(left), right_pair(right))


def mul_t(left, right):
    return fold(
        lax.dot_general(
            left_pair(left),
            right_pair_t(right),
            (((1,), (1,)), ((), ())),
            preferred_element_type=jnp.float32,
        )
    )


def iotas(rows=CHUNK, cols=CHUNK):
    return (
        lax.broadcasted_iota(jnp.int32, (rows, cols), 0),
        lax.broadcasted_iota(jnp.int32, (rows, cols), 1),
    )


def silu_parts(value):
    gate = jax.nn.sigmoid(value)
    return gate, value * gate


def tap_masks(start_first, start_second, row_index):
    keeps = []
    for offset in range(1, 4):
        first = jnp.where(row_index < offset, 1.0 - start_first, 1.0)
        second = jnp.where(
            (row_index >= CHUNK // 2) & (row_index < CHUNK // 2 + offset), 1.0 - start_second, 1.0
        )
        keeps.append(first * second)
    return keeps


def shifted_rows(current, before, keeps):
    joined = jnp.concatenate([before, current], axis=0)
    return [current] + [
        pltpu.roll(joined, offset, 0)[8:] * keeps[offset - 1] for offset in range(1, 4)
    ]


def conv_rows(rows_by_offset, taps):
    total = rows_by_offset[0] * taps[3:4]
    for offset in range(1, 4):
        total = total + rows_by_offset[offset] * taps[3 - offset : 4 - offset]
    return total


def chunk_cols(rows):
    return jnp.transpose(jnp.concatenate([rows, jnp.zeros((CHUNK - 8, CHUNK), jnp.float32)], axis=0))


def decay_matrix(rows, cols, start_second):
    row_index, col_index = iotas()
    gap = cols[:, 0:1] - rows[0:1, :]
    lower = row_index >= col_index
    cross = (row_index >= CHUNK // 2) & (col_index < CHUNK // 2)
    decay = jnp.where(lower, jnp.exp(jnp.where(lower, gap, 0.0)), 0.0)
    return decay * jnp.where(cross, 1.0 - start_second, 1.0)


def head_rows(raw_refs, place_ref, chunk, part):
    def load(start, count):
        rows = pl.ds(pl.multiple_of(start, 8), count)
        return jnp.where(half == 0, raw_refs[0][rows, lanes], raw_refs[1][rows, lanes])

    lanes = slice(None) if part == GATE_ALONE else slice(part * CHUNK, (part + 1) * CHUNK)
    half = place_ref[2, chunk]
    current = jnp.concatenate(
        [load(place_ref[0, chunk], ROWS_A), load(place_ref[1, chunk], ROWS_B)], axis=0
    )
    if part > 2:
        return current
    earlier = jnp.maximum(chunk - 1, 0)
    half = place_ref[2, earlier]
    return current, load(place_ref[1, earlier] + ROWS_B - 8, 8)


def put_rows(out_ref, place_ref, chunk, lanes, value):
    half = place_ref[2, chunk]
    first = pl.ds(pl.multiple_of(place_ref[0, chunk], 16), ROWS_A)
    second = pl.ds(pl.multiple_of(place_ref[1, chunk], 16), ROWS_B)
    out_ref[half, first, lanes] = value[:ROWS_A]
    out_ref[half, second, lanes] = value[ROWS_A:]


def spread_sum(rows, matrix):
    high, rest = split(rows)
    mid = rest
    low = (rows - high.astype(jnp.float32) - mid.astype(jnp.float32)).astype(jnp.bfloat16)
    parts = jnp.concatenate([high, mid, low, jnp.zeros_like(low)], axis=0)
    wide = jnp.dot(parts, matrix.astype(jnp.bfloat16), preferred_element_type=jnp.float32)
    return wide[:8] + wide[8:16] + wide[16:24]


def gate_rows(decay_cols, starts, params_ref):
    row_index, col_index = iotas()
    pair = jnp.transpose(decay_cols)[:8]
    position = col_index[:8]
    kind = row_index[:8]
    carry, same = 1.0 - starts[0], 1.0 - starts[1]
    second = position >= CHUNK // 2
    beta = jax.nn.sigmoid(pair[1:2])
    inside = pair[0:1] + params_ref[1, 0]
    soft = jax.nn.softplus(inside)
    decay_log = -jnp.exp(params_ref[0, 0] + jnp.zeros((8, CHUNK), jnp.float32)) * soft
    total = spread_sum(decay_log, (row_index <= col_index).astype(jnp.float32))
    end = total[:, CHUNK - 1 :]
    gam = jnp.exp(total) * carry * jnp.where(second, same, 1.0)
    tail = jnp.exp(end - total) * jnp.where(second, 1.0, same)
    span = jnp.exp(end) * carry * same
    rows = jnp.where(kind == 0, total, jnp.where(kind == 1, beta, jnp.where(kind == 2, gam, tail)))
    return jnp.where(kind == 4, span, rows)


def convolved(raw_refs, place_ref, starts, taps_ref, chunk, row_index):
    keeps = tap_masks(starts[0], starts[1], row_index)
    pieces = []
    for part in range(3):
        current, before = head_rows(raw_refs, place_ref, chunk, part)
        rows_by_offset = shifted_rows(current, before, keeps)
        pieces.append((rows_by_offset, conv_rows(rows_by_offset, taps_ref[part])))
    return keeps, pieces


def start_flags(starts_ref, chunk):
    return (
        starts_ref[2 * chunk].astype(jnp.float32),
        starts_ref[2 * chunk + 1].astype(jnp.float32),
    )


def normed_qkv(pieces):
    acts = [piece[1] * jax.nn.sigmoid(piece[1]) for piece in pieces]
    q_scale = lax.rsqrt(jnp.sum(acts[0] * acts[0], axis=-1, keepdims=True) + 1e-06)
    k_scale = lax.rsqrt(jnp.sum(acts[1] * acts[1], axis=-1, keepdims=True) + 1e-06)
    return acts[0] * q_scale * CHUNK ** (-0.5), acts[1] * k_scale, acts[2], q_scale, k_scale


def inverse_lower(stricts):
    row_index, col_index = iotas()
    eye = (row_index == col_index).astype(jnp.float32)
    near = row_index // 16 == col_index // 16
    powers = [jnp.where(near, strict, 0.0) for strict in stricts]
    inverses = [eye - power for power in powers]
    powers = [mul(power, power) for power in powers]
    for step in range(3):
        rights = [right_pair(power) for power in powers]
        if step < 2:
            stacks = [
                left_pair(jnp.concatenate([inverse, power], axis=0))
                for inverse, power in zip(inverses, powers)
            ]
            both = [mul_pairs(stack, right) for stack, right in zip(stacks, rights)]
            inverses = [inverse + pair[:CHUNK] for inverse, pair in zip(inverses, both)]
            powers = [pair[CHUNK:] for pair in both]
        else:
            inverses = [
                inverse + mul_pairs(left_pair(inverse), right)
                for inverse, right in zip(inverses, rights)
            ]
    for width in (16, 32, 64):
        beside = (row_index // (2 * width) == col_index // (2 * width)) & (
            row_index // width != col_index // width
        )
        crossed = [
            mul(inverse, jnp.where(beside, strict, 0.0))
            for inverse, strict in zip(inverses, stricts)
        ]
        inverses = [inverse - mul(cross, inverse) for cross, inverse in zip(crossed, inverses)]
    return inverses


def prepare_kernel(place_ref, starts_ref, params_ref, raw0_ref, raw1_ref, taps_ref,
                   rows_out_ref, inv_ref, kkf_ref, p_ref, uw_ref, m_ref, mt_ref, b_ref, r_ref, pu_ref):
    row_index, col_index = iotas()
    diagonal = (row_index == col_index).astype(jnp.float32)
    stricts, kept = [], []
    for member in range(PREPARE_BATCH):
        chunk = pl.program_id(0) * PREPARE_BATCH + member
        starts = start_flags(starts_ref, chunk)
        raw_refs = (raw0_ref, raw1_ref)
        _, pieces = convolved(raw_refs, place_ref, starts, taps_ref, chunk, row_index)
        queries, keys_in, values_in, _, _ = normed_qkv(pieces)
        rows = gate_rows(head_rows(raw_refs, place_ref, chunk, 4), starts, params_ref)
        rows_out_ref[member] = rows
        cols = chunk_cols(rows)
        decay = decay_matrix(rows, cols, starts[1])
        beta, gam, tail = cols[:, 1:2], cols[:, 2:3], cols[:, 3:4]
        scores = mul_t(jnp.concatenate([keys_in, queries], axis=0), keys_in)
        kkf = jnp.where(row_index > col_index, scores[:CHUNK] * decay, 0.0)
        inner = scores[CHUNK:] * decay
        stricts.append(kkf * beta)
        kkf_ref[member] = kkf
        p_ref[member] = inner
        pair = jnp.concatenate([values_in * beta, keys_in * (beta * gam)], axis=1)
        stack = jnp.concatenate([jnp.transpose(keys_in * tail), inner], axis=0)
        kept.append((pair, stack, diagonal * rows[4:5], queries * gam))
    inverses = inverse_lower(stricts)
    joined = [mul(inverse, pair) for inverse, (pair, _, _, _) in zip(inverses, kept)]
    both = [mul(stack, join) for join, (_, stack, _, _) in zip(joined, kept)]
    for member in range(PREPARE_BATCH):
        _, _, span, faded = kept[member]
        inv_ref[member] = inverses[member]
        uw_ref[member] = joined[member]
        state_map = span - both[member][:CHUNK, CHUNK:]
        m_ref[member] = left_pair(state_map)
        mt_ref[member] = left_pair(jnp.transpose(state_map))
        b_ref[member] = both[member][:CHUNK, :CHUNK]
        r_ref[member] = faded - both[member][CHUNK:, CHUNK:]
        pu_ref[member] = both[member][CHUNK:, :CHUNK]


def whole(shape):
    return pl.BlockSpec(shape, lambda *_: (0,) * len(shape))


def per_batch(shape, turned=False, steps=4):
    def place(step, *_):
        return ((steps - 1 - step) if turned else step,) + (0,) * (len(shape) - 1)

    return pl.BlockSpec(shape, place)


def shaped(shape, dtype=jnp.float32):
    return jax.ShapeDtypeStruct(shape, dtype)


def prepare(place, starts, params, raw0, raw1, taps):
    chunks = place.shape[1]
    square = (PREPARE_BATCH, CHUNK, CHUNK)
    wide = (PREPARE_BATCH, CHUNK, 2 * CHUNK)
    kinds = [((PREPARE_BATCH, 8, CHUNK), jnp.float32), (square, jnp.float32), (square, jnp.float32), (square, jnp.float32),
             (wide, jnp.float32), (wide, jnp.bfloat16), (wide, jnp.bfloat16), (square, jnp.float32),
             (square, jnp.float32), (square, jnp.float32)]
    return pl.pallas_call(
        prepare_kernel,
        grid_spec=pltpu.PrefetchScalarGridSpec(
            num_scalar_prefetch=3,
            grid=(chunks // PREPARE_BATCH,),
            in_specs=[whole(raw0.shape), whole(raw1.shape), whole(taps.shape)],
            out_specs=[per_batch(shape) for shape, _ in kinds],
        ),
        out_shape=[shaped((chunks,) + shape[1:], dtype) for shape, dtype in kinds],
        compiler_params=pltpu.CompilerParams(vmem_limit_bytes=VMEM_MAX),
        cost_estimate=spends(18),
        name="prepare",
    )(place, starts, params, raw0, raw1, taps)


def gate_rows_of(gate_refs, place_ref, chunk):
    return head_rows(gate_refs, place_ref, chunk, GATE_ALONE)


def scan_kernel(place_ref, m_ref, b_ref, r_ref, pu_ref, gate0_ref, gate1_ref, gain_ref,
                state_out_ref, core_ref, mixed_ref, state_ref):
    @pl.when(pl.program_id(0) == 0)
    def _():
        state_ref[...] = jnp.zeros_like(state_ref)

    state = state_ref[...]
    for member in range(SCAN_BATCH):
        chunk = pl.program_id(0) * SCAN_BATCH + member
        state_out_ref[member] = state
        pair = right_pair(state)
        core = mul_pairs(left_pair(r_ref[member]), pair) + pu_ref[member]
        state = mul_pairs(m_ref[member], pair) + b_ref[member]
        _, gate = silu_parts(gate_rows_of((gate0_ref, gate1_ref), place_ref, chunk))
        core_ref[member] = core
        scale = lax.rsqrt(jnp.mean(core * core, axis=-1, keepdims=True) + 1e-05)
        mixed = (core * scale * gain_ref[...] * gate).astype(jnp.bfloat16)
        mixed_ref[member] = mixed
    state_ref[...] = state


def gate_columns(raw):
    return pl.BlockSpec((raw.shape[0], CHUNK), lambda *_: (0, 3))


def scan_states(place, m, b, r, pu, raw0, raw1, gain):
    chunks = m.shape[0]
    square = (SCAN_BATCH, CHUNK, CHUNK)
    wide = (SCAN_BATCH, CHUNK, 2 * CHUNK)
    return pl.pallas_call(
        scan_kernel,
        grid_spec=pltpu.PrefetchScalarGridSpec(
            num_scalar_prefetch=1,
            grid=(chunks // SCAN_BATCH,),
            in_specs=[per_batch(wide), per_batch(square), per_batch(square), per_batch(square),
                      gate_columns(raw0), gate_columns(raw1), whole((1, CHUNK))],
            out_specs=[per_batch(square)] * 3,
            scratch_shapes=[pltpu.VMEM((CHUNK, CHUNK), jnp.float32)],
        ),
        out_shape=[shaped((chunks, CHUNK, CHUNK)), shaped((chunks, CHUNK, CHUNK)),
                   shaped((chunks, CHUNK, CHUNK), jnp.bfloat16)],
        compiler_params=pltpu.CompilerParams(vmem_limit_bytes=VMEM_MAX),
        cost_estimate=spends(7),
        name="scan_states",
    )(place, m, b, r, pu, raw0, raw1, gain)


def back_scan_kernel(place_ref, mt_ref, r_ref, core_ref, gate0_ref, gate1_ref, dmixed_ref, gain_ref,
                     dcore_ref, dstate_out_ref, dgate_ref, dgain_ref, dstate_ref):
    step = pl.program_id(0)

    @pl.when(step == 0)
    def _():
        dstate_ref[...] = jnp.zeros_like(dstate_ref)
        dgain_ref[...] = jnp.zeros_like(dgain_ref)

    gain = gain_ref[...]
    dgain = jnp.zeros((8, CHUNK), jnp.float32)
    terms = []
    for member in reversed(range(SCAN_BATCH)):
        chunk = (pl.num_programs(0) - 1 - step) * SCAN_BATCH + member
        core = core_ref[member]
        raw_gate = gate_rows_of((gate0_ref, gate1_ref), place_ref, chunk)
        dmixed = dmixed_ref[member].astype(jnp.float32)
        gate, gated = silu_parts(raw_gate)
        scale = lax.rsqrt(jnp.mean(core * core, axis=-1, keepdims=True) + 1e-05)
        unit = core * scale
        dscaled = dmixed * gated
        dgate = dmixed * unit * gain * (gate * (1.0 + raw_gate * (1.0 - gate)))
        dgate_ref[member] = dgate.astype(jnp.bfloat16)
        product = dscaled * unit
        dgain = dgain + jnp.sum(product.reshape(CHUNK // 8, 8, CHUNK), axis=0)
        dunit = dscaled * gain
        dcore = scale * (dunit - unit * jnp.mean(dunit * unit, axis=-1, keepdims=True))
        dcore_ref[member] = dcore
        terms.append((member, mul(jnp.transpose(r_ref[member]), dcore)))
    dgain_ref[...] += dgain
    dstate = dstate_ref[...]
    for member, term in terms:
        dstate_out_ref[member] = dstate
        dstate = mul_pairs(mt_ref[member], right_pair(dstate)) + term
    dstate_ref[...] = dstate


def back_scan(place, mt, r, core, raw0, raw1, dmixed, gain):
    chunks = mt.shape[0]
    square = (SCAN_BATCH, CHUNK, CHUNK)
    wide = (SCAN_BATCH, CHUNK, 2 * CHUNK)
    turned = partial(per_batch, turned=True, steps=chunks // SCAN_BATCH)
    return pl.pallas_call(
        back_scan_kernel,
        grid_spec=pltpu.PrefetchScalarGridSpec(
            num_scalar_prefetch=1,
            grid=(chunks // SCAN_BATCH,),
            in_specs=[turned(wide), turned(square), turned(square),
                      gate_columns(raw0), gate_columns(raw1), turned(square), whole((1, CHUNK))],
            out_specs=[turned(square), turned(square), turned(square), whole((8, CHUNK))],
            scratch_shapes=[pltpu.VMEM((CHUNK, CHUNK), jnp.float32)],
        ),
        out_shape=[shaped((chunks, CHUNK, CHUNK)), shaped((chunks, CHUNK, CHUNK)),
                   shaped((chunks, CHUNK, CHUNK), jnp.bfloat16), shaped((8, CHUNK))],
        compiler_params=pltpu.CompilerParams(vmem_limit_bytes=VMEM_MAX),
        cost_estimate=spends(7),
        name="back_scan",
    )(place, mt, r, core, raw0, raw1, dmixed, gain)


def lane_sum(value):
    return jnp.sum(value, axis=1, keepdims=True)


def back_kernel(place_ref, starts_ref, params_ref, raw0_ref, raw1_ref, rows_ref, taps_ref, inv_ref, kkf_ref,
                p_ref, uw_ref, state_ref, dstate_ref, dcore_ref, dgate_ref,
                draw0_ref, draw1_ref, dtaps_ref, dparams_ref, next_ref, draw_ref):
    step = pl.program_id(0)
    row_index, col_index = iotas()
    lower = row_index >= col_index
    strict = row_index > col_index

    @pl.when(step == 0)
    def _():
        next_ref[...] = jnp.zeros_like(next_ref)
        dtaps_ref[...] = jnp.zeros_like(dtaps_ref)
        dparams_ref[...] = jnp.zeros_like(dparams_ref)

    raw_refs = (raw0_ref, raw1_ref)
    members = range(BACK_BATCH)
    setups = []
    for member in members:
        chunk = (pl.num_programs(0) - 1 - step) * BACK_BATCH + member
        starts = start_flags(starts_ref, chunk)
        keeps, pieces = convolved(raw_refs, place_ref, starts, taps_ref, chunk, row_index)
        queries, keys_in, values_in, q_scale, k_scale = normed_qkv(pieces)
        rows = rows_ref[member]
        cols = chunk_cols(rows)
        decay = decay_matrix(rows, cols, starts[1])
        setups.append((starts, keeps, pieces, queries, keys_in, values_in, q_scale, k_scale, rows, cols, decay))
    fresh = [
        uw_ref[i][:, :CHUNK] - mul(uw_ref[i][:, CHUNK:], state_ref[i]) for i in members
    ]
    dfresh = [
        mul(jnp.transpose(p_ref[i]), dcore_ref[i])
        + mul(setups[i][4] * setups[i][9][:, 3:4], dstate_ref[i])
        for i in members
    ]
    through = [
        mul_t(jnp.concatenate([dcore_ref[i], dfresh[i]], axis=0), state_ref[i]) for i in members
    ]
    dinner = [jnp.where(lower, mul_t(dcore_ref[i], fresh[i]), 0.0) for i in members]
    dkeys_tail = [mul_t(fresh[i], dstate_ref[i]) for i in members]
    dboth = [
        mul(
            jnp.transpose(inv_ref[i]),
            jnp.concatenate([dfresh[i], -through[i][CHUNK:]], axis=1),
        )
        for i in members
    ]
    dstrict = [jnp.where(strict, -mul_t(dboth[i], uw_ref[i]), 0.0) for i in members]
    stacked, crossed = [], []
    for i in members:
        queries, keys_in, cols, decay = setups[i][3], setups[i][4], setups[i][9], setups[i][10]
        dscores_n = dstrict[i] * decay * cols[:, 1:2]
        dscores = dinner[i] * decay
        stacked.append(
            mul(jnp.concatenate([dscores, dscores_n + jnp.transpose(dscores_n)], axis=0), keys_in)
        )
        crossed.append(mul(jnp.transpose(dscores), queries))
    for i in reversed(members):
        starts, keeps, pieces, queries, keys_in, values_in, q_scale, k_scale, rows, cols, _ = setups[i]
        beta, gam, tail = cols[:, 1:2], cols[:, 2:3], cols[:, 3:4]
        dqueries_faded = through[i][:CHUNK]
        dvalues_beta, dkeys_beta = dboth[i][:, :CHUNK], dboth[i][:, CHUNK:]
        keys_gam = keys_in * gam
        dqueries = stacked[i][:CHUNK] + dqueries_faded * gam
        dkeys = (
            stacked[i][CHUNK:]
            + crossed[i]
            + dkeys_beta * (beta * gam)
            + dkeys_tail[i] * tail
        )
        dvalues = dvalues_beta * beta

        dkkf = dstrict[i] * kkf_ref[i]
        flow = dkkf * beta + dinner[i] * p_ref[i]
        tail_term = lane_sum(dkeys_tail[i] * keys_in * tail)
        dbeta = lane_sum(dkkf + dvalues_beta * values_in + dkeys_beta * keys_gam)
        dsum = (
            lane_sum(flow + (dqueries_faded * queries + dkeys_beta * keys_in * beta) * gam)
            - tail_term
        )
        last = jnp.sum(tail_term) + jnp.sum(state_ref[i] * dstate_ref[i] * rows[4:5, 0:1])
        last_col = jnp.where(row_index[:, :1] == CHUNK - 1, last, 0.0)
        packed = jnp.where(
            col_index == 0, dsum + last_col, jnp.where(col_index == 1, dbeta, 0.0)
        )
        turned = jnp.transpose(packed)[:8]
        flow_rows = jnp.sum(flow, axis=0, keepdims=True)
        kind = row_index[:8]
        dtotal = jnp.where(kind == 0, turned - flow_rows, 0.0)
        dlog = spread_sum(dtotal, lower.astype(jnp.float32))[0:1]
        chunk = (pl.num_programs(0) - 1 - step) * BACK_BATCH + i
        pair = jnp.transpose(head_rows(raw_refs, place_ref, chunk, 4))[:8]
        inside = pair[0:1] + params_ref[1, 0]
        rate = -jnp.exp(params_ref[0, 0] + jnp.zeros((1, CHUNK), jnp.float32))
        dinside = dlog * rate * jax.nn.sigmoid(inside)
        beta_row = rows[1:2]
        dbeta_raw = turned[1:2] * beta_row * (1.0 - beta_row)
        drate = dlog * rate * jax.nn.softplus(inside)
        dparams_ref[...] += jnp.where(kind == 0, drate, jnp.where(kind == 1, dinside, 0.0))
        ddecay = jnp.where(kind == 0, dinside, jnp.where(kind == 1, dbeta_raw, 0.0))
        put_rows(draw_ref, place_ref, chunk, slice(3 * CHUNK, 4 * CHUNK), dgate_ref[i])
        put_rows(
            draw_ref, place_ref, chunk, slice(4 * CHUNK, 5 * CHUNK), chunk_cols(ddecay).astype(jnp.bfloat16)
        )

        d_scaled_q = dqueries * CHUNK ** (-0.5)
        gates = [jax.nn.sigmoid(piece[1]) for piece in pieces]
        unit_q, unit_k = pieces[0][1] * gates[0] * q_scale, pieces[1][1] * gates[1] * k_scale
        dact = [
            q_scale * (d_scaled_q - unit_q * lane_sum(d_scaled_q * unit_q)),
            k_scale * (dkeys - unit_k * lane_sum(dkeys * unit_k)),
            dvalues,
        ]
        for part in range(3):
            rows_by_offset, conv = pieces[part]
            gate = gates[part]
            dconv = dact[part] * (gate * (1.0 + conv * (1.0 - gate)))
            taps = taps_ref[part]
            after = next_ref[part]
            draw = dconv * taps[3:4]
            for offset in range(1, 4):
                kept = jnp.concatenate([dconv * keeps[offset - 1], after], axis=0)
                draw = draw + pltpu.roll(kept, CHUNK + 8 - offset, 0)[:CHUNK] * taps[3 - offset : 4 - offset]
            lanes = slice(part * CHUNK, (part + 1) * CHUNK)
            put_rows(draw_ref, place_ref, chunk, lanes, draw.astype(jnp.bfloat16))
            for offset in range(4):
                dtaps_ref[part, 3 - offset : 4 - offset] += jnp.sum(
                    dconv * rows_by_offset[offset], axis=0, keepdims=True
                )
            next_ref[part] = dconv[:8] * (1.0 - starts[0])

    @pl.when(step == pl.num_programs(0) - 1)
    def _():
        draw0_ref[...] = draw_ref[0]
        draw1_ref[...] = draw_ref[1]


def back(place, starts, params, raw0, raw1, rows, taps, inverse, kkf, inner, joined, states, dstates, dcore, dgate):
    chunks = rows.shape[0]
    square = (BACK_BATCH, CHUNK, CHUNK)
    wide = (BACK_BATCH, CHUNK, 2 * CHUNK)
    turned = partial(per_batch, turned=True, steps=chunks // BACK_BATCH)
    draw = (2,) + raw0.shape
    return pl.pallas_call(
        back_kernel,
        grid_spec=pltpu.PrefetchScalarGridSpec(
            num_scalar_prefetch=3,
            grid=(chunks // BACK_BATCH,),
            in_specs=[whole(raw0.shape), whole(raw1.shape), turned((BACK_BATCH, 8, CHUNK)), whole(taps.shape),
                      turned(square), turned(square), turned(square), turned(wide), turned(square),
                      turned(square), turned(square), turned(square)],
            out_specs=[whole(raw0.shape), whole(raw0.shape), whole((3, 4, CHUNK)), whole((8, CHUNK))],
            scratch_shapes=[pltpu.VMEM((3, 8, CHUNK), jnp.float32), pltpu.VMEM(draw, jnp.bfloat16)],
        ),
        out_shape=[shaped(raw0.shape, jnp.bfloat16)] * 2 + [shaped((3, 4, CHUNK)), shaped((8, CHUNK))],
        compiler_params=pltpu.CompilerParams(vmem_limit_bytes=VMEM_MAX),
        cost_estimate=spends(24),
        name="back",
    )(place, starts, params, raw0, raw1, rows, taps, inverse, kkf, inner, joined, states, dstates, dcore, dgate)


def document_starts(doc_lengths, block_count):
    bounds = jnp.cumsum(doc_lengths)[:-1]
    blocks = jnp.arange(block_count, dtype=jnp.int32)
    opens = jnp.any(blocks[:, None] == bounds[None, :], axis=1) | (blocks == 0)
    return opens.astype(jnp.int32)


def mixer_forward(place, prepared, raw0, raw1, out_gain):
    rows, inverse, kkf, inner, joined, m, mt, b, r, pu = prepared
    states, core, mixed = scan_states(place, m, b, r, pu, raw0, raw1, out_gain)
    return mixed, (rows, inverse, kkf, inner, joined, mt, r, states, core)


def mixer_backward_scan(place, raw0, raw1, out_gain, kept, dmixed):
    mt, r, core = kept[5], kept[6], kept[8]
    return back_scan(place, mt, r, core, raw0, raw1, dmixed, out_gain)


def mixer_backward(place, starts, params, raw0, raw1, taps, kept, dstates, dcore, dgate):
    rows, inverse, kkf, inner, joined, _, _, states, _ = kept
    return back(
        place, starts, params, raw0, raw1, rows, taps, inverse, kkf, inner, joined, states, dstates, dcore, dgate
    )


from jax.sharding import PartitionSpec as P

LANES = 128
HALF = 384
GROUP = 256
SIDE = 64


def exchange_perm(count, shifted, sizes):
    pairs = []
    for target in range(count):
        source, scale, rest = 0, 1, target
        for size, offset in zip(reversed(sizes), reversed(shifted)):
            source += (rest % size + offset) % size * scale
            rest //= size
            scale *= size
        pairs.append((source, target))
    return pairs


def from_head(value, dz=0, dx=0, dc=0):
    return lax.ppermute(value, "head", exchange_perm(16, (dz, dx, dc), (4, 2, 2)))


def from_dp(value, dy=0, dx=0):
    return lax.ppermute(value, "dp", exchange_perm(8, (dy, dx), (4, 2)))


def after(value, *earlier):
    return lax.optimization_barrier((value,) + earlier)[0]


def gather_turn(value, cut, beside=()):
    first, second = value[:cut], value[cut:]
    arrived = [take_zx(first, 0, 1)] + [take_zx(second, k, 0) for k in (1, 2, 3)]
    arrived = lax.optimization_barrier(tuple(arrived) + tuple(beside))
    pair = jnp.concatenate([first, arrived[0]], axis=0)
    column = jnp.concatenate([second, *arrived[1:4]], axis=0)
    return lax.optimization_barrier((pair, column))


def gather_end(pair, column):
    return [pair] + [take_zx(pair, k, 0) for k in (1, 2, 3)], [column, take_zx(column, 0, 1)]


def take_zx(value, ring, side):
    return from_head(value, dz=ring, dx=side)


def take_yx(value, ring, side):
    return from_dp(value, dy=ring, dx=side)


def wide(value):
    return value.astype(jnp.float32)


def narrow(value):
    return value.astype(jnp.bfloat16)


def sum_rows(pieces, rows):
    total = wide(pieces[0][rows])
    for piece in pieces[1:]:
        total = total + wide(piece[rows])
    return total


def reduce_arrivals(rounds, far, beside=()):
    arrived = [take_zx(rounds[k - 1], -k, 0) for k in (1, 2, 3)] + [take_zx(far, 0, 1)]
    return lax.optimization_barrier(tuple(arrived) + tuple(beside))[:4], arrived[0]


def turn_sum_kernel(*refs):
    rounds, sides, outs = refs[:4], refs[4:6], refs[6:]
    cut = rounds[0].shape[0] // 2
    early, late = slice(0, cut), slice(cut, None)
    total = wide(rounds[0][...])
    for ref in rounds[1:]:
        total = total + wide(ref[...])
    outs[0][...] = total[early]
    outs[1][...] = narrow(total[late])
    total = wide(sides[0][...]) + wide(sides[1][...])
    rest = total.shape[0] // 4
    outs[2][...] = total[:rest]
    for k in (1, 2, 3):
        outs[2 + k][...] = narrow(total[rest * k : rest * (k + 1)])


def reduce_parts(first, near, arrived):
    width = first.shape[1]
    cut, rest = (first.shape[0] // 2, width), (near.shape[0] // 4, width)
    outs = [shaped(cut), shaped(cut, jnp.bfloat16), shaped(rest)] + [shaped(rest, jnp.bfloat16)] * 3
    return whole_call(turn_sum_kernel, outs, "turn_sum", (), first, *arrived[:3], near, arrived[3])


def small_kernel(gain1_ref, gain2_ref, out_gain_ref, params_ref, taps_ref, out_grad_ref, sent_ref, rows_ref):
    for row in range(8):
        for half in range(2):
            lanes = slice(half * LANES, (half + 1) * LANES)
            place = 2 * row + half
            rows_ref[place : place + 1] = gain1_ref[row, 0:1, lanes]
            rows_ref[16 + place : 17 + place] = gain2_ref[:, place * LANES : (place + 1) * LANES]
    rows_ref[32:40] = out_gain_ref[...]
    rows_ref[40:48] = params_ref[...]
    for part in range(3):
        rows_ref[48 + 4 * part : 52 + 4 * part] = taps_ref[part]
    rows_ref[60:] = jnp.zeros_like(rows_ref[60:])
    small = rows_ref[...]
    high, rest = split(small)
    low = narrow(small - wide(high) - wide(rest))
    pieces = jnp.concatenate([high, rest, low], axis=0)
    for target in range(8):
        sent_ref[target, :GROUP] = out_grad_ref[target]
        sent_ref[target, GROUP:] = pieces


def side_sum_kernel(near_ref, crossed_ref, *out_refs):
    for k, out_ref in enumerate(out_refs):
        for half in range(2):
            rows = slice(SIDE * (4 * half + k), SIDE * (4 * half + k + 1))
            total = wide(near_ref[rows]) + wide(crossed_ref[rows])
            out_ref[SIDE * half : SIDE * (half + 1)] = total if k == 0 else narrow(total)


def ring_sum_kernel(over_ref, arrived_ref, kept_ref, sent_ref):
    half = kept_ref.shape[0]
    for target, side in ((kept_ref, over_ref[0]), (sent_ref, 1 - over_ref[0])):
        rows = pl.ds(pl.multiple_of(side * half, 16), half)
        total = wide(arrived_ref[0, rows])
        for source in (1, 2, 3):
            total = total + wide(arrived_ref[source, rows])
        target[...] = total.astype(target.dtype)


def reduce_end(parts):
    return (parts[0], take_zx(parts[1], 0, 1), parts[2]) + tuple(
        take_zx(parts[2 + k], -k, 0) for k in (1, 2, 3)
    )


RINGS = [[0, 2, 4, 6], [1, 3, 5, 7]]


def pair_kernel(over_ref, value_ref, mate_ref, *out_refs):
    rows, start = value_ref.shape[0], 0
    for out_ref in out_refs:
        lanes = slice(start, start + out_ref.shape[1])
        start = lanes.stop
        for source, place in ((value_ref, over_ref[0]), (mate_ref, 1 - over_ref[0])):
            out_ref[pl.ds(pl.multiple_of(place * rows, 16), rows)] = source[:, lanes]


def ordered_pair(value, mate):
    over = (lax.axis_index("dp") % 2)[None].astype(jnp.int32)
    outs = [shaped((2 * value.shape[0], columns), value.dtype) for columns in (2 * HALF, HALF)]
    return whole_call(pair_kernel, outs, "ordered_pair", (over,), value, mate)


def ordered_join_kernel(up_ref, *refs):
    sources, target, sems = refs[:4], refs[4], refs[5]
    rows = sources[0].shape[0]
    copies = []
    for k, ref in enumerate(sources):
        place = lax.rem(up_ref[0] + k, 4)
        copies.append(
            pltpu.make_async_copy(ref, target.at[pl.ds(pl.multiple_of(place * rows, 16), rows)], sems.at[k])
        )
        copies[-1].start()
    for copy in copies:
        copy.wait()


def ordered_join(pieces):
    anywhere = pl.BlockSpec(memory_space=pl.ANY)
    rows, columns = pieces[0].shape
    return pl.pallas_call(
        ordered_join_kernel,
        grid_spec=pltpu.PrefetchScalarGridSpec(
            num_scalar_prefetch=1,
            grid=(1,),
            in_specs=[anywhere] * 4,
            out_specs=whole((4 * rows, columns)),
            scratch_shapes=[pltpu.SemaphoreType.DMA((4,))],
        ),
        out_shape=shaped((4 * rows, columns), pieces[0].dtype),
        compiler_params=pltpu.CompilerParams(vmem_limit_bytes=VMEM_MAX),
        cost_estimate=spends(4),
        name="ordered_join",
    )((lax.axis_index("dp") // 2)[None].astype(jnp.int32), *pieces)


def spread_kernel(over_ref, *refs):
    over, out_ref = over_ref[0], refs[-1]
    count = (len(refs) - 1) // 2
    for place in range(count):
        lanes = slice(place * HALF, (place + 1) * HALF)
        out_ref[0, over, :, lanes] = refs[place][...]
        out_ref[0, 1 - over, :, lanes] = refs[count + place][...]


def spread_pair(value, mate):
    rows, columns = value.shape
    count = columns // HALF
    blocks = [held((rows, HALF), lambda *_, place=place: (0, place)) for place in range(count)]
    return pl.pallas_call(
        spread_kernel,
        grid_spec=pltpu.PrefetchScalarGridSpec(
            num_scalar_prefetch=1,
            grid=(4,),
            in_specs=blocks * 2,
            out_specs=pl.BlockSpec((1, 2, rows, columns), lambda turn, *_: (turn, 0, 0, 0)),
        ),
        out_shape=shaped((4, 2, rows, columns), value.dtype),
        compiler_params=pltpu.CompilerParams(vmem_limit_bytes=VMEM_MAX),
        cost_estimate=spends(3),
        name="spread_pair",
    )((lax.axis_index("dp") % 2)[None].astype(jnp.int32), *[value] * count, *[mate] * count)


def round_ring(spread):
    everything = lax.all_to_all(spread, "dp", 0, 0, tiled=False, axis_index_groups=RINGS)
    return everything.reshape(8 * spread.shape[2], spread.shape[3])


def ring_parts(arrived):
    over = (lax.axis_index("dp") % 2)[None].astype(jnp.int32)
    half = (arrived.shape[1] // 2, arrived.shape[2])
    return whole_call(ring_sum_kernel, [shaped(half), shaped(half, jnp.bfloat16)], "ring_sum", (over,), arrived)


def exchange_ring(value):
    return lax.all_to_all(value, "dp", 0, 0, tiled=False, axis_index_groups=RINGS)


def sum_all(value, axis, count):
    spread = jnp.broadcast_to(value, (count,) + value.shape)
    return jnp.sum(lax.all_to_all(spread, axis, 0, 0, tiled=False), axis=0)


def whole_call(kernel, out_shape, name, scalars, *arrays, scratch=()):
    outs = out_shape if isinstance(out_shape, (list, tuple)) else [out_shape]
    return pl.pallas_call(
        kernel,
        grid_spec=pltpu.PrefetchScalarGridSpec(
            num_scalar_prefetch=len(scalars),
            grid=(1,),
            in_specs=[whole(array.shape) for array in arrays],
            out_specs=[whole(out.shape) for out in outs],
            scratch_shapes=list(scratch),
        ),
        out_shape=list(outs),
        compiler_params=pltpu.CompilerParams(vmem_limit_bytes=VMEM_MAX),
        cost_estimate=spends(3),
        name=name,
    )(*scalars, *arrays)


def rms_parts(values):
    scale = lax.rsqrt(jnp.mean(values * values, axis=-1, keepdims=True) + 1e-05)
    return scale, values * scale


def rms_back(grad, gain, scale, unit):
    inner = grad * gain
    return scale * (inner - unit * jnp.mean(inner * unit, axis=-1, keepdims=True))


def enter_kernel(tokens_ref, gain_ref, normed_ref):
    _, unit = rms_parts(wide(tokens_ref[...]))
    normed_ref[...] = narrow(unit * gain_ref[...])


def project_kernel(own_ref, other_ref, weights_ref, own_out_ref, other_out_ref):
    step = pl.program_id(0)
    half = pl.num_programs(0) // 2

    @pl.when(step < half)
    def _():
        own_out_ref[...] = plain_product(own_ref[...], weights_ref[...])

    @pl.when(step >= half)
    def _():
        other_out_ref[...] = plain_product(other_ref[...], weights_ref[...])


def project(own, other, weights, columns):
    count, width = own.shape
    step = 512
    half = count // step

    def early(size):
        return pl.BlockSpec((step, size), lambda i: (jnp.minimum(i, half - 1), 0))

    def late(size):
        return pl.BlockSpec((step, size), lambda i: (jnp.maximum(i - half, 0), 0))

    return pl.pallas_call(
        project_kernel,
        grid=(2 * half,),
        in_specs=[early(width), late(width), held((width, columns))],
        out_specs=[early(columns), late(columns)],
        out_shape=[shaped((count, columns))] * 2,
        compiler_params=pltpu.CompilerParams(vmem_limit_bytes=VMEM_MAX),
        cost_estimate=spends(5),
        name="project",
    )(own, other, weights)


def unproject_kernel(own_ref, far_ref, weights_ref, far_weights_ref, *piece_refs):
    step = pl.program_id(0)
    total = against(own_rows(own_ref, step), weights_ref[...]) + against(
        own_rows(far_ref, step), far_weights_ref[...]
    )
    put_pieces(narrow(total), piece_refs, step)


def unproject(own, far, weights, far_weights, piece_shapes):
    used = held((weights.shape[0], own.shape[1]))
    return pl.pallas_call(
        unproject_kernel,
        grid=(4,),
        in_specs=[held(own.shape), held(far.shape), used, used],
        out_specs=[whole(shape) for shape in piece_shapes],
        out_shape=[shaped(shape, jnp.bfloat16) for shape in piece_shapes],
        compiler_params=pltpu.CompilerParams(vmem_limit_bytes=VMEM_MAX),
        cost_estimate=spends(8),
        name="unproject",
    )(own, far, weights, far_weights)


def feed_grad_kernel(*refs):
    own_ref, far_ref = refs[8:]
    gate_up, down = 0.0, 0.0
    for normed_ref, cot_ref, dpre_ref, hidden_ref in (refs[:4], refs[4:8]):
        gate_up = gate_up + over_rows(normed_ref[...], dpre_ref[...])
        down = down + over_rows(cot_ref[...], hidden_ref[...])
    gate_up, down = narrow(gate_up), narrow(down)
    own_ref[:, : 2 * HALF] = gate_up[:, : 2 * HALF]
    far_ref[:, : 2 * HALF] = gate_up[:, 2 * HALF :]
    own_ref[:, 2 * HALF :] = down[:, :HALF]
    far_ref[:, 2 * HALF :] = down[:, HALF:]


def feed_grads(*parts):
    arrays, specs = [], []
    width = parts[0][2].shape[1]
    for hidden, dpre, normed, cot in parts:
        rows = pl.BlockSpec((normed.shape[0], GROUP), lambda i: (0, i))
        arrays += [normed, cot, dpre, hidden]
        specs += [rows, rows, held(dpre.shape), held(hidden.shape)]
    out = pl.BlockSpec((GROUP, 3 * HALF), lambda i: (i, 0))
    return pl.pallas_call(
        feed_grad_kernel,
        grid=(width // GROUP,),
        in_specs=specs,
        out_specs=[out, out],
        out_shape=[shaped((width, 3 * HALF), jnp.bfloat16)] * 2,
        compiler_params=pltpu.CompilerParams(vmem_limit_bytes=VMEM_MAX),
        cost_estimate=spends(12),
        name="feed_grads",
    )(*arrays)


def in_grad_kernel(own_ref, other_ref, draw0_ref, draw1_ref, weights_ref, gain_ref, out_ref, part_ref):
    grad = narrow(over_rows(own_ref[...], draw0_ref[...]) + over_rows(other_ref[...], draw1_ref[...]))
    out_ref[0] = grad
    product = wide(grad) * wide(weights_ref[...])
    lanes = product[:, :LANES]
    for start in range(LANES, product.shape[1], LANES):
        lanes = lanes + product[:, start : start + LANES]
    part = jnp.sum(jnp.transpose(lanes), axis=0, keepdims=True) / gain_ref[...]
    part_ref[0] = jnp.broadcast_to(part, part_ref.shape[1:])


def in_grads(own, other, draw0, draw1, weights, gain):
    count, width = own.shape
    used = draw0.shape[1]
    rows = pl.BlockSpec((count, GROUP), lambda i: (0, i))
    grad, part = pl.pallas_call(
        in_grad_kernel,
        grid=(width // GROUP,),
        in_specs=[rows, rows, held(draw0.shape), held(draw1.shape),
                  pl.BlockSpec((GROUP, used), lambda i: (i, 0)), pl.BlockSpec((1, GROUP), lambda i: (0, i))],
        out_specs=[pl.BlockSpec((1, GROUP, used), lambda i: (i // 2, i % 2, 0)),
                   pl.BlockSpec((1, 8, GROUP), lambda i: (i, 0, 0))],
        out_shape=[shaped((4, 2 * GROUP, used), jnp.bfloat16), shaped((width // GROUP, 8, GROUP))],
        compiler_params=pltpu.CompilerParams(vmem_limit_bytes=VMEM_MAX),
        cost_estimate=spends(8),
        name="in_grads",
    )(own, other, draw0, draw1, weights, gain)
    return grad, part


def out_grad_kernel(rows_ref, mixed_ref, out_ref):
    out_ref[0] = narrow(over_rows(rows_ref[...], mixed_ref[...]))


def out_grads(rows, mixed):
    count, width = rows.shape
    return pl.pallas_call(
        out_grad_kernel,
        grid=(width // GROUP,),
        in_specs=[pl.BlockSpec((count, GROUP), lambda i: (0, i)), held(mixed.shape)],
        out_specs=pl.BlockSpec((1, GROUP, mixed.shape[1]), lambda i: (i, 0, 0)),
        out_shape=shaped((width // GROUP, GROUP, mixed.shape[1]), jnp.bfloat16),
        compiler_params=pltpu.CompilerParams(vmem_limit_bytes=VMEM_MAX),
        cost_estimate=spends(6),
        name="out_grads",
    )(rows, mixed)


def own_rows(ref, step):
    first = pl.ds(pl.multiple_of(step * 2 * ROWS_A, 16), 2 * ROWS_A)
    near = pl.ds(pl.multiple_of(8 * ROWS_A + step * ROWS_B, 16), ROWS_B)
    far = pl.ds(pl.multiple_of(8 * ROWS_A + 4 * ROWS_B + step * ROWS_B, 16), ROWS_B)
    return jnp.concatenate([ref[first], ref[near], ref[far]], axis=0)


def put_pieces(total, piece_refs, step):
    side = pl.ds(pl.multiple_of(step * ROWS_B, 16), ROWS_B)
    for k in range(4):

        @pl.when(step == k)
        def _(k=k):
            piece_refs[k][...] = total[: 2 * ROWS_A]

    piece_refs[4][side] = total[2 * ROWS_A : 2 * ROWS_A + ROWS_B]
    piece_refs[5][side] = total[2 * ROWS_A + ROWS_B :]


def attn_kernel(heads_ref, mixed_ref, *refs):
    weight_refs, (rows_ref, gain_ref, resid_ref, normed_ref, total_ref) = refs[:4], refs[4:]
    step = pl.program_id(0)

    @pl.when(step == 0)
    def _():
        total_ref[...] = wide(rows_ref[...])

    mixed = jnp.concatenate([mixed_ref[heads_ref[i % 2, 2 * step + i // 2]] for i in range(4)], axis=1)
    total_ref[...] += against(mixed, jnp.concatenate([ref[0] for ref in weight_refs], axis=1))

    @pl.when(step == pl.num_programs(0) - 1)
    def _():
        resid = total_ref[...]
        resid_ref[...] = resid
        _, unit = rms_parts(resid)
        normed_ref[...] = narrow(unit * gain_ref[...])


def out_weight_specs(out_heads):
    shape = (1,) + out_heads.shape[1:]
    return [
        pl.BlockSpec(shape, lambda step, heads_ref, i=i: (heads_ref[i % 2, 2 * step + i // 2], 0, 0))
        for i in range(4)
    ]


def attend(heads, received, out_heads, rows, gain):
    shape = rows.shape
    return pl.pallas_call(
        attn_kernel,
        grid_spec=pltpu.PrefetchScalarGridSpec(
            num_scalar_prefetch=1,
            grid=(4,),
            in_specs=[whole(received.shape)] + out_weight_specs(out_heads) + [whole(shape), whole(gain.shape)],
            out_specs=[whole(shape), whole(shape)],
            scratch_shapes=[pltpu.VMEM(shape, jnp.float32)],
        ),
        out_shape=[shaped(shape), shaped(shape, jnp.bfloat16)],
        compiler_params=pltpu.CompilerParams(vmem_limit_bytes=VMEM_MAX),
        cost_estimate=spends(10),
        name="attend",
    )(heads, received, *[out_heads] * 4, rows, gain)


def total_of(refs):
    first = refs[0][...] + wide(refs[1][...])
    second = refs[2][...] + wide(refs[3][...]) + wide(refs[4][...]) + wide(refs[5][...])
    return jnp.concatenate([first, second], axis=0)


def middle_kernel(heads_ref, *refs):
    pieces, (resid_ref, cot_ref, gain_ref), weight_refs = refs[:6], refs[6:9], refs[9:13]
    dresid_ref, dattn_ref, dgain_ref, dmixed_ref = refs[13:]
    step = pl.program_id(0)

    @pl.when(step == 0)
    def _():
        grad = total_of(pieces)
        scale, unit = rms_parts(resid_ref[...])
        dgain_ref[...] = jnp.sum(grad * unit, axis=0, keepdims=True)
        dresid = wide(cot_ref[...]) + rms_back(grad, gain_ref[...], scale, unit)
        dresid_ref[...] = dresid
        dattn_ref[...] = narrow(dresid)

    weights = jnp.concatenate([ref[0] for ref in weight_refs], axis=1)
    total = narrow(plain_product(dattn_ref[...], weights))
    for i in range(4):
        dmixed_ref[heads_ref[i % 2, 2 * step + i // 2]] = total[:, i * LANES : (i + 1) * LANES]


def middle(heads, pieces, resid, cot, gain, out_heads):
    shape = resid.shape
    mixed_shape = (16, shape[0], LANES)
    return pl.pallas_call(
        middle_kernel,
        grid_spec=pltpu.PrefetchScalarGridSpec(
            num_scalar_prefetch=1,
            grid=(4,),
            in_specs=[whole(piece.shape) for piece in pieces]
            + [whole(shape), whole(shape), whole(gain.shape)]
            + out_weight_specs(out_heads),
            out_specs=[whole(shape), whole(shape), whole((1, shape[1])), whole(mixed_shape)],
        ),
        out_shape=[shaped(shape), shaped(shape, jnp.bfloat16), shaped((1, shape[1])),
                   shaped(mixed_shape, jnp.bfloat16)],
        compiler_params=pltpu.CompilerParams(vmem_limit_bytes=VMEM_MAX),
        cost_estimate=spends(10),
        name="middle",
    )(heads, *pieces, resid, cot, gain, *[out_heads] * 4)


def leave_kernel(*refs):
    total = refs[0][...] + refs[4][...]
    for ref in refs[1:4]:
        total = total + wide(ref[...])
    refs[5][...] = narrow(total)


def finish_kernel(*refs):
    pieces, (rows_ref, dresid_ref, gain_ref, out_ref) = refs[:6], refs[6:]
    scale, unit = rms_parts(wide(rows_ref[...]))
    out_ref[...] = dresid_ref[...] + rms_back(total_of(pieces), gain_ref[...], scale, unit)


def feed_kernel(halves, count, joins, heads_ref, *refs):
    normed_refs, refs = refs[:count], refs[count:]
    cot_refs, refs = refs[: len(halves)], refs[len(halves) :]
    weight_refs, refs = refs[:4], refs[4:]
    earlier_refs, refs = refs[: 2 * joins], refs[2 * joins :]
    fed_refs, dnormed_refs, refs = refs[:2], refs[2 : 2 + count], refs[2 + count :]
    hidden_ref, dpre_ref, normed_out_ref, cot_out_ref, normed_ref, cot_ref, out_ref, grad_ref = refs
    step, last = pl.program_id(0), pl.num_programs(0) - 1
    size = hidden_ref.shape[0]

    @pl.when(step == 0)
    def _():
        start = 0
        for ref in normed_refs:
            normed_ref[start : start + ref.shape[0]] = ref[...]
            start += ref.shape[0]
        for place, ref in enumerate(cot_refs):
            cot_ref[SIDE * place : SIDE * (place + 1)] = ref[...]

    rows = pl.ds(pl.multiple_of(step * size, 16), size)
    normed, cot = normed_ref[rows], cot_ref[rows]
    normed_out_ref[...] = normed
    cot_out_ref[...] = cot
    out, dnormed = 0.0, 0.0
    for half in range(2):
        gu_ref, down_ref = weight_refs[2 * half], weight_refs[2 * half + 1]
        pre = plain_product(normed, gu_ref[...])
        gate, up = pre[:, :HALF], pre[:, HALF:]
        dhidden = plain_product(cot, down_ref[...])
        sigmoid = jax.nn.sigmoid(gate)
        act = gate * sigmoid
        hidden = narrow(act * up)
        dgate = narrow(dhidden * up * sigmoid * (1.0 + gate * (1.0 - sigmoid)))
        dpre = jnp.concatenate([dgate, narrow(dhidden * act)], axis=1)
        hidden_ref[:, half * HALF : (half + 1) * HALF] = hidden
        dpre_ref[:, 2 * half * HALF : 2 * (half + 1) * HALF] = dpre
        out = out + against(hidden, down_ref[...])
        dnormed = dnormed + against(dpre, gu_ref[...])
    out_ref[rows] = narrow(out)
    grad_ref[rows] = narrow(dnormed)

    @pl.when(step == last)
    def _():
        start = 0
        for ref in dnormed_refs:
            ref[...] = grad_ref[start : start + ref.shape[0]]
            start += ref.shape[0]
        if joins:
            near_ref, far_ref = fed_refs
            for k in range(4):
                first = earlier_refs[0] if k == 0 else out_ref.at[2 * SIDE * (k - 1) : 2 * SIDE * k]
                near_ref[SIDE * k : SIDE * (k + 1)] = first[:SIDE]
                far_ref[SIDE * k : SIDE * (k + 1)] = first[SIDE:]
            near_ref[4 * SIDE :] = earlier_refs[1][...]
            far_ref[4 * SIDE :] = out_ref[6 * SIDE :]
        else:
            fed_refs[0][...] = out_ref[: 2 * SIDE]
            fed_refs[1][...] = out_ref[2 * SIDE :]


def held(shape, place=None):
    place = place or (lambda *_: (0,) * len(shape))
    return pl.BlockSpec(shape, place, pipeline_mode=pl.Buffered(1))


def feed(heads, pieces, halves, cot, own, other, steps, earlier=()):
    width = cot.shape[1]
    shapes = [piece.shape for piece in pieces]
    count = sum(shape[0] for shape in shapes)
    size = count // steps
    gate_up, down = held((width, 2 * HALF)), held((width, HALF))

    def half_block(slot, half):
        return held((SIDE, width), lambda i, heads_ref: (2 * heads_ref[0, slot] + half, 0))

    fed_shapes = [(8 * SIDE, width)] * 2 if earlier else shapes
    row_widths = (2 * HALF, 4 * HALF, width, width)
    outs = pl.pallas_call(
        partial(feed_kernel, tuple(halves), len(pieces), bool(earlier)),
        grid_spec=pltpu.PrefetchScalarGridSpec(
            num_scalar_prefetch=1,
            grid=(steps,),
            in_specs=[held(shape) for shape in shapes]
            + [half_block(*half) for half in halves]
            + [gate_up, down, gate_up, down]
            + [held(piece.shape) for piece in earlier],
            out_specs=[whole(shape) for shape in fed_shapes + shapes]
            + [pl.BlockSpec((size, part), lambda i, *_: (i, 0)) for part in row_widths],
            scratch_shapes=[pltpu.VMEM((count, width), jnp.bfloat16)] * 4,
        ),
        out_shape=[shaped(shape, jnp.bfloat16) for shape in fed_shapes + shapes]
        + [shaped((count, part), jnp.bfloat16) for part in row_widths],
        compiler_params=pltpu.CompilerParams(vmem_limit_bytes=VMEM_MAX),
        cost_estimate=spends(28),
        name="feed",
    )(heads, *pieces, *[cot] * len(halves), *own, *other, *earlier)
    feds = len(fed_shapes)
    return outs[:feds], outs[feds : feds + len(shapes)], outs[feds + len(shapes) :]


def join_kernel(*refs):
    sources, target, sems = refs[:-2], refs[-2], refs[-1]
    copies, start = [], 0
    for place, ref in enumerate(sources):
        copies.append(pltpu.make_async_copy(ref, target.at[pl.ds(start, ref.shape[0])], sems.at[place]))
        copies[-1].start()
        start += ref.shape[0]
    for copy in copies:
        copy.wait()


def join(pieces):
    anywhere = pl.BlockSpec(memory_space=pl.ANY)
    rows = sum(piece.shape[0] for piece in pieces)
    return pl.pallas_call(
        join_kernel,
        in_specs=[anywhere] * len(pieces),
        out_specs=pl.BlockSpec(memory_space=pltpu.VMEM),
        out_shape=shaped((rows, pieces[0].shape[1]), pieces[0].dtype),
        scratch_shapes=[pltpu.SemaphoreType.DMA((len(pieces),))],
        compiler_params=pltpu.CompilerParams(vmem_limit_bytes=VMEM_MAX),
        cost_estimate=spends(3),
        name="join",
    )(*pieces)


def plain_product(left, right):
    return jnp.dot(left, right, preferred_element_type=jnp.float32)


def against(left, right):
    return lax.dot_general(left, right, (((1,), (1,)), ((), ())), preferred_element_type=jnp.float32)


def over_rows(left, right):
    return lax.dot_general(left, right, (((0,), (0,)), ((), ())), preferred_element_type=jnp.float32)


def tables():
    head = lax.axis_index("head")
    ring, side, core = head // 4, head // 2 % 2, head % 2
    chunk = jnp.arange(16, dtype=jnp.int32)
    dz, dx, dc = (chunk // 4 - ring) % 4, (chunk // 2 + side) % 2, (chunk + core) % 2
    place = jnp.stack([ROWS_A * (2 * dz + dx), 8 * ROWS_A + ROWS_B * (4 * dx + dz), dc]).astype(jnp.int32)
    step = jnp.arange(8, dtype=jnp.int32)
    chip = ((step + ring) % 4) * 2 + (step // 4 + side) % 2
    heads = jnp.stack([2 * chip + core, 2 * chip + 1 - core]).astype(jnp.int32)
    return place, heads


def body(
    tokens,
    cotangent,
    doc_spans,
    norm1_gain,
    q_weight,
    k_weight,
    v_weight,
    gate_out_weight,
    decay_weight,
    conv_weight,
    gate_params,
    out_gain,
    out_weight,
    norm2_gain,
    gate_weight,
    up_weight,
    down_weight,
):
    place, heads = tables()
    starts = document_starts(doc_spans[0], 32)
    out_gain_row = out_gain[None, :]
    gain1_row, gain2_row = norm1_gain[None, :], norm2_gain[None, :]
    rows_shape = tokens.shape
    width = rows_shape[1]

    def pad(weight, columns):
        return jnp.pad(weight, ((0, 0), (0, columns - weight.shape[1])))

    (normed1,) = whole_call(enter_kernel, shaped(rows_shape, jnp.bfloat16), "enter", (), tokens, gain1_row)

    packed = (conv_weight, decay_weight, q_weight, k_weight, v_weight, gate_out_weight, out_weight)
    conv_now, decay_now, *square_now = lax.optimization_barrier(packed + (normed1,))[:7]
    taps_block = jnp.pad(conv_now.reshape(12, 16), ((0, GROUP - 12), (0, 0)))
    side_block = pad(jnp.concatenate([decay_now[:, 0], taps_block], axis=1), LANES)
    pack_one = jnp.concatenate(square_now[:4] + [side_block] + square_now[4:], axis=1)
    wide_now = lax.optimization_barrier((gate_weight, up_weight, down_weight, normed1))[:3]
    pack_two = jnp.concatenate([pad(weight, HALF) for weight in wide_now], axis=1)
    cut, used = pack_one.shape[1], 5 * LANES

    mate_one = take_yx(pack_one, 0, 1)
    pair, column = gather_turn(normed1, ROWS_A, beside=(mate_one, pack_two))
    pair, column, mate_one = lax.optimization_barrier((pair, column, mate_one))
    mate_two = take_yx(after(pack_two, mate_one), 0, 1)
    mine_one = round_ring(spread_pair(pack_one, mate_one))
    rings, columns = gather_end(pair, column)
    rings, columns, mine_one, mate_two = lax.optimization_barrier((rings, columns, mine_one, mate_two))
    pair_gu, pair_down = ordered_pair(pack_two, mate_two)
    normed1_own = join(rings + columns)
    normed1_other = from_head(normed1_own, dc=1)
    raw0, raw1 = project(normed1_own, normed1_other, mine_one, used)
    taps = mine_one.reshape(8, GROUP, cut)[:, :12, 4 * LANES + 2 : 4 * LANES + 18]
    taps = wide(taps.transpose(1, 0, 2).reshape(3, 4, LANES))

    gu_arrived = [take_yx(pair_gu, k, 0) for k in (1, 2, 3)]

    out_heads = lax.all_gather(mine_one[:, used:], "head")
    prepared = prepare(place, starts, gate_params, raw0, raw1, taps)
    mixed, kept = mixer_forward(place, prepared, raw0, raw1, out_gain_row)
    mixed, gu_arrived, out_heads, pair_down = lax.optimization_barrier((mixed, gu_arrived, out_heads, pair_down))
    down_arrived = [take_yx(pair_down, k, 0) for k in (1, 2, 3)]
    cot_group = lax.all_gather(after(cotangent, out_heads), "head", axis=0, tiled=True)
    received = lax.all_to_all(mixed, "head", 0, 0, tiled=False)
    resid, normed2 = attend(heads, received, out_heads, tokens, gain2_row)
    gu_arrived, down_arrived = lax.optimization_barrier((gu_arrived, down_arrived, normed2))[:2]
    own_two = (ordered_join([pair_gu, *gu_arrived]), ordered_join([pair_down, *down_arrived]))
    pair, column = gather_turn(normed2, SIDE, beside=own_two)
    other_two = tuple(from_head(after(weights, pair), dc=1) for weights in own_two)
    rings, columns = gather_end(pair, column)
    near_halves = [(0, 0), (4, 0)] + [(k, 1) for k in range(4)]
    far_halves = [half for k in (1, 2, 3) for half in ((k, 0), (4 + k, 0))] + [(4 + k, 1) for k in range(4)]
    fed_early, (dpair, dnear), kept_near = feed(
        heads, [pair, column], near_halves, cot_group, own_two, other_two, 1
    )
    rings, columns, dpair = lax.optimization_barrier((rings, columns, dpair))
    (fed_near, fed_far), (*drings, dfar), kept_far = feed(
        heads, rings[1:] + columns[1:], far_halves, cot_group, own_two, other_two, 2, fed_early
    )

    parts = reduce_parts(dpair, dnear, reduce_arrivals(drings, dfar)[0])
    feed_own, feed_other = feed_grads(kept_near, kept_far)
    parts, feed_own, feed_other = lax.optimization_barrier((parts, feed_own, feed_other))
    feed_grad = narrow(wide(feed_own) + wide(from_head(feed_other, dc=1)))
    dnormed2_pieces = reduce_end(parts)
    resid_then = after(resid, feed_grad)
    dresid, dattn, dgain2, dmixed = middle(heads, dnormed2_pieces, resid_then, cotangent, gain2_row, out_heads)
    dmixed_mine = lax.all_to_all(dmixed, "head", 0, 0, tiled=False)
    dcore, dstates, dgate, dgain_out = mixer_backward_scan(place, raw0, raw1, out_gain_row, kept, dmixed_mine)

    feed_arrived = exchange_ring(after(feed_grad, dmixed_mine).reshape(4, 2 * GROUP, 3 * HALF))
    fed_crossed = take_zx(after(fed_far, dcore), 0, 1)
    dattn_group = lax.all_gather(dattn, "head", axis=0, tiled=True)
    weights_other = from_head(after(mine_one, dmixed), dc=1)

    draw0, draw1, dtaps, dparams = mixer_backward(
        place, starts, gate_params, raw0, raw1, taps, kept, dstates, dcore, dgate
    )
    draw0, draw1, weights_other = lax.optimization_barrier((draw0, draw1, weights_other))
    draw_far = from_head(draw1, dc=1)
    in_grad, gain1_part = in_grads(normed1_own, normed1_other, draw0, draw1, mine_one, gain1_row)
    draw_far = after(draw_far, in_grad)
    dnormed1 = unproject(draw0, draw_far, mine_one, weights_other, [(2 * ROWS_A, width)] * 4 + [(4 * ROWS_B, width)] * 2)
    dnormed1, feed_arrived, dattn_then, in_grad = lax.optimization_barrier(
        (dnormed1, feed_arrived, dattn_group, in_grad)
    )
    in_arrived = exchange_ring(in_grad)
    feed_kept, feed_sent = ring_parts(feed_arrived)
    out_grad = out_grads(dattn_then, mixed.reshape(dattn_group.shape[0], LANES))
    (sent,) = whole_call(
        small_kernel,
        shaped((8, GROUP + 192, LANES), jnp.bfloat16),
        "small",
        (),
        gain1_part,
        dgain2,
        dgain_out,
        dparams,
        dtaps,
        out_grad,
        scratch=[pltpu.VMEM((64, LANES), jnp.float32)],
    )
    half_rows = (2 * SIDE, width)
    in_kept, in_sent = ring_parts(in_arrived)
    fed_sums = whole_call(
        side_sum_kernel, [shaped(half_rows)] + [shaped(half_rows, jnp.bfloat16)] * 3, "side_sum", (), fed_near, after(fed_crossed, sent)
    )
    arrived, first_arrived = reduce_arrivals(
        dnormed1[1:4], dnormed1[5], beside=(feed_kept, feed_sent, in_kept, in_sent, sent, *fed_sums)
    )
    parts = reduce_parts(dnormed1[0], dnormed1[4], arrived)
    dnormed1_pieces = reduce_end(parts)
    fed_sums, feed_sent, in_sent = lax.optimization_barrier((fed_sums, feed_sent, in_sent, parts))[:3]
    fed_pieces = [fed_sums[0]] + [take_zx(fed_sums[k], -k, 0) for k in (1, 2, 3)]
    one_total = in_kept + wide(take_yx(in_sent, 0, 1))
    got = lax.all_to_all(after(sent, in_arrived, first_arrived), "dp", 0, 0, tiled=False)
    dnormed1_pieces, got = lax.optimization_barrier((dnormed1_pieces, got))
    out_total = jnp.sum(wide(got[:, :GROUP]), axis=0)
    pieces = wide(got[:, GROUP:]).reshape(8, 3, 64, LANES)
    small = jnp.sum(pieces[:, 0] + pieces[:, 1] + pieces[:, 2], axis=0)
    shared = sum_all(small[:40], "head", 16)
    fed_pieces, shared = lax.optimization_barrier((fed_pieces, shared))
    (block_out,) = whole_call(leave_kernel, shaped(rows_shape, jnp.bfloat16), "leave", (), *fed_pieces, resid)
    feed_got, shared = lax.optimization_barrier((take_yx(feed_sent, 0, 1), shared))
    feed_total = feed_kept + wide(feed_got)

    gain1_total = shared[:16].reshape(-1)
    gain2_total = shared[16:32].reshape(-1)
    out_gain_total = jnp.sum(shared[32:40], axis=0)
    params_total = jnp.sum(small[40:48], axis=1)[:2, None]
    taps_total = lax.dynamic_slice_in_dim(
        small[48:60].reshape(3, 4, LANES), lax.axis_index("dp") * 16, 16, 2
    )
    (tokens_grad,) = whole_call(
        finish_kernel, shaped(rows_shape), "finish", (), *dnormed1_pieces, tokens, dresid, gain1_row
    )
    hidden_units = gate_weight.shape[1]
    return (
        block_out,
        tokens_grad,
        gain1_total,
        one_total[:, :LANES],
        one_total[:, LANES : 2 * LANES],
        one_total[:, 2 * LANES : 3 * LANES],
        one_total[:, 3 * LANES : 4 * LANES],
        one_total[:, 4 * LANES : 4 * LANES + 2][:, None, :],
        taps_total,
        params_total,
        out_gain_total,
        out_total,
        gain2_total,
        feed_total[:, :hidden_units],
        feed_total[:, HALF : HALF + hidden_units],
        feed_total[:, 2 * HALF : 2 * HALF + hidden_units],
    )


def solution(mesh):
    rows, weight = P(("dp", "head"), None), P("dp", "head")
    weight3, taps = P("dp", "head", None), P(None, None, ("head", "dp"))
    params = P(None, "head")
    in_specs = (
        rows, rows, P("dp", None), P(), weight, weight, weight, weight, weight3, taps, params, P(),
        weight, P(), weight, weight, weight,
    )
    out_specs = (
        rows, rows, P(), weight, weight, weight, weight, weight3, taps, params, P(),
        weight, P(), weight, weight, weight,
    )
    return jax.shard_map(body, mesh=mesh, in_specs=in_specs, out_specs=out_specs, check_vma=False)
```

```python
from functools import partial

import jax
import jax.numpy as jnp
from jax import lax
from jax.experimental import pallas as pl
from jax.experimental.pallas import tpu as pltpu

CHUNK = 128
PREPARE_BATCH = 8
SCAN_BATCH = 4
BACK_BATCH = 2
ROWS_A = 80
ROWS_B = 48
GATE_ALONE = 9
VMEM_MAX = 56 * 1024 * 1024


def spends(microseconds):
    return pl.CostEstimate(flops=int(microseconds * 1e6), bytes_accessed=1 << 10, transcendentals=0)


def split(value):
    high = value.astype(jnp.bfloat16)
    return high, (value - high.astype(jnp.float32)).astype(jnp.bfloat16)


def left_pair(value):
    return jnp.concatenate(split(value), axis=1)


def right_pair(value):
    high, low = split(value)
    wide = jnp.concatenate([high, low], axis=1)
    return jnp.concatenate([wide, wide], axis=0)


def right_pair_t(value):
    high, low = split(value)
    return jnp.concatenate(
        [jnp.concatenate([high, high], axis=1), jnp.concatenate([low, low], axis=1)], axis=0
    )


def fold(wide):
    half = wide.shape[1] // 2
    return wide[:, :half] + wide[:, half:]


def mul_pairs(left, right):
    return fold(jnp.dot(left, right, preferred_element_type=jnp.float32))


def mul(left, right):
    return mul_pairs(left_pair(left), right_pair(right))


def mul_t(left, right):
    return fold(
        lax.dot_general(
            left_pair(left),
            right_pair_t(right),
            (((1,), (1,)), ((), ())),
            preferred_element_type=jnp.float32,
        )
    )


def iotas(rows=CHUNK, cols=CHUNK):
    return (
        lax.broadcasted_iota(jnp.int32, (rows, cols), 0),
        lax.broadcasted_iota(jnp.int32, (rows, cols), 1),
    )


def silu_parts(value):
    gate = jax.nn.sigmoid(value)
    return gate, value * gate


def tap_masks(start_first, start_second, row_index):
    keeps = []
    for offset in range(1, 4):
        first = jnp.where(row_index < offset, 1.0 - start_first, 1.0)
        second = jnp.where(
            (row_index >= CHUNK // 2) & (row_index < CHUNK // 2 + offset), 1.0 - start_second, 1.0
        )
        keeps.append(first * second)
    return keeps


def shifted_rows(current, before, keeps):
    joined = jnp.concatenate([before, current], axis=0)
    return [current] + [
        pltpu.roll(joined, offset, 0)[8:] * keeps[offset - 1] for offset in range(1, 4)
    ]


def conv_rows(rows_by_offset, taps):
    total = rows_by_offset[0] * taps[3:4]
    for offset in range(1, 4):
        total = total + rows_by_offset[offset] * taps[3 - offset : 4 - offset]
    return total


def chunk_cols(rows):
    return jnp.transpose(jnp.concatenate([rows, jnp.zeros((CHUNK - 8, CHUNK), jnp.float32)], axis=0))


def decay_matrix(rows, cols, start_second):
    row_index, col_index = iotas()
    gap = cols[:, 0:1] - rows[0:1, :]
    lower = row_index >= col_index
    cross = (row_index >= CHUNK // 2) & (col_index < CHUNK // 2)
    decay = jnp.where(lower, jnp.exp(jnp.where(lower, gap, 0.0)), 0.0)
    return decay * jnp.where(cross, 1.0 - start_second, 1.0)


def head_rows(raw_refs, place_ref, chunk, part):
    def load(start, count):
        rows = pl.ds(pl.multiple_of(start, 8), count)
        return jnp.where(half == 0, raw_refs[0][rows, lanes], raw_refs[1][rows, lanes])

    lanes = slice(None) if part == GATE_ALONE else slice(part * CHUNK, (part + 1) * CHUNK)
    half = place_ref[2, chunk]
    current = jnp.concatenate(
        [load(place_ref[0, chunk], ROWS_A), load(place_ref[1, chunk], ROWS_B)], axis=0
    )
    if part > 2:
        return current
    earlier = jnp.maximum(chunk - 1, 0)
    half = place_ref[2, earlier]
    return current, load(place_ref[1, earlier] + ROWS_B - 8, 8)


def put_rows(out_ref, place_ref, chunk, lanes, value):
    half = place_ref[2, chunk]
    first = pl.ds(pl.multiple_of(place_ref[0, chunk], 16), ROWS_A)
    second = pl.ds(pl.multiple_of(place_ref[1, chunk], 16), ROWS_B)
    out_ref[half, first, lanes] = value[:ROWS_A]
    out_ref[half, second, lanes] = value[ROWS_A:]


def spread_sum(rows, matrix):
    high, rest = split(rows)
    mid = rest
    low = (rows - high.astype(jnp.float32) - mid.astype(jnp.float32)).astype(jnp.bfloat16)
    parts = jnp.concatenate([high, mid, low, jnp.zeros_like(low)], axis=0)
    wide = jnp.dot(parts, matrix.astype(jnp.bfloat16), preferred_element_type=jnp.float32)
    return wide[:8] + wide[8:16] + wide[16:24]


def gate_rows(decay_cols, starts, params_ref):
    row_index, col_index = iotas()
    pair = jnp.transpose(decay_cols)[:8]
    position = col_index[:8]
    kind = row_index[:8]
    carry, same = 1.0 - starts[0], 1.0 - starts[1]
    second = position >= CHUNK // 2
    beta = jax.nn.sigmoid(pair[1:2])
    inside = pair[0:1] + params_ref[1, 0]
    soft = jax.nn.softplus(inside)
    decay_log = -jnp.exp(params_ref[0, 0] + jnp.zeros((8, CHUNK), jnp.float32)) * soft
    total = spread_sum(decay_log, (row_index <= col_index).astype(jnp.float32))
    end = total[:, CHUNK - 1 :]
    gam = jnp.exp(total) * carry * jnp.where(second, same, 1.0)
    tail = jnp.exp(end - total) * jnp.where(second, 1.0, same)
    span = jnp.exp(end) * carry * same
    rows = jnp.where(kind == 0, total, jnp.where(kind == 1, beta, jnp.where(kind == 2, gam, tail)))
    return jnp.where(kind == 4, span, rows)


def convolved(raw_refs, place_ref, starts, taps_ref, chunk, row_index):
    keeps = tap_masks(starts[0], starts[1], row_index)
    pieces = []
    for part in range(3):
        current, before = head_rows(raw_refs, place_ref, chunk, part)
        rows_by_offset = shifted_rows(current, before, keeps)
        pieces.append((rows_by_offset, conv_rows(rows_by_offset, taps_ref[part])))
    return keeps, pieces


def start_flags(starts_ref, chunk):
    return (
        starts_ref[2 * chunk].astype(jnp.float32),
        starts_ref[2 * chunk + 1].astype(jnp.float32),
    )


def normed_qkv(pieces):
    acts = [piece[1] * jax.nn.sigmoid(piece[1]) for piece in pieces]
    q_scale = lax.rsqrt(jnp.sum(acts[0] * acts[0], axis=-1, keepdims=True) + 1e-06)
    k_scale = lax.rsqrt(jnp.sum(acts[1] * acts[1], axis=-1, keepdims=True) + 1e-06)
    return acts[0] * q_scale * CHUNK ** (-0.5), acts[1] * k_scale, acts[2], q_scale, k_scale


def inverse_lower(stricts):
    row_index, col_index = iotas()
    eye = (row_index == col_index).astype(jnp.float32)
    near = row_index // 16 == col_index // 16
    powers = [jnp.where(near, strict, 0.0) for strict in stricts]
    inverses = [eye - power for power in powers]
    powers = [mul(power, power) for power in powers]
    for step in range(3):
        rights = [right_pair(power) for power in powers]
        if step < 2:
            stacks = [
                left_pair(jnp.concatenate([inverse, power], axis=0))
                for inverse, power in zip(inverses, powers)
            ]
            both = [mul_pairs(stack, right) for stack, right in zip(stacks, rights)]
            inverses = [inverse + pair[:CHUNK] for inverse, pair in zip(inverses, both)]
            powers = [pair[CHUNK:] for pair in both]
        else:
            inverses = [
                inverse + mul_pairs(left_pair(inverse), right)
                for inverse, right in zip(inverses, rights)
            ]
    for width in (16, 32, 64):
        beside = (row_index // (2 * width) == col_index // (2 * width)) & (
            row_index // width != col_index // width
        )
        crossed = [
            mul(inverse, jnp.where(beside, strict, 0.0))
            for inverse, strict in zip(inverses, stricts)
        ]
        inverses = [inverse - mul(cross, inverse) for cross, inverse in zip(crossed, inverses)]
    return inverses


def prepare_kernel(place_ref, starts_ref, params_ref, raw0_ref, raw1_ref, taps_ref,
                   rows_out_ref, inv_ref, kkf_ref, p_ref, uw_ref, m_ref, mt_ref, b_ref, r_ref, pu_ref):
    row_index, col_index = iotas()
    diagonal = (row_index == col_index).astype(jnp.float32)
    stricts, kept = [], []
    for member in range(PREPARE_BATCH):
        chunk = pl.program_id(0) * PREPARE_BATCH + member
        starts = start_flags(starts_ref, chunk)
        raw_refs = (raw0_ref, raw1_ref)
        _, pieces = convolved(raw_refs, place_ref, starts, taps_ref, chunk, row_index)
        queries, keys_in, values_in, _, _ = normed_qkv(pieces)
        rows = gate_rows(head_rows(raw_refs, place_ref, chunk, 4), starts, params_ref)
        rows_out_ref[member] = rows
        cols = chunk_cols(rows)
        decay = decay_matrix(rows, cols, starts[1])
        beta, gam, tail = cols[:, 1:2], cols[:, 2:3], cols[:, 3:4]
        scores = mul_t(jnp.concatenate([keys_in, queries], axis=0), keys_in)
        kkf = jnp.where(row_index > col_index, scores[:CHUNK] * decay, 0.0)
        inner = scores[CHUNK:] * decay
        stricts.append(kkf * beta)
        kkf_ref[member] = kkf
        p_ref[member] = inner
        pair = jnp.concatenate([values_in * beta, keys_in * (beta * gam)], axis=1)
        stack = jnp.concatenate([jnp.transpose(keys_in * tail), inner], axis=0)
        kept.append((pair, stack, diagonal * rows[4:5], queries * gam))
    inverses = inverse_lower(stricts)
    joined = [mul(inverse, pair) for inverse, (pair, _, _, _) in zip(inverses, kept)]
    both = [mul(stack, join) for join, (_, stack, _, _) in zip(joined, kept)]
    for member in range(PREPARE_BATCH):
        _, _, span, faded = kept[member]
        inv_ref[member] = inverses[member]
        uw_ref[member] = joined[member]
        state_map = span - both[member][:CHUNK, CHUNK:]
        m_ref[member] = left_pair(state_map)
        mt_ref[member] = left_pair(jnp.transpose(state_map))
        b_ref[member] = both[member][:CHUNK, :CHUNK]
        r_ref[member] = faded - both[member][CHUNK:, CHUNK:]
        pu_ref[member] = both[member][CHUNK:, :CHUNK]


def whole(shape):
    return pl.BlockSpec(shape, lambda *_: (0,) * len(shape))


def per_batch(shape, turned=False, steps=4):
    def place(step, *_):
        return ((steps - 1 - step) if turned else step,) + (0,) * (len(shape) - 1)

    return pl.BlockSpec(shape, place)


def shaped(shape, dtype=jnp.float32):
    return jax.ShapeDtypeStruct(shape, dtype)


def prepare(place, starts, params, raw0, raw1, taps):
    chunks = place.shape[1]
    square = (PREPARE_BATCH, CHUNK, CHUNK)
    wide = (PREPARE_BATCH, CHUNK, 2 * CHUNK)
    kinds = [((PREPARE_BATCH, 8, CHUNK), jnp.float32), (square, jnp.float32), (square, jnp.float32), (square, jnp.float32),
             (wide, jnp.float32), (wide, jnp.bfloat16), (wide, jnp.bfloat16), (square, jnp.float32),
             (square, jnp.float32), (square, jnp.float32)]
    return pl.pallas_call(
        prepare_kernel,
        grid_spec=pltpu.PrefetchScalarGridSpec(
            num_scalar_prefetch=3,
            grid=(chunks // PREPARE_BATCH,),
            in_specs=[whole(raw0.shape), whole(raw1.shape), whole(taps.shape)],
            out_specs=[per_batch(shape) for shape, _ in kinds],
        ),
        out_shape=[shaped((chunks,) + shape[1:], dtype) for shape, dtype in kinds],
        compiler_params=pltpu.CompilerParams(vmem_limit_bytes=VMEM_MAX),
        cost_estimate=spends(18),
        name="prepare",
    )(place, starts, params, raw0, raw1, taps)


def gate_rows_of(gate_refs, place_ref, chunk):
    return head_rows(gate_refs, place_ref, chunk, GATE_ALONE)


def scan_kernel(place_ref, m_ref, b_ref, r_ref, pu_ref, gate0_ref, gate1_ref, gain_ref,
                state_out_ref, core_ref, mixed_ref, state_ref):
    @pl.when(pl.program_id(0) == 0)
    def _():
        state_ref[...] = jnp.zeros_like(state_ref)

    state = state_ref[...]
    for member in range(SCAN_BATCH):
        chunk = pl.program_id(0) * SCAN_BATCH + member
        state_out_ref[member] = state
        pair = right_pair(state)
        core = mul_pairs(left_pair(r_ref[member]), pair) + pu_ref[member]
        state = mul_pairs(m_ref[member], pair) + b_ref[member]
        _, gate = silu_parts(gate_rows_of((gate0_ref, gate1_ref), place_ref, chunk))
        core_ref[member] = core
        scale = lax.rsqrt(jnp.mean(core * core, axis=-1, keepdims=True) + 1e-05)
        mixed = (core * scale * gain_ref[...] * gate).astype(jnp.bfloat16)
        mixed_ref[member] = mixed
    state_ref[...] = state


def gate_columns(raw):
    return pl.BlockSpec((raw.shape[0], CHUNK), lambda *_: (0, 3))


def scan_states(place, m, b, r, pu, raw0, raw1, gain):
    chunks = m.shape[0]
    square = (SCAN_BATCH, CHUNK, CHUNK)
    wide = (SCAN_BATCH, CHUNK, 2 * CHUNK)
    return pl.pallas_call(
        scan_kernel,
        grid_spec=pltpu.PrefetchScalarGridSpec(
            num_scalar_prefetch=1,
            grid=(chunks // SCAN_BATCH,),
            in_specs=[per_batch(wide), per_batch(square), per_batch(square), per_batch(square),
                      gate_columns(raw0), gate_columns(raw1), whole((1, CHUNK))],
            out_specs=[per_batch(square)] * 3,
            scratch_shapes=[pltpu.VMEM((CHUNK, CHUNK), jnp.float32)],
        ),
        out_shape=[shaped((chunks, CHUNK, CHUNK)), shaped((chunks, CHUNK, CHUNK)),
                   shaped((chunks, CHUNK, CHUNK), jnp.bfloat16)],
        compiler_params=pltpu.CompilerParams(vmem_limit_bytes=VMEM_MAX),
        cost_estimate=spends(7),
        name="scan_states",
    )(place, m, b, r, pu, raw0, raw1, gain)


def back_scan_kernel(place_ref, mt_ref, r_ref, core_ref, gate0_ref, gate1_ref, dmixed_ref, gain_ref,
                     dcore_ref, dstate_out_ref, dgate_ref, dgain_ref, dstate_ref):
    step = pl.program_id(0)

    @pl.when(step == 0)
    def _():
        dstate_ref[...] = jnp.zeros_like(dstate_ref)
        dgain_ref[...] = jnp.zeros_like(dgain_ref)

    gain = gain_ref[...]
    dgain = jnp.zeros((8, CHUNK), jnp.float32)
    terms = []
    for member in reversed(range(SCAN_BATCH)):
        chunk = (pl.num_programs(0) - 1 - step) * SCAN_BATCH + member
        core = core_ref[member]
        raw_gate = gate_rows_of((gate0_ref, gate1_ref), place_ref, chunk)
        dmixed = dmixed_ref[member].astype(jnp.float32)
        gate, gated = silu_parts(raw_gate)
        scale = lax.rsqrt(jnp.mean(core * core, axis=-1, keepdims=True) + 1e-05)
        unit = core * scale
        dscaled = dmixed * gated
        dgate = dmixed * unit * gain * (gate * (1.0 + raw_gate * (1.0 - gate)))
        dgate_ref[member] = dgate.astype(jnp.bfloat16)
        product = dscaled * unit
        dgain = dgain + jnp.sum(product.reshape(CHUNK // 8, 8, CHUNK), axis=0)
        dunit = dscaled * gain
        dcore = scale * (dunit - unit * jnp.mean(dunit * unit, axis=-1, keepdims=True))
        dcore_ref[member] = dcore
        terms.append((member, mul(jnp.transpose(r_ref[member]), dcore)))
    dgain_ref[...] += dgain
    dstate = dstate_ref[...]
    for member, term in terms:
        dstate_out_ref[member] = dstate
        dstate = mul_pairs(mt_ref[member], right_pair(dstate)) + term
    dstate_ref[...] = dstate


def back_scan(place, mt, r, core, raw0, raw1, dmixed, gain):
    chunks = mt.shape[0]
    square = (SCAN_BATCH, CHUNK, CHUNK)
    wide = (SCAN_BATCH, CHUNK, 2 * CHUNK)
    turned = partial(per_batch, turned=True, steps=chunks // SCAN_BATCH)
    return pl.pallas_call(
        back_scan_kernel,
        grid_spec=pltpu.PrefetchScalarGridSpec(
            num_scalar_prefetch=1,
            grid=(chunks // SCAN_BATCH,),
            in_specs=[turned(wide), turned(square), turned(square),
                      gate_columns(raw0), gate_columns(raw1), turned(square), whole((1, CHUNK))],
            out_specs=[turned(square), turned(square), turned(square), whole((8, CHUNK))],
            scratch_shapes=[pltpu.VMEM((CHUNK, CHUNK), jnp.float32)],
        ),
        out_shape=[shaped((chunks, CHUNK, CHUNK)), shaped((chunks, CHUNK, CHUNK)),
                   shaped((chunks, CHUNK, CHUNK), jnp.bfloat16), shaped((8, CHUNK))],
        compiler_params=pltpu.CompilerParams(vmem_limit_bytes=VMEM_MAX),
        cost_estimate=spends(7),
        name="back_scan",
    )(place, mt, r, core, raw0, raw1, dmixed, gain)


def lane_sum(value):
    return jnp.sum(value, axis=1, keepdims=True)


def back_kernel(place_ref, starts_ref, params_ref, raw0_ref, raw1_ref, rows_ref, taps_ref, inv_ref, kkf_ref,
                p_ref, uw_ref, state_ref, dstate_ref, dcore_ref, dgate_ref,
                draw0_ref, draw1_ref, dtaps_ref, dparams_ref, next_ref, draw_ref):
    step = pl.program_id(0)
    row_index, col_index = iotas()
    lower = row_index >= col_index
    strict = row_index > col_index

    @pl.when(step == 0)
    def _():
        next_ref[...] = jnp.zeros_like(next_ref)
        dtaps_ref[...] = jnp.zeros_like(dtaps_ref)
        dparams_ref[...] = jnp.zeros_like(dparams_ref)

    raw_refs = (raw0_ref, raw1_ref)
    members = range(BACK_BATCH)
    setups = []
    for member in members:
        chunk = (pl.num_programs(0) - 1 - step) * BACK_BATCH + member
        starts = start_flags(starts_ref, chunk)
        keeps, pieces = convolved(raw_refs, place_ref, starts, taps_ref, chunk, row_index)
        queries, keys_in, values_in, q_scale, k_scale = normed_qkv(pieces)
        rows = rows_ref[member]
        cols = chunk_cols(rows)
        decay = decay_matrix(rows, cols, starts[1])
        setups.append((starts, keeps, pieces, queries, keys_in, values_in, q_scale, k_scale, rows, cols, decay))
    fresh = [
        uw_ref[i][:, :CHUNK] - mul(uw_ref[i][:, CHUNK:], state_ref[i]) for i in members
    ]
    dfresh = [
        mul(jnp.transpose(p_ref[i]), dcore_ref[i])
        + mul(setups[i][4] * setups[i][9][:, 3:4], dstate_ref[i])
        for i in members
    ]
    through = [
        mul_t(jnp.concatenate([dcore_ref[i], dfresh[i]], axis=0), state_ref[i]) for i in members
    ]
    dinner = [jnp.where(lower, mul_t(dcore_ref[i], fresh[i]), 0.0) for i in members]
    dkeys_tail = [mul_t(fresh[i], dstate_ref[i]) for i in members]
    dboth = [
        mul(
            jnp.transpose(inv_ref[i]),
            jnp.concatenate([dfresh[i], -through[i][CHUNK:]], axis=1),
        )
        for i in members
    ]
    dstrict = [jnp.where(strict, -mul_t(dboth[i], uw_ref[i]), 0.0) for i in members]
    stacked, crossed = [], []
    for i in members:
        queries, keys_in, cols, decay = setups[i][3], setups[i][4], setups[i][9], setups[i][10]
        dscores_n = dstrict[i] * decay * cols[:, 1:2]
        dscores = dinner[i] * decay
        stacked.append(
            mul(jnp.concatenate([dscores, dscores_n + jnp.transpose(dscores_n)], axis=0), keys_in)
        )
        crossed.append(mul(jnp.transpose(dscores), queries))
    for i in reversed(members):
        starts, keeps, pieces, queries, keys_in, values_in, q_scale, k_scale, rows, cols, _ = setups[i]
        beta, gam, tail = cols[:, 1:2], cols[:, 2:3], cols[:, 3:4]
        dqueries_faded = through[i][:CHUNK]
        dvalues_beta, dkeys_beta = dboth[i][:, :CHUNK], dboth[i][:, CHUNK:]
        keys_gam = keys_in * gam
        dqueries = stacked[i][:CHUNK] + dqueries_faded * gam
        dkeys = (
            stacked[i][CHUNK:]
            + crossed[i]
            + dkeys_beta * (beta * gam)
            + dkeys_tail[i] * tail
        )
        dvalues = dvalues_beta * beta

        dkkf = dstrict[i] * kkf_ref[i]
        flow = dkkf * beta + dinner[i] * p_ref[i]
        tail_term = lane_sum(dkeys_tail[i] * keys_in * tail)
        dbeta = lane_sum(dkkf + dvalues_beta * values_in + dkeys_beta * keys_gam)
        dsum = (
            lane_sum(flow + (dqueries_faded * queries + dkeys_beta * keys_in * beta) * gam)
            - tail_term
        )
        last = jnp.sum(tail_term) + jnp.sum(state_ref[i] * dstate_ref[i] * rows[4:5, 0:1])
        last_col = jnp.where(row_index[:, :1] == CHUNK - 1, last, 0.0)
        packed = jnp.where(
            col_index == 0, dsum + last_col, jnp.where(col_index == 1, dbeta, 0.0)
        )
        turned = jnp.transpose(packed)[:8]
        flow_rows = jnp.sum(flow, axis=0, keepdims=True)
        kind = row_index[:8]
        dtotal = jnp.where(kind == 0, turned - flow_rows, 0.0)
        dlog = spread_sum(dtotal, lower.astype(jnp.float32))[0:1]
        chunk = (pl.num_programs(0) - 1 - step) * BACK_BATCH + i
        pair = jnp.transpose(head_rows(raw_refs, place_ref, chunk, 4))[:8]
        inside = pair[0:1] + params_ref[1, 0]
        rate = -jnp.exp(params_ref[0, 0] + jnp.zeros((1, CHUNK), jnp.float32))
        dinside = dlog * rate * jax.nn.sigmoid(inside)
        beta_row = rows[1:2]
        dbeta_raw = turned[1:2] * beta_row * (1.0 - beta_row)
        drate = dlog * rate * jax.nn.softplus(inside)
        dparams_ref[...] += jnp.where(kind == 0, drate, jnp.where(kind == 1, dinside, 0.0))
        ddecay = jnp.where(kind == 0, dinside, jnp.where(kind == 1, dbeta_raw, 0.0))
        put_rows(draw_ref, place_ref, chunk, slice(3 * CHUNK, 4 * CHUNK), dgate_ref[i])
        put_rows(
            draw_ref, place_ref, chunk, slice(4 * CHUNK, 5 * CHUNK), chunk_cols(ddecay).astype(jnp.bfloat16)
        )

        d_scaled_q = dqueries * CHUNK ** (-0.5)
        gates = [jax.nn.sigmoid(piece[1]) for piece in pieces]
        unit_q, unit_k = pieces[0][1] * gates[0] * q_scale, pieces[1][1] * gates[1] * k_scale
        dact = [
            q_scale * (d_scaled_q - unit_q * lane_sum(d_scaled_q * unit_q)),
            k_scale * (dkeys - unit_k * lane_sum(dkeys * unit_k)),
            dvalues,
        ]
        for part in range(3):
            rows_by_offset, conv = pieces[part]
            gate = gates[part]
            dconv = dact[part] * (gate * (1.0 + conv * (1.0 - gate)))
            taps = taps_ref[part]
            after = next_ref[part]
            draw = dconv * taps[3:4]
            for offset in range(1, 4):
                kept = jnp.concatenate([dconv * keeps[offset - 1], after], axis=0)
                draw = draw + pltpu.roll(kept, CHUNK + 8 - offset, 0)[:CHUNK] * taps[3 - offset : 4 - offset]
            lanes = slice(part * CHUNK, (part + 1) * CHUNK)
            put_rows(draw_ref, place_ref, chunk, lanes, draw.astype(jnp.bfloat16))
            for offset in range(4):
                dtaps_ref[part, 3 - offset : 4 - offset] += jnp.sum(
                    dconv * rows_by_offset[offset], axis=0, keepdims=True
                )
            next_ref[part] = dconv[:8] * (1.0 - starts[0])

    @pl.when(step == pl.num_programs(0) - 1)
    def _():
        draw0_ref[...] = draw_ref[0]
        draw1_ref[...] = draw_ref[1]


def back(place, starts, params, raw0, raw1, rows, taps, inverse, kkf, inner, joined, states, dstates, dcore, dgate):
    chunks = rows.shape[0]
    square = (BACK_BATCH, CHUNK, CHUNK)
    wide = (BACK_BATCH, CHUNK, 2 * CHUNK)
    turned = partial(per_batch, turned=True, steps=chunks // BACK_BATCH)
    draw = (2,) + raw0.shape
    return pl.pallas_call(
        back_kernel,
        grid_spec=pltpu.PrefetchScalarGridSpec(
            num_scalar_prefetch=3,
            grid=(chunks // BACK_BATCH,),
            in_specs=[whole(raw0.shape), whole(raw1.shape), turned((BACK_BATCH, 8, CHUNK)), whole(taps.shape),
                      turned(square), turned(square), turned(square), turned(wide), turned(square),
                      turned(square), turned(square), turned(square)],
            out_specs=[whole(raw0.shape), whole(raw0.shape), whole((3, 4, CHUNK)), whole((8, CHUNK))],
            scratch_shapes=[pltpu.VMEM((3, 8, CHUNK), jnp.float32), pltpu.VMEM(draw, jnp.bfloat16)],
        ),
        out_shape=[shaped(raw0.shape, jnp.bfloat16)] * 2 + [shaped((3, 4, CHUNK)), shaped((8, CHUNK))],
        compiler_params=pltpu.CompilerParams(vmem_limit_bytes=VMEM_MAX),
        cost_estimate=spends(24),
        name="back",
    )(place, starts, params, raw0, raw1, rows, taps, inverse, kkf, inner, joined, states, dstates, dcore, dgate)


def document_starts(doc_lengths, block_count):
    bounds = jnp.cumsum(doc_lengths)[:-1]
    blocks = jnp.arange(block_count, dtype=jnp.int32)
    opens = jnp.any(blocks[:, None] == bounds[None, :], axis=1) | (blocks == 0)
    return opens.astype(jnp.int32)


def mixer_forward(place, prepared, raw0, raw1, out_gain):
    rows, inverse, kkf, inner, joined, m, mt, b, r, pu = prepared
    states, core, mixed = scan_states(place, m, b, r, pu, raw0, raw1, out_gain)
    return mixed, (rows, inverse, kkf, inner, joined, mt, r, states, core)


def mixer_backward_scan(place, raw0, raw1, out_gain, kept, dmixed):
    mt, r, core = kept[5], kept[6], kept[8]
    return back_scan(place, mt, r, core, raw0, raw1, dmixed, out_gain)


def mixer_backward(place, starts, params, raw0, raw1, taps, kept, dstates, dcore, dgate):
    rows, inverse, kkf, inner, joined, _, _, states, _ = kept
    return back(
        place, starts, params, raw0, raw1, rows, taps, inverse, kkf, inner, joined, states, dstates, dcore, dgate
    )


from jax.sharding import PartitionSpec as P

LANES = 128
HALF = 384
GROUP = 256
SIDE = 64


def exchange_perm(count, shifted, sizes):
    pairs = []
    for target in range(count):
        source, scale, rest = 0, 1, target
        for size, offset in zip(reversed(sizes), reversed(shifted)):
            source += (rest % size + offset) % size * scale
            rest //= size
            scale *= size
        pairs.append((source, target))
    return pairs


def from_head(value, dz=0, dx=0, dc=0):
    return lax.ppermute(value, "head", exchange_perm(16, (dz, dx, dc), (4, 2, 2)))


def from_dp(value, dy=0, dx=0):
    return lax.ppermute(value, "dp", exchange_perm(8, (dy, dx), (4, 2)))


def after(value, *earlier):
    return lax.optimization_barrier((value,) + earlier)[0]


def gather_turn(value, cut, beside=()):
    first, second = value[:cut], value[cut:]
    arrived = [take_zx(first, 0, 1)] + [take_zx(second, k, 0) for k in (1, 2, 3)]
    arrived = lax.optimization_barrier(tuple(arrived) + tuple(beside))
    pair = jnp.concatenate([first, arrived[0]], axis=0)
    column = jnp.concatenate([second, *arrived[1:4]], axis=0)
    return lax.optimization_barrier((pair, column))


def gather_end(pair, column):
    return [pair] + [take_zx(pair, k, 0) for k in (1, 2, 3)], [column, take_zx(column, 0, 1)]


def take_zx(value, ring, side):
    return from_head(value, dz=ring, dx=side)


def take_yx(value, ring, side):
    return from_dp(value, dy=ring, dx=side)


def wide(value):
    return value.astype(jnp.float32)


def narrow(value):
    return value.astype(jnp.bfloat16)


def sum_rows(pieces, rows):
    total = wide(pieces[0][rows])
    for piece in pieces[1:]:
        total = total + wide(piece[rows])
    return total


def reduce_arrivals(rounds, far, beside=()):
    arrived = [take_zx(rounds[k - 1], -k, 0) for k in (1, 2, 3)] + [take_zx(far, 0, 1)]
    return lax.optimization_barrier(tuple(arrived) + tuple(beside))[:4], arrived[0]


def turn_sum_kernel(*refs):
    rounds, sides, outs = refs[:4], refs[4:6], refs[6:]
    cut = rounds[0].shape[0] // 2
    early, late = slice(0, cut), slice(cut, None)
    total = wide(rounds[0][...])
    for ref in rounds[1:]:
        total = total + wide(ref[...])
    outs[0][...] = total[early]
    outs[1][...] = narrow(total[late])
    total = wide(sides[0][...]) + wide(sides[1][...])
    rest = total.shape[0] // 4
    outs[2][...] = total[:rest]
    for k in (1, 2, 3):
        outs[2 + k][...] = narrow(total[rest * k : rest * (k + 1)])


def reduce_parts(first, near, arrived):
    width = first.shape[1]
    cut, rest = (first.shape[0] // 2, width), (near.shape[0] // 4, width)
    outs = [shaped(cut), shaped(cut, jnp.bfloat16), shaped(rest)] + [shaped(rest, jnp.bfloat16)] * 3
    return whole_call(turn_sum_kernel, outs, "turn_sum", (), first, *arrived[:3], near, arrived[3])


def small_kernel(gain1_ref, gain2_ref, out_gain_ref, params_ref, taps_ref, out_grad_ref, sent_ref, rows_ref):
    for row in range(8):
        for half in range(2):
            lanes = slice(half * LANES, (half + 1) * LANES)
            place = 2 * row + half
            rows_ref[place : place + 1] = gain1_ref[row, 0:1, lanes]
            rows_ref[16 + place : 17 + place] = gain2_ref[:, place * LANES : (place + 1) * LANES]
    rows_ref[32:40] = out_gain_ref[...]
    rows_ref[40:48] = params_ref[...]
    for part in range(3):
        rows_ref[48 + 4 * part : 52 + 4 * part] = taps_ref[part]
    rows_ref[60:] = jnp.zeros_like(rows_ref[60:])
    small = rows_ref[...]
    high, rest = split(small)
    low = narrow(small - wide(high) - wide(rest))
    pieces = jnp.concatenate([high, rest, low], axis=0)
    for target in range(8):
        sent_ref[target, :GROUP] = out_grad_ref[target]
        sent_ref[target, GROUP:] = pieces


def side_sum_kernel(near_ref, crossed_ref, *out_refs):
    for k, out_ref in enumerate(out_refs):
        for half in range(2):
            rows = slice(SIDE * (4 * half + k), SIDE * (4 * half + k + 1))
            total = wide(near_ref[rows]) + wide(crossed_ref[rows])
            out_ref[SIDE * half : SIDE * (half + 1)] = total if k == 0 else narrow(total)


def ring_sum_kernel(over_ref, arrived_ref, kept_ref, sent_ref):
    half = kept_ref.shape[0]
    for target, side in ((kept_ref, over_ref[0]), (sent_ref, 1 - over_ref[0])):
        rows = pl.ds(pl.multiple_of(side * half, 16), half)
        total = wide(arrived_ref[0, rows])
        for source in (1, 2, 3):
            total = total + wide(arrived_ref[source, rows])
        target[...] = total.astype(target.dtype)


def reduce_end(parts):
    return (parts[0], take_zx(parts[1], 0, 1), parts[2]) + tuple(
        take_zx(parts[2 + k], -k, 0) for k in (1, 2, 3)
    )


RINGS = [[0, 2, 4, 6], [1, 3, 5, 7]]


def pair_kernel(over_ref, value_ref, mate_ref, *out_refs):
    rows, start = value_ref.shape[0], 0
    for out_ref in out_refs:
        lanes = slice(start, start + out_ref.shape[1])
        start = lanes.stop
        for source, place in ((value_ref, over_ref[0]), (mate_ref, 1 - over_ref[0])):
            out_ref[pl.ds(pl.multiple_of(place * rows, 16), rows)] = source[:, lanes]


def ordered_pair(value, mate):
    over = (lax.axis_index("dp") % 2)[None].astype(jnp.int32)
    outs = [shaped((2 * value.shape[0], columns), value.dtype) for columns in (2 * HALF, HALF)]
    return whole_call(pair_kernel, outs, "ordered_pair", (over,), value, mate)


def ordered_join_kernel(up_ref, *refs):
    sources, target, sems = refs[:4], refs[4], refs[5]
    rows = sources[0].shape[0]
    copies = []
    for k, ref in enumerate(sources):
        place = lax.rem(up_ref[0] + k, 4)
        copies.append(
            pltpu.make_async_copy(ref, target.at[pl.ds(pl.multiple_of(place * rows, 16), rows)], sems.at[k])
        )
        copies[-1].start()
    for copy in copies:
        copy.wait()


def ordered_join(pieces):
    anywhere = pl.BlockSpec(memory_space=pl.ANY)
    rows, columns = pieces[0].shape
    return pl.pallas_call(
        ordered_join_kernel,
        grid_spec=pltpu.PrefetchScalarGridSpec(
            num_scalar_prefetch=1,
            grid=(1,),
            in_specs=[anywhere] * 4,
            out_specs=whole((4 * rows, columns)),
            scratch_shapes=[pltpu.SemaphoreType.DMA((4,))],
        ),
        out_shape=shaped((4 * rows, columns), pieces[0].dtype),
        compiler_params=pltpu.CompilerParams(vmem_limit_bytes=VMEM_MAX),
        cost_estimate=spends(4),
        name="ordered_join",
    )((lax.axis_index("dp") // 2)[None].astype(jnp.int32), *pieces)


def spread_kernel(over_ref, *refs):
    over, out_ref = over_ref[0], refs[-1]
    count = (len(refs) - 1) // 2
    for place in range(count):
        lanes = slice(place * HALF, (place + 1) * HALF)
        out_ref[0, over, :, lanes] = refs[place][...]
        out_ref[0, 1 - over, :, lanes] = refs[count + place][...]


def spread_pair(value, mate):
    rows, columns = value.shape
    count = columns // HALF
    blocks = [held((rows, HALF), lambda *_, place=place: (0, place)) for place in range(count)]
    return pl.pallas_call(
        spread_kernel,
        grid_spec=pltpu.PrefetchScalarGridSpec(
            num_scalar_prefetch=1,
            grid=(4,),
            in_specs=blocks * 2,
            out_specs=pl.BlockSpec((1, 2, rows, columns), lambda turn, *_: (turn, 0, 0, 0)),
        ),
        out_shape=shaped((4, 2, rows, columns), value.dtype),
        compiler_params=pltpu.CompilerParams(vmem_limit_bytes=VMEM_MAX),
        cost_estimate=spends(3),
        name="spread_pair",
    )((lax.axis_index("dp") % 2)[None].astype(jnp.int32), *[value] * count, *[mate] * count)


def round_ring(spread):
    everything = lax.all_to_all(spread, "dp", 0, 0, tiled=False, axis_index_groups=RINGS)
    return everything.reshape(8 * spread.shape[2], spread.shape[3])


def ring_parts(arrived):
    over = (lax.axis_index("dp") % 2)[None].astype(jnp.int32)
    half = (arrived.shape[1] // 2, arrived.shape[2])
    return whole_call(ring_sum_kernel, [shaped(half), shaped(half, jnp.bfloat16)], "ring_sum", (over,), arrived)


def exchange_ring(value):
    return lax.all_to_all(value, "dp", 0, 0, tiled=False, axis_index_groups=RINGS)


def sum_all(value, axis, count):
    spread = jnp.broadcast_to(value, (count,) + value.shape)
    return jnp.sum(lax.all_to_all(spread, axis, 0, 0, tiled=False), axis=0)


def whole_call(kernel, out_shape, name, scalars, *arrays, scratch=()):
    outs = out_shape if isinstance(out_shape, (list, tuple)) else [out_shape]
    return pl.pallas_call(
        kernel,
        grid_spec=pltpu.PrefetchScalarGridSpec(
            num_scalar_prefetch=len(scalars),
            grid=(1,),
            in_specs=[whole(array.shape) for array in arrays],
            out_specs=[whole(out.shape) for out in outs],
            scratch_shapes=list(scratch),
        ),
        out_shape=list(outs),
        compiler_params=pltpu.CompilerParams(vmem_limit_bytes=VMEM_MAX),
        cost_estimate=spends(3),
        name=name,
    )(*scalars, *arrays)


def rms_parts(values):
    scale = lax.rsqrt(jnp.mean(values * values, axis=-1, keepdims=True) + 1e-05)
    return scale, values * scale


def rms_back(grad, gain, scale, unit):
    inner = grad * gain
    return scale * (inner - unit * jnp.mean(inner * unit, axis=-1, keepdims=True))


def enter_kernel(tokens_ref, gain_ref, normed_ref):
    _, unit = rms_parts(wide(tokens_ref[...]))
    normed_ref[...] = narrow(unit * gain_ref[...])


def project_kernel(own_ref, other_ref, weights_ref, own_out_ref, other_out_ref):
    step = pl.program_id(0)
    half = pl.num_programs(0) // 2

    @pl.when(step < half)
    def _():
        own_out_ref[...] = plain_product(own_ref[...], weights_ref[...])

    @pl.when(step >= half)
    def _():
        other_out_ref[...] = plain_product(other_ref[...], weights_ref[...])


def project(own, other, weights, columns):
    count, width = own.shape
    step = 512
    half = count // step

    def early(size):
        return pl.BlockSpec((step, size), lambda i: (jnp.minimum(i, half - 1), 0))

    def late(size):
        return pl.BlockSpec((step, size), lambda i: (jnp.maximum(i - half, 0), 0))

    return pl.pallas_call(
        project_kernel,
        grid=(2 * half,),
        in_specs=[early(width), late(width), held((width, columns))],
        out_specs=[early(columns), late(columns)],
        out_shape=[shaped((count, columns))] * 2,
        compiler_params=pltpu.CompilerParams(vmem_limit_bytes=VMEM_MAX),
        cost_estimate=spends(5),
        name="project",
    )(own, other, weights)


def unproject_kernel(own_ref, far_ref, weights_ref, far_weights_ref, *piece_refs):
    step = pl.program_id(0)
    total = against(own_rows(own_ref, step), weights_ref[...]) + against(
        own_rows(far_ref, step), far_weights_ref[...]
    )
    put_pieces(narrow(total), piece_refs, step)


def unproject(own, far, weights, far_weights, piece_shapes):
    used = held((weights.shape[0], own.shape[1]))
    return pl.pallas_call(
        unproject_kernel,
        grid=(4,),
        in_specs=[held(own.shape), held(far.shape), used, used],
        out_specs=[whole(shape) for shape in piece_shapes],
        out_shape=[shaped(shape, jnp.bfloat16) for shape in piece_shapes],
        compiler_params=pltpu.CompilerParams(vmem_limit_bytes=VMEM_MAX),
        cost_estimate=spends(8),
        name="unproject",
    )(own, far, weights, far_weights)


def feed_grad_kernel(*refs):
    own_ref, far_ref = refs[8:]
    gate_up, down = 0.0, 0.0
    for normed_ref, cot_ref, dpre_ref, hidden_ref in (refs[:4], refs[4:8]):
        gate_up = gate_up + over_rows(normed_ref[...], dpre_ref[...])
        down = down + over_rows(cot_ref[...], hidden_ref[...])
    gate_up, down = narrow(gate_up), narrow(down)
    own_ref[:, : 2 * HALF] = gate_up[:, : 2 * HALF]
    far_ref[:, : 2 * HALF] = gate_up[:, 2 * HALF :]
    own_ref[:, 2 * HALF :] = down[:, :HALF]
    far_ref[:, 2 * HALF :] = down[:, HALF:]


def feed_grads(*parts):
    arrays, specs = [], []
    width = parts[0][2].shape[1]
    for hidden, dpre, normed, cot in parts:
        rows = pl.BlockSpec((normed.shape[0], GROUP), lambda i: (0, i))
        arrays += [normed, cot, dpre, hidden]
        specs += [rows, rows, held(dpre.shape), held(hidden.shape)]
    out = pl.BlockSpec((GROUP, 3 * HALF), lambda i: (i, 0))
    return pl.pallas_call(
        feed_grad_kernel,
        grid=(width // GROUP,),
        in_specs=specs,
        out_specs=[out, out],
        out_shape=[shaped((width, 3 * HALF), jnp.bfloat16)] * 2,
        compiler_params=pltpu.CompilerParams(vmem_limit_bytes=VMEM_MAX),
        cost_estimate=spends(12),
        name="feed_grads",
    )(*arrays)


def in_grad_kernel(own_ref, other_ref, draw0_ref, draw1_ref, weights_ref, gain_ref, out_ref, part_ref):
    grad = narrow(over_rows(own_ref[...], draw0_ref[...]) + over_rows(other_ref[...], draw1_ref[...]))
    out_ref[0] = grad
    product = wide(grad) * wide(weights_ref[...])
    lanes = product[:, :LANES]
    for start in range(LANES, product.shape[1], LANES):
        lanes = lanes + product[:, start : start + LANES]
    part = jnp.sum(jnp.transpose(lanes), axis=0, keepdims=True) / gain_ref[...]
    part_ref[0] = jnp.broadcast_to(part, part_ref.shape[1:])


def in_grads(own, other, draw0, draw1, weights, gain):
    count, width = own.shape
    used = draw0.shape[1]
    rows = pl.BlockSpec((count, GROUP), lambda i: (0, i))
    grad, part = pl.pallas_call(
        in_grad_kernel,
        grid=(width // GROUP,),
        in_specs=[rows, rows, held(draw0.shape), held(draw1.shape),
                  pl.BlockSpec((GROUP, used), lambda i: (i, 0)), pl.BlockSpec((1, GROUP), lambda i: (0, i))],
        out_specs=[pl.BlockSpec((1, GROUP, used), lambda i: (i // 2, i % 2, 0)),
                   pl.BlockSpec((1, 8, GROUP), lambda i: (i, 0, 0))],
        out_shape=[shaped((4, 2 * GROUP, used), jnp.bfloat16), shaped((width // GROUP, 8, GROUP))],
        compiler_params=pltpu.CompilerParams(vmem_limit_bytes=VMEM_MAX),
        cost_estimate=spends(8),
        name="in_grads",
    )(own, other, draw0, draw1, weights, gain)
    return grad, part


def out_grad_kernel(rows_ref, mixed_ref, out_ref):
    out_ref[0] = narrow(over_rows(rows_ref[...], mixed_ref[...]))


def out_grads(rows, mixed):
    count, width = rows.shape
    return pl.pallas_call(
        out_grad_kernel,
        grid=(width // GROUP,),
        in_specs=[pl.BlockSpec((count, GROUP), lambda i: (0, i)), held(mixed.shape)],
        out_specs=pl.BlockSpec((1, GROUP, mixed.shape[1]), lambda i: (i, 0, 0)),
        out_shape=shaped((width // GROUP, GROUP, mixed.shape[1]), jnp.bfloat16),
        compiler_params=pltpu.CompilerParams(vmem_limit_bytes=VMEM_MAX),
        cost_estimate=spends(6),
        name="out_grads",
    )(rows, mixed)


def own_rows(ref, step):
    first = pl.ds(pl.multiple_of(step * 2 * ROWS_A, 16), 2 * ROWS_A)
    near = pl.ds(pl.multiple_of(8 * ROWS_A + step * ROWS_B, 16), ROWS_B)
    far = pl.ds(pl.multiple_of(8 * ROWS_A + 4 * ROWS_B + step * ROWS_B, 16), ROWS_B)
    return jnp.concatenate([ref[first], ref[near], ref[far]], axis=0)


def put_pieces(total, piece_refs, step):
    side = pl.ds(pl.multiple_of(step * ROWS_B, 16), ROWS_B)
    for k in range(4):

        @pl.when(step == k)
        def _(k=k):
            piece_refs[k][...] = total[: 2 * ROWS_A]

    piece_refs[4][side] = total[2 * ROWS_A : 2 * ROWS_A + ROWS_B]
    piece_refs[5][side] = total[2 * ROWS_A + ROWS_B :]


def attn_kernel(heads_ref, mixed_ref, *refs):
    weight_refs, (rows_ref, gain_ref, resid_ref, normed_ref, total_ref) = refs[:4], refs[4:]
    step = pl.program_id(0)

    @pl.when(step == 0)
    def _():
        total_ref[...] = wide(rows_ref[...])

    mixed = jnp.concatenate([mixed_ref[heads_ref[i % 2, 2 * step + i // 2]] for i in range(4)], axis=1)
    total_ref[...] += against(mixed, jnp.concatenate([ref[0] for ref in weight_refs], axis=1))

    @pl.when(step == pl.num_programs(0) - 1)
    def _():
        resid = total_ref[...]
        resid_ref[...] = resid
        _, unit = rms_parts(resid)
        normed_ref[...] = narrow(unit * gain_ref[...])


def out_weight_specs(out_heads):
    shape = (1,) + out_heads.shape[1:]
    return [
        pl.BlockSpec(shape, lambda step, heads_ref, i=i: (heads_ref[i % 2, 2 * step + i // 2], 0, 0))
        for i in range(4)
    ]


def attend(heads, received, out_heads, rows, gain):
    shape = rows.shape
    return pl.pallas_call(
        attn_kernel,
        grid_spec=pltpu.PrefetchScalarGridSpec(
            num_scalar_prefetch=1,
            grid=(4,),
            in_specs=[whole(received.shape)] + out_weight_specs(out_heads) + [whole(shape), whole(gain.shape)],
            out_specs=[whole(shape), whole(shape)],
            scratch_shapes=[pltpu.VMEM(shape, jnp.float32)],
        ),
        out_shape=[shaped(shape), shaped(shape, jnp.bfloat16)],
        compiler_params=pltpu.CompilerParams(vmem_limit_bytes=VMEM_MAX),
        cost_estimate=spends(10),
        name="attend",
    )(heads, received, *[out_heads] * 4, rows, gain)


def total_of(refs):
    first = refs[0][...] + wide(refs[1][...])
    second = refs[2][...] + wide(refs[3][...]) + wide(refs[4][...]) + wide(refs[5][...])
    return jnp.concatenate([first, second], axis=0)


def middle_kernel(heads_ref, *refs):
    pieces, (resid_ref, cot_ref, gain_ref), weight_refs = refs[:6], refs[6:9], refs[9:13]
    dresid_ref, dattn_ref, dgain_ref, dmixed_ref = refs[13:]
    step = pl.program_id(0)

    @pl.when(step == 0)
    def _():
        grad = total_of(pieces)
        scale, unit = rms_parts(resid_ref[...])
        dgain_ref[...] = jnp.sum(grad * unit, axis=0, keepdims=True)
        dresid = wide(cot_ref[...]) + rms_back(grad, gain_ref[...], scale, unit)
        dresid_ref[...] = dresid
        dattn_ref[...] = narrow(dresid)

    weights = jnp.concatenate([ref[0] for ref in weight_refs], axis=1)
    total = narrow(plain_product(dattn_ref[...], weights))
    for i in range(4):
        dmixed_ref[heads_ref[i % 2, 2 * step + i // 2]] = total[:, i * LANES : (i + 1) * LANES]


def middle(heads, pieces, resid, cot, gain, out_heads):
    shape = resid.shape
    mixed_shape = (16, shape[0], LANES)
    return pl.pallas_call(
        middle_kernel,
        grid_spec=pltpu.PrefetchScalarGridSpec(
            num_scalar_prefetch=1,
            grid=(4,),
            in_specs=[whole(piece.shape) for piece in pieces]
            + [whole(shape), whole(shape), whole(gain.shape)]
            + out_weight_specs(out_heads),
            out_specs=[whole(shape), whole(shape), whole((1, shape[1])), whole(mixed_shape)],
        ),
        out_shape=[shaped(shape), shaped(shape, jnp.bfloat16), shaped((1, shape[1])),
                   shaped(mixed_shape, jnp.bfloat16)],
        compiler_params=pltpu.CompilerParams(vmem_limit_bytes=VMEM_MAX),
        cost_estimate=spends(10),
        name="middle",
    )(heads, *pieces, resid, cot, gain, *[out_heads] * 4)


def leave_kernel(*refs):
    total = refs[0][...] + refs[4][...]
    for ref in refs[1:4]:
        total = total + wide(ref[...])
    refs[5][...] = narrow(total)


def finish_kernel(*refs):
    pieces, (rows_ref, dresid_ref, gain_ref, out_ref) = refs[:6], refs[6:]
    scale, unit = rms_parts(wide(rows_ref[...]))
    out_ref[...] = dresid_ref[...] + rms_back(total_of(pieces), gain_ref[...], scale, unit)


def feed_kernel(halves, count, joins, heads_ref, *refs):
    normed_refs, refs = refs[:count], refs[count:]
    cot_refs, refs = refs[: len(halves)], refs[len(halves) :]
    weight_refs, refs = refs[:4], refs[4:]
    earlier_refs, refs = refs[: 2 * joins], refs[2 * joins :]
    fed_refs, dnormed_refs, refs = refs[:2], refs[2 : 2 + count], refs[2 + count :]
    hidden_ref, dpre_ref, normed_out_ref, cot_out_ref, normed_ref, cot_ref, out_ref, grad_ref = refs
    step, last = pl.program_id(0), pl.num_programs(0) - 1
    size = hidden_ref.shape[0]

    @pl.when(step == 0)
    def _():
        start = 0
        for ref in normed_refs:
            normed_ref[start : start + ref.shape[0]] = ref[...]
            start += ref.shape[0]
        for place, ref in enumerate(cot_refs):
            cot_ref[SIDE * place : SIDE * (place + 1)] = ref[...]

    rows = pl.ds(pl.multiple_of(step * size, 16), size)
    normed, cot = normed_ref[rows], cot_ref[rows]
    normed_out_ref[...] = normed
    cot_out_ref[...] = cot
    out, dnormed = 0.0, 0.0
    for half in range(2):
        gu_ref, down_ref = weight_refs[2 * half], weight_refs[2 * half + 1]
        pre = plain_product(normed, gu_ref[...])
        gate, up = pre[:, :HALF], pre[:, HALF:]
        dhidden = plain_product(cot, down_ref[...])
        sigmoid = jax.nn.sigmoid(gate)
        act = gate * sigmoid
        hidden = narrow(act * up)
        dgate = narrow(dhidden * up * sigmoid * (1.0 + gate * (1.0 - sigmoid)))
        dpre = jnp.concatenate([dgate, narrow(dhidden * act)], axis=1)
        hidden_ref[:, half * HALF : (half + 1) * HALF] = hidden
        dpre_ref[:, 2 * half * HALF : 2 * (half + 1) * HALF] = dpre
        out = out + against(hidden, down_ref[...])
        dnormed = dnormed + against(dpre, gu_ref[...])
    out_ref[rows] = narrow(out)
    grad_ref[rows] = narrow(dnormed)

    @pl.when(step == last)
    def _():
        start = 0
        for ref in dnormed_refs:
            ref[...] = grad_ref[start : start + ref.shape[0]]
            start += ref.shape[0]
        if joins:
            near_ref, far_ref = fed_refs
            for k in range(4):
                first = earlier_refs[0] if k == 0 else out_ref.at[2 * SIDE * (k - 1) : 2 * SIDE * k]
                near_ref[SIDE * k : SIDE * (k + 1)] = first[:SIDE]
                far_ref[SIDE * k : SIDE * (k + 1)] = first[SIDE:]
            near_ref[4 * SIDE :] = earlier_refs[1][...]
            far_ref[4 * SIDE :] = out_ref[6 * SIDE :]
        else:
            fed_refs[0][...] = out_ref[: 2 * SIDE]
            fed_refs[1][...] = out_ref[2 * SIDE :]


def held(shape, place=None):
    place = place or (lambda *_: (0,) * len(shape))
    return pl.BlockSpec(shape, place, pipeline_mode=pl.Buffered(1))


def feed(heads, pieces, halves, cot, own, other, steps, earlier=()):
    width = cot.shape[1]
    shapes = [piece.shape for piece in pieces]
    count = sum(shape[0] for shape in shapes)
    size = count // steps
    gate_up, down = held((width, 2 * HALF)), held((width, HALF))

    def half_block(slot, half):
        return held((SIDE, width), lambda i, heads_ref: (2 * heads_ref[0, slot] + half, 0))

    fed_shapes = [(8 * SIDE, width)] * 2 if earlier else shapes
    row_widths = (2 * HALF, 4 * HALF, width, width)
    outs = pl.pallas_call(
        partial(feed_kernel, tuple(halves), len(pieces), bool(earlier)),
        grid_spec=pltpu.PrefetchScalarGridSpec(
            num_scalar_prefetch=1,
            grid=(steps,),
            in_specs=[held(shape) for shape in shapes]
            + [half_block(*half) for half in halves]
            + [gate_up, down, gate_up, down]
            + [held(piece.shape) for piece in earlier],
            out_specs=[whole(shape) for shape in fed_shapes + shapes]
            + [pl.BlockSpec((size, part), lambda i, *_: (i, 0)) for part in row_widths],
            scratch_shapes=[pltpu.VMEM((count, width), jnp.bfloat16)] * 4,
        ),
        out_shape=[shaped(shape, jnp.bfloat16) for shape in fed_shapes + shapes]
        + [shaped((count, part), jnp.bfloat16) for part in row_widths],
        compiler_params=pltpu.CompilerParams(vmem_limit_bytes=VMEM_MAX),
        cost_estimate=spends(28),
        name="feed",
    )(heads, *pieces, *[cot] * len(halves), *own, *other, *earlier)
    feds = len(fed_shapes)
    return outs[:feds], outs[feds : feds + len(shapes)], outs[feds + len(shapes) :]


def join_kernel(*refs):
    sources, target, sems = refs[:-2], refs[-2], refs[-1]
    copies, start = [], 0
    for place, ref in enumerate(sources):
        copies.append(pltpu.make_async_copy(ref, target.at[pl.ds(start, ref.shape[0])], sems.at[place]))
        copies[-1].start()
        start += ref.shape[0]
    for copy in copies:
        copy.wait()


def join(pieces):
    anywhere = pl.BlockSpec(memory_space=pl.ANY)
    rows = sum(piece.shape[0] for piece in pieces)
    return pl.pallas_call(
        join_kernel,
        in_specs=[anywhere] * len(pieces),
        out_specs=pl.BlockSpec(memory_space=pltpu.VMEM),
        out_shape=shaped((rows, pieces[0].shape[1]), pieces[0].dtype),
        scratch_shapes=[pltpu.SemaphoreType.DMA((len(pieces),))],
        compiler_params=pltpu.CompilerParams(vmem_limit_bytes=VMEM_MAX),
        cost_estimate=spends(3),
        name="join",
    )(*pieces)


def plain_product(left, right):
    return jnp.dot(left, right, preferred_element_type=jnp.float32)


def against(left, right):
    return lax.dot_general(left, right, (((1,), (1,)), ((), ())), preferred_element_type=jnp.float32)


def over_rows(left, right):
    return lax.dot_general(left, right, (((0,), (0,)), ((), ())), preferred_element_type=jnp.float32)


def tables():
    head = lax.axis_index("head")
    ring, side, core = head // 4, head // 2 % 2, head % 2
    chunk = jnp.arange(16, dtype=jnp.int32)
    dz, dx, dc = (chunk // 4 - ring) % 4, (chunk // 2 + side) % 2, (chunk + core) % 2
    place = jnp.stack([ROWS_A * (2 * dz + dx), 8 * ROWS_A + ROWS_B * (4 * dx + dz), dc]).astype(jnp.int32)
    step = jnp.arange(8, dtype=jnp.int32)
    chip = ((step + ring) % 4) * 2 + (step // 4 + side) % 2
    heads = jnp.stack([2 * chip + core, 2 * chip + 1 - core]).astype(jnp.int32)
    return place, heads


def body(
    tokens,
    cotangent,
    doc_spans,
    norm1_gain,
    q_weight,
    k_weight,
    v_weight,
    gate_out_weight,
    decay_weight,
    conv_weight,
    gate_params,
    out_gain,
    out_weight,
    norm2_gain,
    gate_weight,
    up_weight,
    down_weight,
):
    place, heads = tables()
    starts = document_starts(doc_spans[0], 32)
    out_gain_row = out_gain[None, :]
    gain1_row, gain2_row = norm1_gain[None, :], norm2_gain[None, :]
    rows_shape = tokens.shape
    width = rows_shape[1]

    def pad(weight, columns):
        return jnp.pad(weight, ((0, 0), (0, columns - weight.shape[1])))

    (normed1,) = whole_call(enter_kernel, shaped(rows_shape, jnp.bfloat16), "enter", (), tokens, gain1_row)

    packed = (conv_weight, decay_weight, q_weight, k_weight, v_weight, gate_out_weight, out_weight)
    conv_now, decay_now, *square_now = lax.optimization_barrier(packed + (normed1,))[:7]
    taps_block = jnp.pad(conv_now.reshape(12, 16), ((0, GROUP - 12), (0, 0)))
    side_block = pad(jnp.concatenate([decay_now[:, 0], taps_block], axis=1), LANES)
    pack_one = jnp.concatenate(square_now[:4] + [side_block] + square_now[4:], axis=1)
    wide_now = lax.optimization_barrier((gate_weight, up_weight, down_weight, normed1))[:3]
    pack_two = jnp.concatenate([pad(weight, HALF) for weight in wide_now], axis=1)
    cut, used = pack_one.shape[1], 5 * LANES

    mate_one = take_yx(pack_one, 0, 1)
    pair, column = gather_turn(normed1, ROWS_A, beside=(mate_one, pack_two))
    pair, column, mate_one = lax.optimization_barrier((pair, column, mate_one))
    mate_two = take_yx(after(pack_two, mate_one), 0, 1)
    mine_one = round_ring(spread_pair(pack_one, mate_one))
    rings, columns = gather_end(pair, column)
    rings, columns, mine_one, mate_two = lax.optimization_barrier((rings, columns, mine_one, mate_two))
    pair_gu, pair_down = ordered_pair(pack_two, mate_two)
    normed1_own = join(rings + columns)
    normed1_other = from_head(normed1_own, dc=1)
    raw0, raw1 = project(normed1_own, normed1_other, mine_one, used)
    taps = mine_one.reshape(8, GROUP, cut)[:, :12, 4 * LANES + 2 : 4 * LANES + 18]
    taps = wide(taps.transpose(1, 0, 2).reshape(3, 4, LANES))

    gu_arrived = [take_yx(pair_gu, k, 0) for k in (1, 2, 3)]

    out_heads = lax.all_gather(mine_one[:, used:], "head")
    prepared = prepare(place, starts, gate_params, raw0, raw1, taps)
    mixed, kept = mixer_forward(place, prepared, raw0, raw1, out_gain_row)
    mixed, gu_arrived, out_heads, pair_down = lax.optimization_barrier((mixed, gu_arrived, out_heads, pair_down))
    down_arrived = [take_yx(pair_down, k, 0) for k in (1, 2, 3)]
    cot_group = lax.all_gather(after(cotangent, out_heads), "head", axis=0, tiled=True)
    received = lax.all_to_all(mixed, "head", 0, 0, tiled=False)
    resid, normed2 = attend(heads, received, out_heads, tokens, gain2_row)
    gu_arrived, down_arrived = lax.optimization_barrier((gu_arrived, down_arrived, normed2))[:2]
    own_two = (ordered_join([pair_gu, *gu_arrived]), ordered_join([pair_down, *down_arrived]))
    pair, column = gather_turn(normed2, SIDE, beside=own_two)
    other_two = tuple(from_head(after(weights, pair), dc=1) for weights in own_two)
    rings, columns = gather_end(pair, column)
    near_halves = [(0, 0), (4, 0)] + [(k, 1) for k in range(4)]
    far_halves = [half for k in (1, 2, 3) for half in ((k, 0), (4 + k, 0))] + [(4 + k, 1) for k in range(4)]
    fed_early, (dpair, dnear), kept_near = feed(
        heads, [pair, column], near_halves, cot_group, own_two, other_two, 1
    )
    rings, columns, dpair = lax.optimization_barrier((rings, columns, dpair))
    (fed_near, fed_far), (*drings, dfar), kept_far = feed(
        heads, rings[1:] + columns[1:], far_halves, cot_group, own_two, other_two, 2, fed_early
    )

    parts = reduce_parts(dpair, dnear, reduce_arrivals(drings, dfar)[0])
    feed_own, feed_other = feed_grads(kept_near, kept_far)
    parts, feed_own, feed_other = lax.optimization_barrier((parts, feed_own, feed_other))
    feed_grad = narrow(wide(feed_own) + wide(from_head(feed_other, dc=1)))
    dnormed2_pieces = reduce_end(parts)
    resid_then = after(resid, feed_grad)
    dresid, dattn, dgain2, dmixed = middle(heads, dnormed2_pieces, resid_then, cotangent, gain2_row, out_heads)
    dmixed_mine = lax.all_to_all(dmixed, "head", 0, 0, tiled=False)
    dcore, dstates, dgate, dgain_out = mixer_backward_scan(place, raw0, raw1, out_gain_row, kept, dmixed_mine)

    feed_arrived = exchange_ring(after(feed_grad, dmixed_mine).reshape(4, 2 * GROUP, 3 * HALF))
    fed_crossed = take_zx(after(fed_far, dcore), 0, 1)
    dattn_group = lax.all_gather(dattn, "head", axis=0, tiled=True)
    weights_other = from_head(after(mine_one, dmixed), dc=1)

    draw0, draw1, dtaps, dparams = mixer_backward(
        place, starts, gate_params, raw0, raw1, taps, kept, dstates, dcore, dgate
    )
    draw0, draw1, weights_other = lax.optimization_barrier((draw0, draw1, weights_other))
    draw_far = from_head(draw1, dc=1)
    in_grad, gain1_part = in_grads(normed1_own, normed1_other, draw0, draw1, mine_one, gain1_row)
    draw_far = after(draw_far, in_grad)
    dnormed1 = unproject(draw0, draw_far, mine_one, weights_other, [(2 * ROWS_A, width)] * 4 + [(4 * ROWS_B, width)] * 2)
    dnormed1, feed_arrived, dattn_then, in_grad = lax.optimization_barrier(
        (dnormed1, feed_arrived, dattn_group, in_grad)
    )
    in_arrived = exchange_ring(in_grad)
    feed_kept, feed_sent = ring_parts(feed_arrived)
    out_grad = out_grads(dattn_then, mixed.reshape(dattn_group.shape[0], LANES))
    (sent,) = whole_call(
        small_kernel,
        shaped((8, GROUP + 192, LANES), jnp.bfloat16),
        "small",
        (),
        gain1_part,
        dgain2,
        dgain_out,
        dparams,
        dtaps,
        out_grad,
        scratch=[pltpu.VMEM((64, LANES), jnp.float32)],
    )
    half_rows = (2 * SIDE, width)
    in_kept, in_sent = ring_parts(in_arrived)
    fed_sums = whole_call(
        side_sum_kernel, [shaped(half_rows)] + [shaped(half_rows, jnp.bfloat16)] * 3, "side_sum", (), fed_near, after(fed_crossed, sent)
    )
    arrived, first_arrived = reduce_arrivals(
        dnormed1[1:4], dnormed1[5], beside=(feed_kept, feed_sent, in_kept, in_sent, sent, *fed_sums)
    )
    parts = reduce_parts(dnormed1[0], dnormed1[4], arrived)
    dnormed1_pieces = reduce_end(parts)
    fed_sums, feed_sent = lax.optimization_barrier((fed_sums, feed_sent, parts))[:2]
    in_sent = after(in_sent, *dnormed1_pieces)
    fed_pieces = [fed_sums[0]] + [take_zx(fed_sums[k], -k, 0) for k in (1, 2, 3)]
    one_total = in_kept + wide(take_yx(in_sent, 0, 1))
    got = lax.all_to_all(after(sent, in_arrived, first_arrived), "dp", 0, 0, tiled=False)
    dnormed1_pieces, got = lax.optimization_barrier((dnormed1_pieces, got))
    out_total = jnp.sum(wide(got[:, :GROUP]), axis=0)
    pieces = wide(got[:, GROUP:]).reshape(8, 3, 64, LANES)
    small = jnp.sum(pieces[:, 0] + pieces[:, 1] + pieces[:, 2], axis=0)
    shared = sum_all(small[:40], "head", 16)
    fed_pieces, shared = lax.optimization_barrier((fed_pieces, shared))
    (block_out,) = whole_call(leave_kernel, shaped(rows_shape, jnp.bfloat16), "leave", (), *fed_pieces, resid)
    feed_got, shared = lax.optimization_barrier((take_yx(feed_sent, 0, 1), shared))
    feed_total = feed_kept + wide(feed_got)

    gain1_total = shared[:16].reshape(-1)
    gain2_total = shared[16:32].reshape(-1)
    out_gain_total = jnp.sum(shared[32:40], axis=0)
    params_total = jnp.sum(small[40:48], axis=1)[:2, None]
    taps_total = lax.dynamic_slice_in_dim(
        small[48:60].reshape(3, 4, LANES), lax.axis_index("dp") * 16, 16, 2
    )
    (tokens_grad,) = whole_call(
        finish_kernel, shaped(rows_shape), "finish", (), *dnormed1_pieces, tokens, dresid, gain1_row
    )
    hidden_units = gate_weight.shape[1]
    return (
        block_out,
        tokens_grad,
        gain1_total,
        one_total[:, :LANES],
        one_total[:, LANES : 2 * LANES],
        one_total[:, 2 * LANES : 3 * LANES],
        one_total[:, 3 * LANES : 4 * LANES],
        one_total[:, 4 * LANES : 4 * LANES + 2][:, None, :],
        taps_total,
        params_total,
        out_gain_total,
        out_total,
        gain2_total,
        feed_total[:, :hidden_units],
        feed_total[:, HALF : HALF + hidden_units],
        feed_total[:, 2 * HALF : 2 * HALF + hidden_units],
    )


def solution(mesh):
    rows, weight = P(("dp", "head"), None), P("dp", "head")
    weight3, taps = P("dp", "head", None), P(None, None, ("head", "dp"))
    params = P(None, "head")
    in_specs = (
        rows, rows, P("dp", None), P(), weight, weight, weight, weight, weight3, taps, params, P(),
        weight, P(), weight, weight, weight,
    )
    out_specs = (
        rows, rows, P(), weight, weight, weight, weight, weight3, taps, params, P(),
        weight, P(), weight, weight, weight,
    )
    return jax.shard_map(body, mesh=mesh, in_specs=in_specs, out_specs=out_specs, check_vma=False)
```
